32 devices in a mesh: gx: 4 (over x, core), gy: 2 (over y), gz: 4 (over z).
Axes of the slice: x: 2, y: 2, z: 4, core: 2. Of those that a mesh axis runs over, the one named last changes fastest.
Arguments:
- source: float32 [32, 32, 512], P('gx', 'gy', 'gz'), may hold values from -6 to 6
- state: float32 [32, 32, 512], P('gx', 'gy', 'gz'), may hold values from -6 to 6
- log_coef: float32 [32, 32, 512], P('gx', 'gy', 'gz'), may hold values from -1 to 1
- lateral: float32 [32, 32], P('gx', 'gy'), may hold values from -0.5 to 0.5
- owners: int32 [4, 2, 4], P('gx', 'gy'), may hold values from 0 to 3, as said below
Outputs:
- adjoint_field: float32 [32, 32, 512], P('gx', 'gy', 'gz')
- lateral_gradient: float32 [32, 32], P('gx', ('gy', 'gz'))
The draws below stay inside these ranges and needn't reach their ends.
Inputs may be any that keep to these rules, and one draw needn't show every extreme that they name: Along each line, the devices with equal owners entries form a contiguous run of at most 2 devices, and every line has a run of exactly 2; the entry names the device that solves that run's level-2 system, which need not belong to the run; different runs of a line name different devices.
All inputs are finite; a program needn't handle non-finite values.
Results may differ from the reference program's by a relative error of at most 0.0003.
Values sent between devices are 32-bit elements; how exact they have to be, the bound alone decides.
A program may use at most 64 MiB of HBM per device.

```python
import math
import jax
import jax.numpy as jnp
from jax import lax

CX = 8
CY = 16
CZ = 128
SWEEPS = 3
RUN = 2
ANISO = 200
NX = 32
NY = 32
NZ = 512
N_GX = 4
N_GY = 2
N_GZ = 4


def draw_source(key, part):
    coord_y = jnp.arange(NY).astype(jnp.float32)[None, :, None] / NY
    base = jnp.clip(jax.random.normal(key, (NX, NY, NZ), jnp.float32), -5.0, 5.0)
    return base + 0.4 + 0.3 * jnp.cos(2.0 * math.pi * coord_y)


def draw_owners(key, part):
    first_key = jax.random.fold_in(key, 11)
    second_key = jax.random.fold_in(key, 12)
    lead = jax.random.randint(first_key, (N_GX, N_GY, 1), 0, min(N_GZ - RUN, RUN) + 1, dtype=jnp.int32)
    others = jax.random.randint(second_key, (N_GX, N_GY, N_GZ), 1, RUN + 1, dtype=jnp.int32)
    fixed_run = jnp.full((N_GX, N_GY, 1), RUN, jnp.int32)
    lengths = jnp.concatenate([lead, fixed_run, others[:, :, :N_GZ - 2]], axis=2)
    starts = jnp.concatenate([jnp.zeros((N_GX, N_GY, 1), jnp.int32), jnp.cumsum(lengths, axis=2)[:, :, :-1]], axis=2)
    places = jnp.arange(N_GZ).astype(jnp.int32)
    starts_wide = starts[:, :, None, :]
    before = starts_wide <= places[:, None]
    run_start = jnp.max(jnp.where(before, starts_wide, 0), axis=3).astype(jnp.int32)
    run_end = jnp.min(jnp.where(before, N_GZ, jnp.minimum(starts_wide, N_GZ)), axis=3).astype(jnp.int32)
    line_x = jnp.arange(N_GX).astype(jnp.int32)[:, None, None]
    line_y = jnp.arange(N_GY).astype(jnp.int32)[None, :, None]
    pattern = (line_x + line_y) % 3
    head_far = (run_start + N_GZ // 2) % N_GZ
    head_next = run_end % N_GZ
    head_prev = (run_start + N_GZ - 1) % N_GZ
    chosen = jnp.where(pattern == 0, head_far, jnp.where(pattern == 1, head_next, head_prev))
    return chosen.astype(jnp.int32)


def shard_levels(stream_key, extent, pieces, smallest, largest):
    factor_of = 1.0
    for axis_at, blocks in pieces:
        steps = jax.random.uniform(jax.random.fold_in(jax.random.fold_in(stream_key, 6), axis_at), (blocks,), jnp.float32, smallest / len(pieces), largest / len(pieces))
        factor_of = factor_of * jnp.repeat(jnp.exp(steps), extent[axis_at] // blocks).reshape((-1,) + (1,) * (len(extent) - 1 - axis_at))
    return factor_of


def bell_draw(rng, dims, scale, most, pieces=(), kind=jnp.bfloat16):
    gain = shard_levels(rng, dims, pieces, -0.22, 0.18) if pieces else 1.0
    values = jax.random.normal(rng, dims, jnp.float32) * scale * gain
    return jnp.minimum(jnp.maximum(values, -most), most).astype(kind)


def setup_inputs(seed: int = 0) -> dict:
    key_list = jax.random.split(jax.random.key(seed), 6)
    return {
        "source": draw_source(jax.random.fold_in(key_list[5], 71), 0),
        "state": bell_draw(key_list[1], (NX, NY, NZ), 1.0, 6.0, ((0, 4), (1, 2), (2, 4)), jnp.float32),
        "log_coef": jnp.clip(jax.random.uniform(key_list[2], (NX, NY, NZ), jnp.float32, -1.0, 1.0) * shard_levels(key_list[2], (NX, NY, NZ), ((0, 4), (1, 2), (2, 4)), -0.4, 0.0), -1.0, 1.0),
        "lateral": jnp.clip(jax.random.uniform(key_list[3], (NX, NY), jnp.float32, -0.5, 0.5) * shard_levels(key_list[3], (NX, NY), ((0, 4), (1, 2)), -0.4, 0.0), -0.5, 0.5),
        "owners": draw_owners(jax.random.fold_in(key_list[5], 71), 0),
    }


omega_relax = 0.8
neighbour_offsets = ((2, 1, 1), (0, 1, 1), (1, 2, 1), (1, 0, 1), (1, 1, 2), (1, 1, 0))

def neighbour(padded, offset, shape):
    return padded[offset[0]:offset[0] + shape[0], offset[1]:offset[1] + shape[1], offset[2]:offset[2] + shape[2]]

def face_scale(scale, order_index):
    if order_index >= 4:
        return scale * ANISO
    return scale

def level_weights(coef, scale):
    padded = jnp.pad(coef, 1, mode='edge')
    weights = []
    for order_index, offset in enumerate(neighbour_offsets):
        weights.append(face_scale(scale, order_index) * (0.5 * (coef + neighbour(padded, offset, coef.shape))))
    total = weights[0]
    for extra in weights[1:]:
        total = total + extra
    return (weights, total)

def operate(field, weights, total):
    padded = jnp.pad(field, 1)
    result = total * field
    for order_index, offset in enumerate(neighbour_offsets):
        result = result - weights[order_index] * neighbour(padded, offset, field.shape)
    return result

def smooth(field, rhs, weights, total, from_zero):
    remaining = SWEEPS
    if from_zero:
        field = omega_relax * rhs / total
        remaining = SWEEPS - 1
    for repeat in range(remaining):
        field = field + omega_relax * (rhs - operate(field, weights, total)) / total
    return field

def restrict(field):
    shape = field.shape
    return field.reshape(shape[0] // 2, 2, shape[1] // 2, 2, shape[2] // 2, 2).mean(axis=(1, 3, 5))

def prolong(field):
    shape = field.shape
    spread = jnp.broadcast_to(field[:, None, :, None, :, None], (shape[0], 2, shape[1], 2, shape[2], 2))
    return spread.reshape(2 * shape[0], 2 * shape[1], 2 * shape[2])

def line_solve(rhs, total, lower):
    upper = jnp.concatenate([lower[..., 1:], jnp.zeros_like(lower[..., :1])], axis=-1)
    solved = lax.linalg.tridiagonal_solve(-lower, total, -upper, rhs[..., None])
    return solved[..., 0]

def reference(source, state, log_coef, lateral, owners):
    coef = jnp.exp(log_coef + lateral[:, :, None])
    fine_weights, fine_total = level_weights(coef, 1.0)
    mid_coef = restrict(coef)
    mid_weights, mid_total = level_weights(mid_coef, 0.25)
    low_coef = restrict(mid_coef)
    low_weights, low_total = level_weights(low_coef, 0.0625)
    zeros_fine = jnp.zeros_like(source)
    adjoint = smooth(zeros_fine, source, fine_weights, fine_total, True)
    mid_rhs = restrict(source - operate(adjoint, fine_weights, fine_total))
    mid_field = smooth(jnp.zeros_like(mid_rhs), mid_rhs, mid_weights, mid_total, True)
    low_rhs = restrict(mid_rhs - operate(mid_field, mid_weights, mid_total))
    depth = jnp.arange(NZ // 4).astype(jnp.int32)
    block = (depth // (CZ // 4)).astype(jnp.int32)
    first = depth % (CZ // 4) == 0
    rows_line = (jnp.arange(NX // 4) // (CX // 4)).astype(jnp.int32)
    cols_line = (jnp.arange(NY // 4) // (CY // 4)).astype(jnp.int32)
    owner_cell = owners[rows_line[:, None, None], cols_line[None, :, None], block[None, None, :]]
    previous = jnp.maximum(block - 1, 0).astype(jnp.int32)
    owner_prev = owners[rows_line[:, None, None], cols_line[None, :, None], previous[None, None, :]]
    cut = first[None, None, :] & ((block == 0)[None, None, :] | (owner_cell != owner_prev))
    lower = jnp.where(cut, jnp.zeros_like(low_weights[5]), low_weights[5])
    correction = line_solve(low_rhs, low_total, lower)
    mid_field = smooth(mid_field + prolong(correction), mid_rhs, mid_weights, mid_total, False)
    adjoint = smooth(adjoint + prolong(mid_field), source, fine_weights, fine_total, False)
    adjoint_pad = jnp.pad(adjoint, 1)
    state_pad = jnp.pad(state, 1)
    inside_pad = jnp.pad(jnp.ones_like(adjoint), 1)
    grad_terms = jnp.zeros_like(adjoint)
    for offset in neighbour_offsets:
        raw = neighbour(inside_pad, offset, adjoint.shape)
        factor = jnp.where(raw == 0.0, 1.0, 0.5)
        grad_terms = grad_terms + factor * (adjoint - neighbour(adjoint_pad, offset, adjoint.shape)) * (state - neighbour(state_pad, offset, state.shape))
    summed = lax.optimization_barrier(jnp.sum(coef * grad_terms, axis=2))
    return (adjoint, summed * (-1.0 / math.sqrt(NZ)))
```

```python
import functools
import math

import jax
import jax.numpy as jnp
from jax import lax
from jax.experimental import pallas as pl
from jax.experimental.pallas import tpu as pltpu
from jax.sharding import PartitionSpec as P

ANISO = 200.0
OMEGA = 0.8
HALO = 10
SEND = 16
MESH = pl.DeviceIdType.MESH
F32 = jnp.float32


def kernel(
    n_x, n_y, n_z, cx_len, cy_len, cz_len, n_total,
    source_ref, state_ref, logc_ref, lat_ref, owners_ref,
    adj_ref, grad_ref,
    gath, sgath, stage_lo, stage_hi, sstage_lo, sstage_hi,
    c0, x0, y0, z0, d0, i0, b0, va, vb,
    c1, x1, y1, z1, d1, i1, b1, ma, mb,
    c2, z2, d2, r2, im2, spike,
    s0, iface, sides, mid_lo, mid_hi, spk_lo, spk_hi, part,
    main_send, main_recv, lo_send, lo_recv, hi_send, hi_recv,
    st_send, st_recv, stz_send, stz_recv,
    mid_send, mid_recv, if_send, if_recv, pt_send, pt_recv,
):
    nd = n_x * n_y
    lanes = cx_len * cy_len
    gx, gy, gz = lax.axis_index("gx"), lax.axis_index("gy"), lax.axis_index("gz")
    me = gx * n_y + gy
    up, down = lax.rem(gz + 1, n_z), lax.rem(gz + n_z - 1, n_z)
    Z0, Z1, Z2 = cz_len + 2 * HALO, cz_len // 2 + HALO, cz_len // 4 + 2
    H1 = HALO // 2
    L1, L2 = cz_len // 2, cz_len // 4

    def place(k, z):
        peer = lax.rem(me + k, nd)
        return (lax.div(peer, n_y), lax.rem(peer, n_y), z)

    barrier = pltpu.get_barrier_semaphore()
    greeted = [place(k, gz) for k in range(1, nd)]
    greeted += [place(k, z) for z in (up, down) for k in range(nd)]
    greeted += [(gx, gy, lax.rem(gz + j, n_z)) for j in range(2, n_z - 1)]
    for device in greeted:
        pl.semaphore_signal(barrier, inc=1, device_id=device, device_id_type=MESH)

    lane = lax.broadcasted_iota(jnp.int32, (nd, lanes), 1)
    sub = lax.broadcasted_iota(jnp.int32, (nd, lanes), 0)
    xs, ys = lane // cy_len, lane % cy_len
    dx, dy = sub // n_y, sub % n_y
    lane8 = lax.broadcasted_iota(jnp.int32, (cx_len, lanes), 1)
    row8 = lax.broadcasted_iota(jnp.int32, (cx_len, lanes), 0)
    lat = jnp.zeros((cx_len, lanes), F32)
    for y in range(cy_len):
        lat = jnp.where(lane8 % cy_len == y, lat_ref[:, y : y + 1], lat)
    lat = jnp.sum(jnp.where(lane8 // cy_len == row8, lat, 0.0), axis=0, keepdims=True)

    def rows_of(ref):
        return ref[...].reshape(lanes, cz_len).T

    coef = jnp.exp(rows_of(logc_ref) + lat)
    src = rows_of(source_ref)
    state = rows_of(state_ref)
    gath[me, 0:cz_len, :] = coef
    gath[me, cz_len : 2 * cz_len, :] = src
    line = owners_ref[0]
    for j in range(16):
        if 0 < j < n_z:
            same = jnp.broadcast_to(line[:, j : j + 1], (1, lanes)) == jnp.broadcast_to(
                line[:, j - 1 : j], (1, lanes)
            )
            gath[me, 2 * cz_len + j : 2 * cz_len + j + 1, :] = jnp.where(same, 1.0, 0.0)
        else:
            gath[me, 2 * cz_len + j : 2 * cz_len + j + 1, :] = jnp.zeros((1, lanes), F32)
    stage_lo[0:SEND, :] = coef[cz_len - SEND :]
    stage_lo[SEND : 2 * SEND, :] = src[cz_len - SEND :]
    stage_hi[0:SEND, :] = coef[:SEND]
    stage_hi[SEND : 2 * SEND, :] = src[:SEND]
    sgath[me, 0:cz_len, :] = state
    sstage_lo[...] = state[cz_len - 8 :]
    sstage_hi[...] = state[:8]
    pl.semaphore_wait(barrier, len(greeted))

    base_lo = 2 * cz_len + 16
    base_hi = base_lo + 2 * SEND
    sent = []

    def copy(src_at, dst_at, ssem, rsem, device):
        c = pltpu.make_async_remote_copy(
            src_ref=src_at, dst_ref=dst_at, send_sem=ssem, recv_sem=rsem,
            device_id=device, device_id_type=MESH,
        )
        c.start()
        return c

    main, los, his = [], [], []
    for k in range(1, nd):
        body = gath.at[me, pl.ds(0, base_lo)]
        main.append(copy(body, body, main_send.at[k], main_recv.at[k], place(k, gz)))
    for k in range(nd):
        los.append(copy(stage_lo, gath.at[me, pl.ds(base_lo, 2 * SEND)],
                        lo_send.at[k], lo_recv.at[k], place(k, up)))
        his.append(copy(stage_hi, gath.at[me, pl.ds(base_hi, 2 * SEND)],
                        hi_send.at[k], hi_recv.at[k], place(k, down)))

    def roll(v, shift, axis):
        return pltpu.roll(v, shift % v.shape[axis], axis)

    def masks(s):
        return dict(
            s=s,
            xhi=(xs >= cx_len - s)[None], xlo=(xs < s)[None],
            yhi=(ys >= cy_len - s)[None], ylo=(ys < s)[None],
            xin=jnp.where((xs >= cx_len - s) & (dx == n_x - 1), 0.0, 0.5)[None],
            yin=jnp.where((ys >= cy_len - s) & (dy == n_y - 1), 0.0, 0.5)[None],
            edge=(
                jnp.where((xs >= cx_len - s) & (dx == n_x - 1), 1.0, 0.0)
                + jnp.where((xs < s) & (dx == 0), 1.0, 0.0)
                + jnp.where((ys >= cy_len - s) & (dy == n_y - 1), 1.0, 0.0)
                + jnp.where((ys < s) & (dy == 0), 1.0, 0.0)
            )[None],
            xbit=(xs // s % 2 == 0)[None], ybit=(ys // s % 2 == 0)[None],
        )

    def pick(mask, a, b):
        return jnp.where(jnp.broadcast_to(mask, a.shape), a, b)

    def x_next(v, m):
        r = roll(v, -m["s"] * cy_len, 2)
        return pick(m["xhi"], roll(r, -n_y, 1), r)

    def x_prev(v, m):
        r = roll(v, m["s"] * cy_len, 2)
        return pick(m["xlo"], roll(r, n_y, 1), r)

    def y_next(v, m):
        r = roll(v, -m["s"], 2)
        return pick(m["yhi"], roll(roll(v, -1, 1), cy_len - m["s"], 2), r)

    def y_prev(v, m):
        r = roll(v, m["s"], 2)
        return pick(m["ylo"], roll(roll(v, 1, 1), m["s"] - cy_len, 2), r)

    def block_mean(pair, m):
        s = m["s"]
        v = pair + pick(m["ybit"], roll(pair, -s, 2), roll(pair, s, 2))
        w = s * cy_len
        v = v + pick(m["xbit"], roll(v, -w, 2), roll(v, w, 2))
        return 0.125 * v

    m0, m1, m2 = masks(1), masks(2), masks(4)
    first_dev, last_dev = gz == 0, gz == n_z - 1
    zero_plane = jnp.zeros((1, nd, lanes), F32)

    def loop(count, step, body):
        def run(i, carry):
            body(i * step)
            return carry
        lax.fori_loop(0, count // step, run, 0)

    def pads(ref):
        ref[0:1] = zero_plane
        ref[ref.shape[0] - 1 :] = zero_plane

    for ref in (c0, va, vb, c1, ma, mb, c2):
        pads(ref)

    def level(c, length, halo, own, scale, m, xr, yr, zr, dr, ir):
        za = scale * ANISO
        zr[length : length + 1] = zero_plane

        def body(i):
            k = i
            here = c[pl.ds(k + 1, 1)]
            below, above = c[pl.ds(k, 1)], c[pl.ds(k + 2, 1)]
            cut_lo = (k == 0) | (first_dev & (k == halo)) | (last_dev & (k == halo + own))
            cut_hi = (k == length - 1) | (first_dev & (k == halo - 1)) | (
                last_dev & (k == halo + own - 1))
            keep_lo = jnp.where(cut_lo, 0.0, 0.5 * za)
            keep_hi = jnp.where(cut_hi, 0.0, 0.5 * za)
            edge_z = jnp.where(cut_lo, za, 0.0) + jnp.where(cut_hi, za, 0.0)
            wz = keep_lo * (below + here)
            zr[pl.ds(k, 1)] = wz
            wx = (scale * m["xin"]) * (here + x_next(here, m))
            wy = (scale * m["yin"]) * (here + y_next(here, m))
            diag = wx + x_prev(wx, m) + wy + y_prev(wy, m) + (scale * m["edge"]) * here
            diag = diag + wz + keep_hi * (above + here) + edge_z * here
            dr[pl.ds(k, 1)] = diag
            if xr is not None:
                xr[pl.ds(k, 1)] = wx
                yr[pl.ds(k, 1)] = wy
                ir[pl.ds(k, 1)] = OMEGA / diag

        loop(length, 1, body)

    def pull(v, k, step, m, xr, yr, zr):
        here = v[pl.ds(k + 1, step)]
        wx, wy = xr[pl.ds(k, step)], yr[pl.ds(k, step)]
        total = zr[pl.ds(k, step)] * v[pl.ds(k, step)]
        total = total + zr[pl.ds(k + 1, step)] * v[pl.ds(k + 2, step)]
        total = total + (wx * x_next(here, m) + x_prev(wx * here, m))
        total = total + (wy * y_next(here, m) + y_prev(wy * here, m))
        return here, total

    def sweep(v, out, b, start, stop, m, xr, yr, zr, ir, step=4):
        def body(i):
            k = start + i
            here, total = pull(v, k, step, m, xr, yr, zr)
            out[pl.ds(k + 1, step)] = (1.0 - OMEGA) * here + ir[pl.ds(k, step)] * (
                b[pl.ds(k, step)] + total)
        loop(stop - start, step, body)

    fine = (m0, x0, y0, z0)
    mid = (m1, x1, y1, z1)

    for c in main:
        c.wait()
    for c in los + his:
        c.wait()
    flat = gath.reshape(nd * gath.shape[1], lanes)
    sflat = sgath.reshape(nd * sgath.shape[1], lanes)

    def plane(row):
        return flat[pl.ds(row, nd, stride=gath.shape[1]), :][None]

    def spread(i):
        c0[pl.ds(1 + HALO + i, 1)] = plane(i)
        b0[pl.ds(HALO + i, 1)] = plane(cz_len + i)

    loop(cz_len, 1, spread)

    def spread_halo(i):
        c0[pl.ds(1 + i, 1)] = plane(base_lo + SEND - HALO + i)
        b0[pl.ds(i, 1)] = plane(base_lo + 2 * SEND - HALO + i)
        c0[pl.ds(1 + HALO + cz_len + i, 1)] = plane(base_hi + i)
        b0[pl.ds(HALO + cz_len + i, 1)] = plane(base_hi + SEND + i)

    loop(HALO, 1, spread_halo)

    states = []
    for k in range(1, nd):
        body = sgath.at[me, pl.ds(0, cz_len)]
        states.append(copy(body, body, st_send.at[k], st_recv.at[k], place(k, gz)))
    states.append(copy(sstage_lo, sgath.at[me, pl.ds(cz_len, 8)],
                       stz_send.at[0], stz_recv.at[0], (gx, gy, up)))
    states.append(copy(sstage_hi, sgath.at[me, pl.ds(cz_len + 8, 8)],
                       stz_send.at[1], stz_recv.at[1], (gx, gy, down)))

    def pairs(ref, k, step):
        v = ref[pl.ds(k, 2 * step)].reshape(step, 2, nd, lanes)
        return v[:, 0] + v[:, 1]

    def coarsen1(K):
        c1[pl.ds(K + 1, 2)] = block_mean(pairs(c0, 1 + 2 * K, 2), m0)

    loop(Z1, 2, coarsen1)

    def coarsen2(K):
        c2[pl.ds(K + 1, 2)] = block_mean(pairs(c1, 1 + H1 - 2 + 2 * K, 2), m1)

    loop(Z2, 2, coarsen2)
    level(c0, Z0, HALO, cz_len, 1.0, m0, x0, y0, z0, d0, i0)
    level(c1, Z1, H1, L1, 0.25, m1, x1, y1, z1, d1, i1)
    level(c2, Z2, 1, L2, 0.0625, m2, None, None, z2, d2, None)

    def first0(k):
        va[pl.ds(k + 1, 4)] = i0[pl.ds(k, 4)] * b0[pl.ds(k, 4)]

    loop(Z0, 4, first0)
    sweep(va, vb, b0, 2, Z0 - 2, *fine, i0)
    sweep(vb, va, b0, 2, Z0 - 2, *fine, i0)

    def resid0_all():
        def body(i):
            K = 2 + i
            k = 2 * K
            here, total = pull(va, k, 4, *fine)
            r = b0[pl.ds(k, 4)] + total - d0[pl.ds(k, 4)] * here
            r = r.reshape(2, 2, nd, lanes)
            b1[pl.ds(K, 2)] = block_mean(r[:, 0] + r[:, 1], m0)
        loop(Z1 - 4, 2, body)

    resid0_all()

    def first1(i):
        k = 2 + i
        ma[pl.ds(k + 1, 2)] = i1[pl.ds(k, 2)] * b1[pl.ds(k, 2)]

    loop(Z1 - 4, 2, first1)
    sweep(ma, mb, b1, 3, Z1 - 3, *mid, i1)
    sweep(mb, ma, b1, 3, Z1 - 3, *mid, i1)

    mids = [
        copy(ma.at[pl.ds(1 + L1, H1)], mid_lo.at[0], mid_send.at[0], mid_recv.at[0], (gx, gy, up)),
        copy(b1.at[pl.ds(L1, H1)], mid_lo.at[1], mid_send.at[1], mid_recv.at[1], (gx, gy, up)),
        copy(ma.at[pl.ds(1 + H1, H1)], mid_hi.at[0], mid_send.at[2], mid_recv.at[2], (gx, gy, down)),
        copy(b1.at[pl.ds(H1, H1)], mid_hi.at[1], mid_send.at[3], mid_recv.at[3], (gx, gy, down)),
    ]

    def resid1(K):
        k = H1 + 2 * K
        here, total = pull(ma, k, 4, *mid)
        r = b1[pl.ds(k, 4)] + total - d1[pl.ds(k, 4)] * here
        r = r.reshape(2, 2, nd, lanes)
        r2[pl.ds(K, 2)] = block_mean(r[:, 0] + r[:, 1], m1)

    loop(L2, 2, resid1)

    inv = 1.0 / d2[1]
    y_now, p_now = r2[0], jnp.ones((nd, lanes), F32)
    im2[0], spike[0, 0], spike[1, 0] = inv, y_now, p_now

    def forward(k, carry):
        inv, y_now, p_now = carry
        e = z2[k + 1]
        t = e * inv
        inv = 1.0 / (d2[k + 1] - e * t)
        y_now = r2[k] + t * y_now
        p_now = t * p_now
        im2[k], spike[0, k], spike[1, k] = inv, y_now, p_now
        return inv, y_now, p_now

    inv, y_now, p_now = lax.fori_loop(1, L2, forward, (inv, y_now, p_now))
    last = (y_now * inv, p_now * inv, inv)
    for i in range(3):
        spike[i, L2 - 1] = last[i]

    def backward(i, carry):
        g, p, q = carry
        k = L2 - 2 - i
        e, inv = z2[k + 2], im2[k]
        g = inv * (spike[0, k] + e * g)
        p = inv * (spike[1, k] + e * p)
        q = inv * (e * q)
        spike[0, k], spike[1, k], spike[2, k] = g, p, q
        return g, p, q

    head = lax.fori_loop(0, L2 - 1, backward, last)
    for i in range(3):
        iface[gz, i] = head[i]
        iface[gz, 3 + i] = last[i]
    iface[gz, 6] = z2[1] * flat[pl.ds(2 * cz_len + gz, nd, stride=gath.shape[1]), :]
    ifs = []
    for j in range(1, n_z):
        ifs.append(copy(iface.at[gz], iface.at[gz], if_send.at[j], if_recv.at[j],
                        (gx, gy, lax.rem(gz + j, n_z))))
    ifs.append(copy(spike.at[:, pl.ds(L2 - 3, 3)], spk_lo, if_send.at[n_z], if_recv.at[n_z],
                    (gx, gy, up)))
    ifs.append(copy(spike.at[:, pl.ds(0, 3)], spk_hi, if_send.at[n_z + 1], if_recv.at[n_z + 1],
                    (gx, gy, down)))

    for c in states:
        c.wait()

    def splane(row):
        return sflat[pl.ds(row, nd, stride=sgath.shape[1]), :][None]

    def spread_state(i):
        s0[pl.ds(1 + i, 1)] = splane(i)

    loop(cz_len, 1, spread_state)
    s0[0:1] = jnp.where(first_dev, 0.0, splane(cz_len + 7))
    s0[cz_len + 1 :] = jnp.where(last_dev, 0.0, splane(cz_len + 8))

    for c in mids + ifs:
        c.wait()

    zero = jnp.zeros((nd, lanes), F32)
    A, B = zero, zero
    kept = []
    for j in range(n_z):
        c = iface[j, 6]
        g, p, q = iface[j, 0], iface[j, 1], iface[j, 2]
        gl, plast, ql = iface[j, 3], iface[j, 4], iface[j, 5]
        inv = 1.0 / (1.0 - p * c * B)
        F = (g + p * c * A) * inv
        G = q * inv
        kept.append((c, A, B, F, G))
        nxt = iface[j + 1, 6] if j + 1 < n_z else zero
        tail = plast * c
        A, B = gl + tail * (A + B * F), (ql + tail * B * G) * nxt
    right = zero
    for j in reversed(range(n_z)):
        c, A, B, F, G = kept[j]
        head = F + G * right
        sides[j, 0] = c * (A + B * head)
        sides[j, 1] = right
        right = c * head

    L, R = sides[gz, 0], sides[gz, 1]

    def twice(v):
        return jnp.broadcast_to(v[:, None], (v.shape[0], 2, nd, lanes)).reshape(
            2 * v.shape[0], nd, lanes)

    def correct(K):
        x = spike[0, pl.ds(K, 2)] + spike[1, pl.ds(K, 2)] * L + spike[2, pl.ds(K, 2)] * R
        k = 1 + H1 + 2 * K
        ma[pl.ds(k, 4)] = ma[pl.ds(k, 4)] + twice(x)

    loop(L2, 2, correct)
    xl = spk_lo[0] + spk_lo[1] * sides[down, 0] + spk_lo[2] * sides[down, 1]
    ma[1 : 1 + H1] = mid_lo[0] + twice(xl)[6 - H1 :]
    b1[0:H1] = mid_lo[1]
    xh = spk_hi[0] + spk_hi[1] * sides[up, 0] + spk_hi[2] * sides[up, 1]
    ma[1 + H1 + L1 : 1 + 2 * H1 + L1] = mid_hi[0] + twice(xh)[:H1]
    b1[H1 + L1 :] = mid_hi[1]

    sweep(ma, mb, b1, 1, Z1 - 1, *mid, i1)
    sweep(mb, ma, b1, 1, Z1 - 1, *mid, i1)
    sweep(ma, mb, b1, 3, Z1 - 3, *mid, i1)

    def raise0(i):
        K = 3 + i
        k = 1 + 2 * K
        va[pl.ds(k, 4)] = va[pl.ds(k, 4)] + twice(mb[pl.ds(K + 1, 2)])

    loop(Z1 - 6, 2, raise0)
    sweep(va, vb, b0, HALO - 4, HALO + cz_len + 4, *fine, i0)
    sweep(vb, va, b0, HALO - 2, HALO + cz_len + 2, *fine, i0)
    sweep(va, vb, b0, HALO - 2, HALO + cz_len + 2, *fine, i0)

    def terms(i, acc):
        a, s = vb[pl.ds(HALO + 1 + i, 1)], s0[pl.ds(1 + i, 1)]
        tx = m0["xin"] * ((a - x_next(a, m0)) * (s - x_next(s, m0)))
        ty = m0["yin"] * ((a - y_next(a, m0)) * (s - y_next(s, m0)))
        t = tx + x_prev(tx, m0) + ty + y_prev(ty, m0) + m0["edge"] * (a * s)
        lo = first_dev & (i == 0)
        hi = last_dev & (i == cz_len - 1)
        below, above = vb[pl.ds(HALO + i, 1)], vb[pl.ds(HALO + 2 + i, 1)]
        t = t + jnp.where(lo, a * s, 0.5 * ((a - below) * (s - s0[pl.ds(i, 1)])))
        t = t + jnp.where(hi, a * s, 0.5 * ((a - above) * (s - s0[pl.ds(2 + i, 1)])))
        return acc + (c0[pl.ds(HALO + 1 + i, 1)] * t)[0]

    acc = lax.fori_loop(0, cz_len, terms, zero)
    part[gz] = acc
    parts = []
    for j in range(1, n_z):
        parts.append(copy(part.at[gz], part.at[gz], pt_send.at[j], pt_recv.at[j],
                          (gx, gy, lax.rem(gz + j, n_z))))

    vflat = vb.reshape(vb.shape[0] * nd, lanes)
    own = vflat[pl.ds((HALO + 1) * nd + me, cz_len, stride=nd), :]
    adj_ref[...] = own.T.reshape(cx_len, cy_len, cz_len)

    for c in parts:
        c.wait()
    total = part[0]
    for j in range(1, n_z):
        total = total + part[j]
    row = jnp.sum(jnp.where(sub == me, total, 0.0), axis=0, keepdims=True)
    row = jnp.broadcast_to(row, (cx_len, lanes)) * (-1.0 / math.sqrt(n_total))
    width = cy_len // n_z
    for j in range(width):
        here = lane8 == row8 * cy_len + gz * width + j
        grad_ref[:, j : j + 1] = jnp.sum(jnp.where(here, row, 0.0), axis=1, keepdims=True)


def solution(mesh):
    n_x, n_y, n_z = mesh.shape["gx"], mesh.shape["gy"], mesh.shape["gz"]
    nd = n_x * n_y

    def per_device(source, state, log_coef, lateral, owners):
        cx, cy, cz = source.shape
        lanes = cx * cy
        Z0, Z1, Z2, H1 = cz + 2 * HALO, cz // 2 + HALO, cz // 4 + 2, HALO // 2
        V = lambda *shape: pltpu.VMEM(shape, F32)
        pln = lambda k: V(k, nd, lanes)
        D = lambda k: pltpu.SemaphoreType.DMA((k,))
        vm = pl.BlockSpec(memory_space=pltpu.VMEM)
        return pl.pallas_call(
            functools.partial(kernel, n_x, n_y, n_z, cx, cy, cz, cz * n_z),
            out_shape=(
                jax.ShapeDtypeStruct((cx, cy, cz), F32),
                jax.ShapeDtypeStruct((cx, cy // n_z), F32),
            ),
            in_specs=[vm] * 5,
            out_specs=(vm, vm),
            scratch_shapes=[
                V(nd, 2 * cz + 16 + 4 * SEND, lanes), V(nd, cz + 16, lanes),
                V(2 * SEND, lanes), V(2 * SEND, lanes), V(8, lanes), V(8, lanes),
                pln(Z0 + 2), pln(Z0), pln(Z0), pln(Z0 + 1), pln(Z0), pln(Z0), pln(Z0),
                pln(Z0 + 2), pln(Z0 + 2),
                pln(Z1 + 2), pln(Z1), pln(Z1), pln(Z1 + 1), pln(Z1), pln(Z1), pln(Z1),
                pln(Z1 + 2), pln(Z1 + 2),
                pln(Z2 + 2), pln(Z2 + 1), pln(Z2), pln(cz // 4), pln(cz // 4),
                V(3, cz // 4, nd, lanes),
                pln(cz + 2), V(n_z, 7, nd, lanes), V(n_z, 2, nd, lanes),
                V(2, H1, nd, lanes), V(2, H1, nd, lanes),
                V(3, 3, nd, lanes), V(3, 3, nd, lanes), V(n_z, nd, lanes),
                D(nd), D(nd), D(nd), D(nd), D(nd), D(nd),
                D(nd), D(nd), D(2), D(2),
                D(4), D(4), D(n_z + 2), D(n_z + 2), D(n_z), D(n_z),
            ],
            compiler_params=pltpu.CompilerParams(
                collective_id=0, has_side_effects=True, vmem_limit_bytes=56 * 1024 * 1024
            ),
            cost_estimate=pl.CostEstimate(
                flops=100_000_000, bytes_accessed=400_000, transcendentals=20_000
            ),
        )(source, state, log_coef, lateral, owners)

    placed = (
        P("gx", "gy", "gz"),
        P("gx", "gy", "gz"),
        P("gx", "gy", "gz"),
        P("gx", "gy"),
        P("gx", "gy", None),
    )
    return jax.shard_map(
        per_device,
        mesh=mesh,
        in_specs=placed,
        out_specs=(P("gx", "gy", "gz"), P("gx", ("gy", "gz"))),
        check_vma=False,
    )
```

```python
import functools
import math

import jax
import jax.numpy as jnp
from jax import lax
from jax.experimental import pallas as pl
from jax.experimental.pallas import tpu as pltpu
from jax.sharding import PartitionSpec as P

ANISO = 200.0
OMEGA = 0.8
HALO = 10
SEND = 16
MESH = pl.DeviceIdType.MESH
F32 = jnp.float32


def kernel(
    n_x, n_y, n_z, cx_len, cy_len, cz_len, n_total,
    source_ref, state_ref, logc_ref, lat_ref, owners_ref,
    adj_ref, grad_ref,
    gath, sgath, stage_lo, stage_hi, sstage_lo, sstage_hi,
    c0, x0, y0, z0, d0, i0, b0, va, vb,
    c1, x1, y1, z1, d1, i1, b1, ma, mb,
    c2, z2, d2, r2, im2, spike,
    s0, iface, sides, mid_lo, mid_hi, spk_lo, spk_hi, part,
    main_send, main_recv, lo_send, lo_recv, hi_send, hi_recv,
    st_send, st_recv, stz_send, stz_recv,
    mid_send, mid_recv, if_send, if_recv, pt_send, pt_recv,
):
    nd = n_x * n_y
    lanes = cx_len * cy_len
    gx, gy, gz = lax.axis_index("gx"), lax.axis_index("gy"), lax.axis_index("gz")
    me = gx * n_y + gy
    up, down = lax.rem(gz + 1, n_z), lax.rem(gz + n_z - 1, n_z)
    Z0, Z1, Z2 = cz_len + 2 * HALO, cz_len // 2 + HALO, cz_len // 4 + 2
    H1 = HALO // 2
    L1, L2 = cz_len // 2, cz_len // 4

    def place(k, z):
        peer = lax.rem(me + k, nd)
        return (lax.div(peer, n_y), lax.rem(peer, n_y), z)

    barrier = pltpu.get_barrier_semaphore()
    greeted = [place(k, gz) for k in range(1, nd)]
    greeted += [place(k, z) for z in (up, down) for k in range(nd)]
    greeted += [(gx, gy, lax.rem(gz + j, n_z)) for j in range(2, n_z - 1)]
    for device in greeted:
        pl.semaphore_signal(barrier, inc=1, device_id=device, device_id_type=MESH)

    lane = lax.broadcasted_iota(jnp.int32, (nd, lanes), 1)
    sub = lax.broadcasted_iota(jnp.int32, (nd, lanes), 0)
    xs, ys = lane // cy_len, lane % cy_len
    dx, dy = sub // n_y, sub % n_y
    lane8 = lax.broadcasted_iota(jnp.int32, (cx_len, lanes), 1)
    row8 = lax.broadcasted_iota(jnp.int32, (cx_len, lanes), 0)
    lat = jnp.zeros((cx_len, lanes), F32)
    for y in range(cy_len):
        lat = jnp.where(lane8 % cy_len == y, lat_ref[:, y : y + 1], lat)
    lat = jnp.sum(jnp.where(lane8 // cy_len == row8, lat, 0.0), axis=0, keepdims=True)

    def rows_of(ref):
        return ref[...].reshape(lanes, cz_len).T

    coef = jnp.exp(rows_of(logc_ref) + lat)
    src = rows_of(source_ref)
    state = rows_of(state_ref)
    gath[me, 0:cz_len, :] = coef
    gath[me, cz_len : 2 * cz_len, :] = src
    line = owners_ref[0]
    for j in range(16):
        if 0 < j < n_z:
            same = jnp.broadcast_to(line[:, j : j + 1], (1, lanes)) == jnp.broadcast_to(
                line[:, j - 1 : j], (1, lanes)
            )
            gath[me, 2 * cz_len + j : 2 * cz_len + j + 1, :] = jnp.where(same, 1.0, 0.0)
        else:
            gath[me, 2 * cz_len + j : 2 * cz_len + j + 1, :] = jnp.zeros((1, lanes), F32)
    stage_lo[0:SEND, :] = coef[cz_len - SEND :]
    stage_lo[SEND : 2 * SEND, :] = src[cz_len - SEND :]
    stage_hi[0:SEND, :] = coef[:SEND]
    stage_hi[SEND : 2 * SEND, :] = src[:SEND]
    sgath[me, 0:cz_len, :] = state
    sstage_lo[...] = state[cz_len - 8 :]
    sstage_hi[...] = state[:8]
    pl.semaphore_wait(barrier, len(greeted))

    base_lo = 2 * cz_len + 16
    base_hi = base_lo + 2 * SEND
    sent = []

    def copy(src_at, dst_at, ssem, rsem, device):
        c = pltpu.make_async_remote_copy(
            src_ref=src_at, dst_ref=dst_at, send_sem=ssem, recv_sem=rsem,
            device_id=device, device_id_type=MESH,
        )
        c.start()
        return c

    main, los, his = [], [], []
    for k in range(1, nd):
        body = gath.at[me, pl.ds(0, base_lo)]
        main.append(copy(body, body, main_send.at[k], main_recv.at[k], place(k, gz)))
    for k in range(nd):
        los.append(copy(stage_lo, gath.at[me, pl.ds(base_lo, 2 * SEND)],
                        lo_send.at[k], lo_recv.at[k], place(k, up)))
        his.append(copy(stage_hi, gath.at[me, pl.ds(base_hi, 2 * SEND)],
                        hi_send.at[k], hi_recv.at[k], place(k, down)))

    def roll(v, shift, axis):
        return pltpu.roll(v, shift % v.shape[axis], axis)

    def masks(s):
        return dict(
            s=s,
            xhi=(xs >= cx_len - s)[None], xlo=(xs < s)[None],
            yhi=(ys >= cy_len - s)[None], ylo=(ys < s)[None],
            xin=jnp.where((xs >= cx_len - s) & (dx == n_x - 1), 0.0, 0.5)[None],
            yin=jnp.where((ys >= cy_len - s) & (dy == n_y - 1), 0.0, 0.5)[None],
            edge=(
                jnp.where((xs >= cx_len - s) & (dx == n_x - 1), 1.0, 0.0)
                + jnp.where((xs < s) & (dx == 0), 1.0, 0.0)
                + jnp.where((ys >= cy_len - s) & (dy == n_y - 1), 1.0, 0.0)
                + jnp.where((ys < s) & (dy == 0), 1.0, 0.0)
            )[None],
            xbit=(xs // s % 2 == 0)[None], ybit=(ys // s % 2 == 0)[None],
        )

    def pick(mask, a, b):
        return jnp.where(jnp.broadcast_to(mask, a.shape), a, b)

    def x_next(v, m):
        r = roll(v, -m["s"] * cy_len, 2)
        return pick(m["xhi"], roll(r, -n_y, 1), r)

    def x_prev(v, m):
        r = roll(v, m["s"] * cy_len, 2)
        return pick(m["xlo"], roll(r, n_y, 1), r)

    def y_next(v, m):
        r = roll(v, -m["s"], 2)
        return pick(m["yhi"], roll(roll(v, -1, 1), cy_len - m["s"], 2), r)

    def y_prev(v, m):
        r = roll(v, m["s"], 2)
        return pick(m["ylo"], roll(roll(v, 1, 1), m["s"] - cy_len, 2), r)

    def block_mean(pair, m):
        s = m["s"]
        v = pair + pick(m["ybit"], roll(pair, -s, 2), roll(pair, s, 2))
        w = s * cy_len
        v = v + pick(m["xbit"], roll(v, -w, 2), roll(v, w, 2))
        return 0.125 * v

    m0, m1, m2 = masks(1), masks(2), masks(4)
    first_dev, last_dev = gz == 0, gz == n_z - 1
    zero_plane = jnp.zeros((1, nd, lanes), F32)

    def chunks(start, stop, body, step=16):
        whole = (stop - start) // step

        def run(i, carry):
            body(start + i * step, step)
            return carry

        lax.fori_loop(0, whole, run, 0)
        if (stop - start) % step:
            body(start + whole * step, (stop - start) % step)

    def pads(ref):
        ref[0:1] = zero_plane
        ref[ref.shape[0] - 1 :] = zero_plane

    for ref in (c0, va, vb, c1, ma, mb, c2):
        pads(ref)

    def level(c, length, halo, own, scale, m, xr, yr, zr, dr, ir):
        half = 0.5 * scale * ANISO
        c[0:1], c[length + 1 :] = c[1:2], c[length : length + 1]
        lo, hi = halo, halo + own + 1
        c[lo : lo + 1] = jnp.where(first_dev, c[lo + 1 : lo + 2], c[lo : lo + 1])
        c[hi : hi + 1] = jnp.where(last_dev, c[hi - 1 : hi], c[hi : hi + 1])

        def body(k, n):
            here = c[pl.ds(k + 1, n)]
            wz = half * (c[pl.ds(k, n)] + here)
            zr[pl.ds(k, n)] = wz
            wx = (scale * m["xin"]) * (here + x_next(here, m))
            wy = (scale * m["yin"]) * (here + y_next(here, m))
            diag = wx + x_prev(wx, m) + wy + y_prev(wy, m) + (scale * m["edge"]) * here
            diag = diag + wz + half * (c[pl.ds(k + 2, n)] + here)
            dr[pl.ds(k, n)] = diag
            if xr is not None:
                xr[pl.ds(k, n)] = wx
                yr[pl.ds(k, n)] = wy
                ir[pl.ds(k, n)] = OMEGA / diag

        chunks(0, length, body)
        zr[0:1] = zero_plane
        zr[length : length + 1] = zero_plane
        lo, hi = halo, halo + own
        zr[lo : lo + 1] = jnp.where(first_dev, 0.0, zr[lo : lo + 1])
        zr[hi : hi + 1] = jnp.where(last_dev, 0.0, zr[hi : hi + 1])

    def pull(v, k, step, m, xr, yr, zr):
        here = v[pl.ds(k + 1, step)]
        wx, wy = xr[pl.ds(k, step)], yr[pl.ds(k, step)]
        total = zr[pl.ds(k, step)] * v[pl.ds(k, step)]
        total = total + zr[pl.ds(k + 1, step)] * v[pl.ds(k + 2, step)]
        total = total + (wx * x_next(here, m) + x_prev(wx * here, m))
        total = total + (wy * y_next(here, m) + y_prev(wy * here, m))
        return here, total

    def sweep(v, out, b, start, stop, m, xr, yr, zr, ir):
        def body(k, n):
            here, total = pull(v, k, n, m, xr, yr, zr)
            out[pl.ds(k + 1, n)] = (1.0 - OMEGA) * here + ir[pl.ds(k, n)] * (
                b[pl.ds(k, n)] + total)
        chunks(start, stop, body)

    fine = (m0, x0, y0, z0)
    mid = (m1, x1, y1, z1)

    for c in main:
        c.wait()
    for c in los + his:
        c.wait()
    flat = gath.reshape(nd * gath.shape[1], lanes)
    sflat = sgath.reshape(nd * sgath.shape[1], lanes)

    def plane(row):
        return flat[pl.ds(row, nd, stride=gath.shape[1]), :][None]

    def spread(i, n):
        for u in range(n):
            c0[pl.ds(1 + HALO + i + u, 1)] = plane(i + u)
            b0[pl.ds(HALO + i + u, 1)] = plane(cz_len + i + u)

    chunks(0, cz_len, spread)
    for i in range(HALO):
        c0[1 + i : 2 + i] = plane(base_lo + SEND - HALO + i)
        b0[i : 1 + i] = plane(base_lo + 2 * SEND - HALO + i)
        c0[1 + HALO + cz_len + i : 2 + HALO + cz_len + i] = plane(base_hi + i)
        b0[HALO + cz_len + i : 1 + HALO + cz_len + i] = plane(base_hi + SEND + i)

    states = []
    for k in range(1, nd):
        body = sgath.at[me, pl.ds(0, cz_len)]
        states.append(copy(body, body, st_send.at[k], st_recv.at[k], place(k, gz)))
    states.append(copy(sstage_lo, sgath.at[me, pl.ds(cz_len, 8)],
                       stz_send.at[0], stz_recv.at[0], (gx, gy, up)))
    states.append(copy(sstage_hi, sgath.at[me, pl.ds(cz_len + 8, 8)],
                       stz_send.at[1], stz_recv.at[1], (gx, gy, down)))

    def pairs(ref, k, step):
        v = ref[pl.ds(k, 2 * step)].reshape(step, 2, nd, lanes)
        return v[:, 0] + v[:, 1]

    def coarsen1(K, n):
        c1[pl.ds(K + 1, n)] = block_mean(pairs(c0, 1 + 2 * K, n), m0)

    chunks(0, Z1, coarsen1)

    def coarsen2(K, n):
        c2[pl.ds(K + 1, n)] = block_mean(pairs(c1, 1 + H1 - 2 + 2 * K, n), m1)

    chunks(0, Z2, coarsen2)
    level(c0, Z0, HALO, cz_len, 1.0, m0, x0, y0, z0, d0, i0)
    level(c1, Z1, H1, L1, 0.25, m1, x1, y1, z1, d1, i1)
    level(c2, Z2, 1, L2, 0.0625, m2, None, None, z2, d2, None)

    def first0(k, n):
        va[pl.ds(k + 1, n)] = i0[pl.ds(k, n)] * b0[pl.ds(k, n)]

    chunks(0, Z0, first0)
    sweep(va, vb, b0, 1, Z0 - 1, *fine, i0)
    sweep(vb, va, b0, 2, Z0 - 2, *fine, i0)

    def residual(v, b, d, k, n, m, *weights):
        here, total = pull(v, k, 2 * n, m, *weights)
        r = b[pl.ds(k, 2 * n)] + total - d[pl.ds(k, 2 * n)] * here
        r = r.reshape(n, 2, nd, lanes)
        return block_mean(r[:, 0] + r[:, 1], m)

    def resid0(K, n):
        b1[pl.ds(K, n)] = residual(va, b0, d0, 2 * K, n, *fine)

    chunks(2, Z1 - 2, resid0, 8)

    def first1(k, n):
        ma[pl.ds(k + 1, n)] = i1[pl.ds(k, n)] * b1[pl.ds(k, n)]

    chunks(2, Z1 - 2, first1)
    sweep(ma, mb, b1, 3, Z1 - 3, *mid, i1)
    sweep(mb, ma, b1, 4, Z1 - 4, *mid, i1)

    mids = [
        copy(ma.at[pl.ds(1 + L1, H1)], mid_lo.at[0], mid_send.at[0], mid_recv.at[0], (gx, gy, up)),
        copy(b1.at[pl.ds(L1, H1)], mid_lo.at[1], mid_send.at[1], mid_recv.at[1], (gx, gy, up)),
        copy(ma.at[pl.ds(1 + H1, H1)], mid_hi.at[0], mid_send.at[2], mid_recv.at[2], (gx, gy, down)),
        copy(b1.at[pl.ds(H1, H1)], mid_hi.at[1], mid_send.at[3], mid_recv.at[3], (gx, gy, down)),
    ]

    def resid1(K, n):
        r2[pl.ds(K, n)] = residual(ma, b1, d1, H1 + 2 * K, n, *mid)

    chunks(0, L2, resid1, 8)

    inv = 1.0 / d2[1]
    y_now, p_now = r2[0], jnp.ones((nd, lanes), F32)
    im2[0], spike[0, 0], spike[1, 0] = inv, y_now, p_now

    def chain(start, stop, step, carry, turn=4):
        whole = (stop - start) // turn

        def run(i, carry):
            for u in range(turn):
                carry = step(start + i * turn + u, carry)
            return carry

        carry = lax.fori_loop(0, whole, run, carry)
        for k in range(start + whole * turn, stop):
            carry = step(k, carry)
        return carry

    def forward(k, carry):
        inv, y_now, p_now = carry
        e = z2[k + 1]
        t = e * inv
        inv = 1.0 / (d2[k + 1] - e * t)
        y_now = r2[k] + t * y_now
        p_now = t * p_now
        im2[k], spike[0, k], spike[1, k] = inv, y_now, p_now
        return inv, y_now, p_now

    inv, y_now, p_now = chain(1, L2, forward, (inv, y_now, p_now))
    last = (y_now * inv, p_now * inv, inv)
    for i in range(3):
        spike[i, L2 - 1] = last[i]

    def backward(i, carry):
        g, p, q = carry
        k = L2 - 2 - i
        e, inv = z2[k + 2], im2[k]
        g = inv * (spike[0, k] + e * g)
        p = inv * (spike[1, k] + e * p)
        q = inv * (e * q)
        spike[0, k], spike[1, k], spike[2, k] = g, p, q
        return g, p, q

    head = chain(0, L2 - 1, backward, last)
    for i in range(3):
        iface[gz, i] = head[i]
        iface[gz, 3 + i] = last[i]
    iface[gz, 6] = z2[1] * flat[pl.ds(2 * cz_len + gz, nd, stride=gath.shape[1]), :]
    ifs = []
    for j in range(1, n_z):
        ifs.append(copy(iface.at[gz], iface.at[gz], if_send.at[j], if_recv.at[j],
                        (gx, gy, lax.rem(gz + j, n_z))))
    ifs.append(copy(spike.at[:, pl.ds(L2 - 3, 3)], spk_lo, if_send.at[n_z], if_recv.at[n_z],
                    (gx, gy, up)))
    ifs.append(copy(spike.at[:, pl.ds(0, 3)], spk_hi, if_send.at[n_z + 1], if_recv.at[n_z + 1],
                    (gx, gy, down)))

    for c in states:
        c.wait()

    def splane(row):
        return sflat[pl.ds(row, nd, stride=sgath.shape[1]), :][None]

    def spread_state(i, n):
        for u in range(n):
            s0[pl.ds(1 + i + u, 1)] = splane(i + u)

    chunks(0, cz_len, spread_state)
    s0[0:1] = jnp.where(first_dev, 0.0, splane(cz_len + 7))
    s0[cz_len + 1 :] = jnp.where(last_dev, 0.0, splane(cz_len + 8))

    for c in mids + ifs:
        c.wait()

    zero = jnp.zeros((nd, lanes), F32)
    A, B = zero, zero
    kept = []
    for j in range(n_z):
        c = iface[j, 6]
        g, p, q = iface[j, 0], iface[j, 1], iface[j, 2]
        gl, plast, ql = iface[j, 3], iface[j, 4], iface[j, 5]
        inv = 1.0 / (1.0 - p * c * B)
        F = (g + p * c * A) * inv
        G = q * inv
        kept.append((c, A, B, F, G))
        nxt = iface[j + 1, 6] if j + 1 < n_z else zero
        tail = plast * c
        A, B = gl + tail * (A + B * F), (ql + tail * B * G) * nxt
    right = zero
    for j in reversed(range(n_z)):
        c, A, B, F, G = kept[j]
        head = F + G * right
        sides[j, 0] = c * (A + B * head)
        sides[j, 1] = right
        right = c * head

    L, R = sides[gz, 0], sides[gz, 1]

    def twice(v):
        return jnp.broadcast_to(v[:, None], (v.shape[0], 2, nd, lanes)).reshape(
            2 * v.shape[0], nd, lanes)

    def correct(K, n):
        x = spike[0, pl.ds(K, n)] + spike[1, pl.ds(K, n)] * L + spike[2, pl.ds(K, n)] * R
        k = 1 + H1 + 2 * K
        ma[pl.ds(k, 2 * n)] = ma[pl.ds(k, 2 * n)] + twice(x)

    chunks(0, L2, correct, 8)
    xl = spk_lo[0] + spk_lo[1] * sides[down, 0] + spk_lo[2] * sides[down, 1]
    ma[1 : 1 + H1] = mid_lo[0] + twice(xl)[6 - H1 :]
    b1[0:H1] = mid_lo[1]
    xh = spk_hi[0] + spk_hi[1] * sides[up, 0] + spk_hi[2] * sides[up, 1]
    ma[1 + H1 + L1 : 1 + 2 * H1 + L1] = mid_hi[0] + twice(xh)[:H1]
    b1[H1 + L1 :] = mid_hi[1]

    sweep(ma, mb, b1, 1, Z1 - 1, *mid, i1)
    sweep(mb, ma, b1, 2, Z1 - 2, *mid, i1)
    sweep(ma, mb, b1, 3, Z1 - 3, *mid, i1)

    def raise0(K, n):
        k = 1 + 2 * K
        va[pl.ds(k, 2 * n)] = va[pl.ds(k, 2 * n)] + twice(mb[pl.ds(K + 1, n)])

    chunks(3, Z1 - 3, raise0, 8)
    sweep(va, vb, b0, HALO - 3, HALO + cz_len + 3, *fine, i0)
    sweep(vb, va, b0, HALO - 2, HALO + cz_len + 2, *fine, i0)
    sweep(va, vb, b0, HALO - 1, HALO + cz_len + 1, *fine, i0)

    lo, hi = HALO, HALO + cz_len + 1
    vb[lo : lo + 1] = jnp.where(first_dev, -vb[lo + 1 : lo + 2], vb[lo : lo + 1])
    vb[hi : hi + 1] = jnp.where(last_dev, -vb[hi - 1 : hi], vb[hi : hi + 1])

    def terms(i, n):
        a, s = vb[pl.ds(HALO + 1 + i, n)], s0[pl.ds(1 + i, n)]
        tx = m0["xin"] * ((a - x_next(a, m0)) * (s - x_next(s, m0)))
        ty = m0["yin"] * ((a - y_next(a, m0)) * (s - y_next(s, m0)))
        t = tx + x_prev(tx, m0) + ty + y_prev(ty, m0) + m0["edge"] * (a * s)
        z = (a - vb[pl.ds(HALO + i, n)]) * (s - s0[pl.ds(i, n)])
        z = z + (a - vb[pl.ds(HALO + 2 + i, n)]) * (s - s0[pl.ds(2 + i, n)])
        return jnp.sum(c0[pl.ds(HALO + 1 + i, n)] * (t + 0.5 * z), axis=0)

    acc = lax.fori_loop(0, cz_len // 16, lambda i, acc: acc + terms(16 * i, 16), zero)
    part[gz] = acc
    parts = []
    for j in range(1, n_z):
        parts.append(copy(part.at[gz], part.at[gz], pt_send.at[j], pt_recv.at[j],
                          (gx, gy, lax.rem(gz + j, n_z))))

    vflat = vb.reshape(vb.shape[0] * nd, lanes)
    own = vflat[pl.ds((HALO + 1) * nd + me, cz_len, stride=nd), :]
    adj_ref[...] = own.T.reshape(cx_len, cy_len, cz_len)

    for c in parts:
        c.wait()
    total = part[0]
    for j in range(1, n_z):
        total = total + part[j]
    row = jnp.sum(jnp.where(sub == me, total, 0.0), axis=0, keepdims=True)
    row = jnp.broadcast_to(row, (cx_len, lanes)) * (-1.0 / math.sqrt(n_total))
    width = cy_len // n_z
    for j in range(width):
        here = lane8 == row8 * cy_len + gz * width + j
        grad_ref[:, j : j + 1] = jnp.sum(jnp.where(here, row, 0.0), axis=1, keepdims=True)


def solution(mesh):
    n_x, n_y, n_z = mesh.shape["gx"], mesh.shape["gy"], mesh.shape["gz"]
    nd = n_x * n_y

    def per_device(source, state, log_coef, lateral, owners):
        cx, cy, cz = source.shape
        lanes = cx * cy
        Z0, Z1, Z2, H1 = cz + 2 * HALO, cz // 2 + HALO, cz // 4 + 2, HALO // 2
        V = lambda *shape: pltpu.VMEM(shape, F32)
        pln = lambda k: V(k, nd, lanes)
        D = lambda k: pltpu.SemaphoreType.DMA((k,))
        vm = pl.BlockSpec(memory_space=pltpu.VMEM)
        return pl.pallas_call(
            functools.partial(kernel, n_x, n_y, n_z, cx, cy, cz, cz * n_z),
            out_shape=(
                jax.ShapeDtypeStruct((cx, cy, cz), F32),
                jax.ShapeDtypeStruct((cx, cy // n_z), F32),
            ),
            in_specs=[vm] * 5,
            out_specs=(vm, vm),
            scratch_shapes=[
                V(nd, 2 * cz + 16 + 4 * SEND, lanes), V(nd, cz + 16, lanes),
                V(2 * SEND, lanes), V(2 * SEND, lanes), V(8, lanes), V(8, lanes),
                pln(Z0 + 2), pln(Z0), pln(Z0), pln(Z0 + 1), pln(Z0), pln(Z0), pln(Z0),
                pln(Z0 + 2), pln(Z0 + 2),
                pln(Z1 + 2), pln(Z1), pln(Z1), pln(Z1 + 1), pln(Z1), pln(Z1), pln(Z1),
                pln(Z1 + 2), pln(Z1 + 2),
                pln(Z2 + 2), pln(Z2 + 1), pln(Z2), pln(cz // 4), pln(cz // 4),
                V(3, cz // 4, nd, lanes),
                pln(cz + 2), V(n_z, 7, nd, lanes), V(n_z, 2, nd, lanes),
                V(2, H1, nd, lanes), V(2, H1, nd, lanes),
                V(3, 3, nd, lanes), V(3, 3, nd, lanes), V(n_z, nd, lanes),
                D(nd), D(nd), D(nd), D(nd), D(nd), D(nd),
                D(nd), D(nd), D(2), D(2),
                D(4), D(4), D(n_z + 2), D(n_z + 2), D(n_z), D(n_z),
            ],
            compiler_params=pltpu.CompilerParams(
                collective_id=0, has_side_effects=True, vmem_limit_bytes=56 * 1024 * 1024
            ),
            cost_estimate=pl.CostEstimate(
                flops=100_000_000, bytes_accessed=400_000, transcendentals=20_000
            ),
        )(source, state, log_coef, lateral, owners)

    placed = (
        P("gx", "gy", "gz"),
        P("gx", "gy", "gz"),
        P("gx", "gy", "gz"),
        P("gx", "gy"),
        P("gx", "gy", None),
    )
    return jax.shard_map(
        per_device,
        mesh=mesh,
        in_specs=placed,
        out_specs=(P("gx", "gy", "gz"), P("gx", ("gy", "gz"))),
        check_vma=False,
    )
```

```python
import functools
import math

import jax
import jax.numpy as jnp
from jax import lax
from jax.experimental import pallas as pl
from jax.experimental.pallas import tpu as pltpu
from jax.sharding import PartitionSpec as P

ANISO = 200.0
OMEGA = 0.8
HALO = 10
SEND = 16
MESH = pl.DeviceIdType.MESH
F32 = jnp.float32


def kernel(
    n_x, n_y, n_z, cx_len, cy_len, cz_len, n_total,
    source_ref, state_ref, logc_ref, lat_ref, owners_ref,
    adj_ref, grad_ref,
    gath, sgath, stage_lo, stage_hi, sstage_lo, sstage_hi,
    c0, x0, w0, y0, z0, d0, i0, b0, va, vb,
    c1, x1, w1, y1, z1, d1, i1, b1, ma, mb,
    c2, z2, d2, r2, im2, spike,
    s0, iface, sides, mid_lo, mid_hi, spk_lo, spk_hi, part,
    main_send, main_recv, src_send, src_recv, lo_send, lo_recv, hi_send, hi_recv,
    st_send, st_recv, stz_send, stz_recv,
    mid_send, mid_recv, if_send, if_recv, pt_send, pt_recv,
):
    nd = n_x * n_y
    lanes = cx_len * cy_len
    gx, gy, gz = lax.axis_index("gx"), lax.axis_index("gy"), lax.axis_index("gz")
    me = gx * n_y + gy
    up, down = lax.rem(gz + 1, n_z), lax.rem(gz + n_z - 1, n_z)
    Z0, Z1, Z2 = cz_len + 2 * HALO, cz_len // 2 + HALO, cz_len // 4 + 2
    H1 = HALO // 2
    L1, L2 = cz_len // 2, cz_len // 4

    def place(k, z):
        peer = lax.rem(me + k, nd)
        return (lax.div(peer, n_y), lax.rem(peer, n_y), z)

    barrier = pltpu.get_barrier_semaphore()
    greeted = [place(k, gz) for k in range(1, nd)]
    greeted += [place(k, z) for z in (up, down) for k in range(nd)]
    greeted += [(gx, gy, lax.rem(gz + j, n_z)) for j in range(2, n_z - 1)]
    for device in greeted:
        pl.semaphore_signal(barrier, inc=1, device_id=device, device_id_type=MESH)

    lane = lax.broadcasted_iota(jnp.int32, (nd, lanes), 1)
    sub = lax.broadcasted_iota(jnp.int32, (nd, lanes), 0)
    y_all = n_y * cy_len
    x_row = lanes // y_all
    xm, ys = lane // y_all, lane % y_all
    xs = sub * x_row + xm
    slot = ys // cy_len - sub % n_y
    lane8 = lax.broadcasted_iota(jnp.int32, (cx_len, lanes), 1)
    row8 = lax.broadcasted_iota(jnp.int32, (cx_len, lanes), 0)
    lat = jnp.zeros((cx_len, lanes), F32)
    for y in range(cy_len):
        lat = jnp.where(lane8 % cy_len == y, lat_ref[:, y : y + 1], lat)
    lane_x = lane8 // cy_len % n_y * x_row + lane8 // y_all
    lat = jnp.sum(jnp.where(lane_x == row8, lat, 0.0), axis=0, keepdims=True)

    def rows_of(ref):
        v = ref[...].reshape(n_y, x_row, cy_len, cz_len)
        v = jnp.stack([v[:, i] for i in range(x_row)])
        return v.reshape(lanes, cz_len).T

    coef = jnp.exp(rows_of(logc_ref) + lat)
    src = rows_of(source_ref)
    state = rows_of(state_ref)
    gath[me, 0:cz_len, :] = coef
    gath[me, cz_len + 16 : 2 * cz_len + 16, :] = src
    line = owners_ref[0]
    for j in range(16):
        if 0 < j < n_z:
            same = jnp.broadcast_to(line[:, j : j + 1], (1, lanes)) == jnp.broadcast_to(
                line[:, j - 1 : j], (1, lanes)
            )
            gath[me, cz_len + j : cz_len + j + 1, :] = jnp.where(same, 1.0, 0.0)
        else:
            gath[me, cz_len + j : cz_len + j + 1, :] = jnp.zeros((1, lanes), F32)
    stage_lo[0:SEND, :] = coef[cz_len - SEND :]
    stage_lo[SEND : 2 * SEND, :] = src[cz_len - SEND :]
    stage_hi[0:SEND, :] = coef[:SEND]
    stage_hi[SEND : 2 * SEND, :] = src[:SEND]
    sgath[me, 0:cz_len, :] = state
    sstage_lo[...] = state[cz_len - 8 :]
    sstage_hi[...] = state[:8]
    pl.semaphore_wait(barrier, len(greeted))

    base_lo = 2 * cz_len + 16
    base_hi = base_lo + 2 * SEND
    sent = []

    def copy(src_at, dst_at, ssem, rsem, device):
        c = pltpu.make_async_remote_copy(
            src_ref=src_at, dst_ref=dst_at, send_sem=ssem, recv_sem=rsem,
            device_id=device, device_id_type=MESH,
        )
        c.start()
        return c

    main, los, his = [], [], []
    for k in range(1, nd):
        body = gath.at[me, pl.ds(0, cz_len + 16)]
        main.append(copy(body, body, main_send.at[k], main_recv.at[k], place(k, gz)))
    for k in range(nd):
        los.append(copy(stage_lo, gath.at[me, pl.ds(base_lo, 2 * SEND)],
                        lo_send.at[k], lo_recv.at[k], place(k, up)))
        his.append(copy(stage_hi, gath.at[me, pl.ds(base_hi, 2 * SEND)],
                        hi_send.at[k], hi_recv.at[k], place(k, down)))
    sources = []
    for k in range(1, nd):
        body = gath.at[me, pl.ds(cz_len + 16, cz_len)]
        sources.append(copy(body, body, src_send.at[k], src_recv.at[k], place(k, gz)))

    def roll(v, shift, axis):
        return pltpu.roll(v, shift % v.shape[axis], axis)

    nx_all = n_x * cx_len

    def masks(s):
        ends_x = jnp.where(xs < s, 1.0, 0.0) + jnp.where(xs >= nx_all - s, 1.0, 0.0)
        ends_y = jnp.where(ys < s, 1.0, 0.0) + jnp.where(ys >= y_all - s, 1.0, 0.0)
        return dict(
            s=s, xhi=(xm >= x_row - s)[None], xlo=(xm < s)[None],
            xin=jnp.where(xs >= nx_all - s, 0.0, 0.5)[None],
            yin=jnp.where(ys >= y_all - s, 0.0, 0.5)[None],
            edge=(ends_x + ends_y)[None],
            xbit=(xs // s % 2 == 0)[None], ybit=(ys // s % 2 == 0)[None],
        )

    def pick(mask, a, b):
        return jnp.where(jnp.broadcast_to(mask, a.shape), a, b)

    def x_next(v, m, row=None):
        s = m["s"]
        if s >= x_row:
            return roll(v, -(s // x_row), 1)
        row = roll(v, -1, 1) if row is None else row
        return roll(pick(m["xlo"], row, v), -s * y_all, 2)

    def x_prev(v, m, row=None):
        s = m["s"]
        if s >= x_row:
            return roll(v, s // x_row, 1)
        row = roll(v, 1, 1) if row is None else row
        return roll(pick(m["xhi"], row, v), s * y_all, 2)

    def y_next(v, m):
        return roll(v, -m["s"], 2)

    def y_prev(v, m):
        return roll(v, m["s"], 2)

    def block_mean(pair, m):
        s = m["s"]
        v = pair + pick(m["ybit"], roll(pair, -s, 2), roll(pair, s, 2))
        if s >= x_row:
            near, far = roll(v, -(s // x_row), 1), roll(v, s // x_row, 1)
        else:
            near, far = roll(v, -s * y_all, 2), roll(v, s * y_all, 2)
        return 0.125 * (v + pick(m["xbit"], near, far))

    def to_plane(v):
        out = v
        for shift in range(1 - n_y, n_y):
            if shift:
                moved = roll(roll(v, -shift, 1), shift * cy_len, 2)
                out = pick((slot == shift)[None], moved, out)
        return out

    m0, m1, m2 = masks(1), masks(2), masks(4)
    first_dev, last_dev = gz == 0, gz == n_z - 1
    zero_plane = jnp.zeros((1, nd, lanes), F32)

    def chunks(start, stop, body, step=16):
        whole = (stop - start) // step

        def run(i, carry):
            body(start + i * step, step)
            return carry

        lax.fori_loop(0, whole, run, 0)
        if (stop - start) % step:
            body(start + whole * step, (stop - start) % step)

    def pads(ref):
        ref[0:1] = zero_plane
        ref[ref.shape[0] - 1 :] = zero_plane

    for ref in (c0, va, vb, c1, ma, mb, c2):
        pads(ref)

    def level(c, length, halo, own, scale, m, xr, wr, yr, zr, dr, ir):
        half = 0.5 * scale * ANISO
        c[0:1], c[length + 1 :] = c[1:2], c[length : length + 1]
        lo, hi = halo, halo + own + 1
        c[lo : lo + 1] = jnp.where(first_dev, c[lo + 1 : lo + 2], c[lo : lo + 1])
        c[hi : hi + 1] = jnp.where(last_dev, c[hi - 1 : hi], c[hi : hi + 1])

        def body(k, n):
            here = c[pl.ds(k + 1, n)]
            wz = half * (c[pl.ds(k, n)] + here)
            zr[pl.ds(k, n)] = wz
            wx = (scale * m["xin"]) * (here + x_next(here, m))
            wy = (scale * m["yin"]) * (here + y_next(here, m))
            wp = x_prev(wx, m)
            diag = wx + wp + wy + y_prev(wy, m) + (scale * m["edge"]) * here
            diag = diag + wz + half * (c[pl.ds(k + 2, n)] + here)
            dr[pl.ds(k, n)] = diag
            if xr is not None:
                xr[pl.ds(k, n)] = wx
                wr[pl.ds(k, n)] = wp
                yr[pl.ds(k, n)] = wy
                ir[pl.ds(k, n)] = OMEGA / diag

        chunks(0, length, body)
        zr[0:1] = zero_plane
        zr[length : length + 1] = zero_plane
        lo, hi = halo, halo + own
        zr[lo : lo + 1] = jnp.where(first_dev, 0.0, zr[lo : lo + 1])
        zr[hi : hi + 1] = jnp.where(last_dev, 0.0, zr[hi : hi + 1])

    def pull(v, k, n, m, xr, wr, yr, zr):
        near, wz = v[pl.ds(k, n + 2)], zr[pl.ds(k, n + 1)]
        here = near[1 : n + 1]
        if m["s"] < x_row:
            rows = v.reshape(v.shape[0] * nd, lanes)
            later = rows[pl.ds((k + 1) * nd + 1, n * nd), :].reshape(n, nd, lanes)
            prior = rows[pl.ds((k + 1) * nd - 1, n * nd), :].reshape(n, nd, lanes)
        else:
            later = prior = None
        wy = yr[pl.ds(k, n)]
        total = wz[:n] * near[:n] + wz[1:] * near[2:]
        total = total + (wy * y_next(here, m) + y_prev(wy * here, m))
        total = total + xr[pl.ds(k, n)] * x_next(here, m, later)
        total = total + wr[pl.ds(k, n)] * x_prev(here, m, prior)
        return here, total

    def sweep(v, out, b, start, stop, m, xr, wr, yr, zr, ir):
        def body(k, n):
            here, total = pull(v, k, n, m, xr, wr, yr, zr)
            out[pl.ds(k + 1, n)] = (1.0 - OMEGA) * here + ir[pl.ds(k, n)] * (
                b[pl.ds(k, n)] + total)
        chunks(start, stop, body)

    fine = (m0, x0, w0, y0, z0)
    mid = (m1, x1, w1, y1, z1)

    for c in main:
        c.wait()
    for c in los + his:
        c.wait()
    flat = gath.reshape(nd * gath.shape[1], lanes)
    sflat = sgath.reshape(nd * sgath.shape[1], lanes)

    def planes(rows, height, start, n):
        return to_plane(jnp.stack(
            [rows[pl.ds(start + u, nd, stride=height), :] for u in range(n)]))

    def gplanes(start, n):
        return planes(flat, gath.shape[1], start, n)

    def spread(i, n):
        c0[pl.ds(1 + HALO + i, n)] = gplanes(i, n)

    chunks(0, cz_len, spread)
    c0[1 : 1 + HALO] = gplanes(base_lo + SEND - HALO, HALO)
    b0[0:HALO] = gplanes(base_lo + 2 * SEND - HALO, HALO)
    c0[1 + HALO + cz_len : 1 + 2 * HALO + cz_len] = gplanes(base_hi, HALO)
    b0[HALO + cz_len :] = gplanes(base_hi + SEND, HALO)

    def pairs(ref, k, step):
        v = ref[pl.ds(k, 2 * step)].reshape(step, 2, nd, lanes)
        return v[:, 0] + v[:, 1]

    def coarsen1(K, n):
        c1[pl.ds(K + 1, n)] = block_mean(pairs(c0, 1 + 2 * K, n), m0)

    chunks(0, Z1, coarsen1)

    def coarsen2(K, n):
        c2[pl.ds(K + 1, n)] = block_mean(pairs(c1, 1 + H1 - 2 + 2 * K, n), m1)

    chunks(0, Z2, coarsen2)
    level(c0, Z0, HALO, cz_len, 1.0, m0, x0, w0, y0, z0, d0, i0)
    level(c1, Z1, H1, L1, 0.25, m1, x1, w1, y1, z1, d1, i1)
    level(c2, Z2, 1, L2, 0.0625, m2, None, None, None, z2, d2, None)

    for c in sources:
        c.wait()

    def spread_source(i, n):
        b0[pl.ds(HALO + i, n)] = gplanes(cz_len + 16 + i, n)

    chunks(0, cz_len, spread_source)

    states = []
    for k in range(1, nd):
        body = sgath.at[me, pl.ds(0, cz_len)]
        states.append(copy(body, body, st_send.at[k], st_recv.at[k], place(k, gz)))
    states.append(copy(sstage_lo, sgath.at[me, pl.ds(cz_len, 8)],
                       stz_send.at[0], stz_recv.at[0], (gx, gy, up)))
    states.append(copy(sstage_hi, sgath.at[me, pl.ds(cz_len + 8, 8)],
                       stz_send.at[1], stz_recv.at[1], (gx, gy, down)))


    def first0(k, n):
        va[pl.ds(k + 1, n)] = i0[pl.ds(k, n)] * b0[pl.ds(k, n)]

    chunks(0, Z0, first0)
    sweep(va, vb, b0, 1, Z0 - 1, *fine, i0)
    sweep(vb, va, b0, 2, Z0 - 2, *fine, i0)

    def residual(v, b, d, k, n, m, *weights):
        here, total = pull(v, k, 2 * n, m, *weights)
        r = b[pl.ds(k, 2 * n)] + total - d[pl.ds(k, 2 * n)] * here
        r = r.reshape(n, 2, nd, lanes)
        return block_mean(r[:, 0] + r[:, 1], m)

    def resid0(K, n):
        b1[pl.ds(K, n)] = residual(va, b0, d0, 2 * K, n, *fine)

    chunks(2, Z1 - 2, resid0, 8)

    def first1(k, n):
        ma[pl.ds(k + 1, n)] = i1[pl.ds(k, n)] * b1[pl.ds(k, n)]

    chunks(2, Z1 - 2, first1)
    sweep(ma, mb, b1, 3, Z1 - 3, *mid, i1)
    sweep(mb, ma, b1, 4, Z1 - 4, *mid, i1)

    mids = [
        copy(ma.at[pl.ds(1 + L1, H1)], mid_lo.at[0], mid_send.at[0], mid_recv.at[0], (gx, gy, up)),
        copy(b1.at[pl.ds(L1, H1)], mid_lo.at[1], mid_send.at[1], mid_recv.at[1], (gx, gy, up)),
        copy(ma.at[pl.ds(1 + H1, H1)], mid_hi.at[0], mid_send.at[2], mid_recv.at[2], (gx, gy, down)),
        copy(b1.at[pl.ds(H1, H1)], mid_hi.at[1], mid_send.at[3], mid_recv.at[3], (gx, gy, down)),
    ]

    def resid1(K, n):
        r2[pl.ds(K, n)] = residual(ma, b1, d1, H1 + 2 * K, n, *mid)

    chunks(0, L2, resid1, 8)

    inv = 1.0 / d2[1]
    y_now, p_now = r2[0], jnp.ones((nd, lanes), F32)
    im2[0], spike[0, 0], spike[1, 0] = inv, y_now, p_now

    def chain(start, stop, step, carry, turn=4):
        whole = (stop - start) // turn

        def run(i, carry):
            for u in range(turn):
                carry = step(start + i * turn + u, carry)
            return carry

        carry = lax.fori_loop(0, whole, run, carry)
        for k in range(start + whole * turn, stop):
            carry = step(k, carry)
        return carry

    def forward(k, carry):
        inv, y_now, p_now = carry
        e = z2[k + 1]
        t = e * inv
        inv = 1.0 / (d2[k + 1] - e * t)
        y_now = r2[k] + t * y_now
        p_now = t * p_now
        im2[k], spike[0, k], spike[1, k] = inv, y_now, p_now
        return inv, y_now, p_now

    inv, y_now, p_now = chain(1, L2, forward, (inv, y_now, p_now))
    last = (y_now * inv, p_now * inv, inv)
    for i in range(3):
        spike[i, L2 - 1] = last[i]

    def backward(i, carry):
        g, p, q = carry
        k = L2 - 2 - i
        e, inv = z2[k + 2], im2[k]
        g = inv * (spike[0, k] + e * g)
        p = inv * (spike[1, k] + e * p)
        q = inv * (e * q)
        spike[0, k], spike[1, k], spike[2, k] = g, p, q
        return g, p, q

    head = chain(0, L2 - 1, backward, last)
    for i in range(3):
        iface[gz, i] = head[i]
        iface[gz, 3 + i] = last[i]
    iface[gz, 6] = z2[1] * gplanes(cz_len + gz, 1)[0]
    ifs = []
    for j in range(1, n_z):
        ifs.append(copy(iface.at[gz], iface.at[gz], if_send.at[j], if_recv.at[j],
                        (gx, gy, lax.rem(gz + j, n_z))))
    ifs.append(copy(spike.at[:, pl.ds(L2 - 3, 3)], spk_lo, if_send.at[n_z], if_recv.at[n_z],
                    (gx, gy, up)))
    ifs.append(copy(spike.at[:, pl.ds(0, 3)], spk_hi, if_send.at[n_z + 1], if_recv.at[n_z + 1],
                    (gx, gy, down)))

    for c in states:
        c.wait()

    def splanes(start, n):
        return planes(sflat, sgath.shape[1], start, n)

    def spread_state(i, n):
        s0[pl.ds(1 + i, n)] = splanes(i, n)

    chunks(0, cz_len, spread_state)
    s0[0:1] = jnp.where(first_dev, 0.0, splanes(cz_len + 7, 1))
    s0[cz_len + 1 :] = jnp.where(last_dev, 0.0, splanes(cz_len + 8, 1))

    for c in mids + ifs:
        c.wait()

    zero = jnp.zeros((nd, lanes), F32)
    A, B = zero, zero
    kept = []
    for j in range(n_z):
        c = iface[j, 6]
        g, p, q = iface[j, 0], iface[j, 1], iface[j, 2]
        gl, plast, ql = iface[j, 3], iface[j, 4], iface[j, 5]
        inv = 1.0 / (1.0 - p * c * B)
        F = (g + p * c * A) * inv
        G = q * inv
        kept.append((c, A, B, F, G))
        nxt = iface[j + 1, 6] if j + 1 < n_z else zero
        tail = plast * c
        A, B = gl + tail * (A + B * F), (ql + tail * B * G) * nxt
    right = zero
    for j in reversed(range(n_z)):
        c, A, B, F, G = kept[j]
        head = F + G * right
        sides[j, 0] = c * (A + B * head)
        sides[j, 1] = right
        right = c * head

    L, R = sides[gz, 0], sides[gz, 1]

    def twice(v):
        return jnp.broadcast_to(v[:, None], (v.shape[0], 2, nd, lanes)).reshape(
            2 * v.shape[0], nd, lanes)

    def correct(K, n):
        x = spike[0, pl.ds(K, n)] + spike[1, pl.ds(K, n)] * L + spike[2, pl.ds(K, n)] * R
        k = 1 + H1 + 2 * K
        ma[pl.ds(k, 2 * n)] = ma[pl.ds(k, 2 * n)] + twice(x)

    chunks(0, L2, correct, 8)
    xl = spk_lo[0] + spk_lo[1] * sides[down, 0] + spk_lo[2] * sides[down, 1]
    ma[1 : 1 + H1] = mid_lo[0] + twice(xl)[6 - H1 :]
    b1[0:H1] = mid_lo[1]
    xh = spk_hi[0] + spk_hi[1] * sides[up, 0] + spk_hi[2] * sides[up, 1]
    ma[1 + H1 + L1 : 1 + 2 * H1 + L1] = mid_hi[0] + twice(xh)[:H1]
    b1[H1 + L1 :] = mid_hi[1]

    sweep(ma, mb, b1, 1, Z1 - 1, *mid, i1)
    sweep(mb, ma, b1, 2, Z1 - 2, *mid, i1)
    sweep(ma, mb, b1, 3, Z1 - 3, *mid, i1)

    def raise0(K, n):
        k = 1 + 2 * K
        va[pl.ds(k, 2 * n)] = va[pl.ds(k, 2 * n)] + twice(mb[pl.ds(K + 1, n)])

    chunks(3, Z1 - 3, raise0, 8)
    sweep(va, vb, b0, HALO - 3, HALO + cz_len + 3, *fine, i0)
    sweep(vb, va, b0, HALO - 2, HALO + cz_len + 2, *fine, i0)
    sweep(va, vb, b0, HALO - 1, HALO + cz_len + 1, *fine, i0)

    lo, hi = HALO, HALO + cz_len + 1
    vb[lo : lo + 1] = jnp.where(first_dev, -vb[lo + 1 : lo + 2], vb[lo : lo + 1])
    vb[hi : hi + 1] = jnp.where(last_dev, -vb[hi - 1 : hi], vb[hi : hi + 1])

    def terms(i, n):
        a, s = vb[pl.ds(HALO + 1 + i, n)], s0[pl.ds(1 + i, n)]
        tx = m0["xin"] * ((a - x_next(a, m0)) * (s - x_next(s, m0)))
        ty = m0["yin"] * ((a - y_next(a, m0)) * (s - y_next(s, m0)))
        t = tx + x_prev(tx, m0) + ty + y_prev(ty, m0) + m0["edge"] * (a * s)
        z = (a - vb[pl.ds(HALO + i, n)]) * (s - s0[pl.ds(i, n)])
        z = z + (a - vb[pl.ds(HALO + 2 + i, n)]) * (s - s0[pl.ds(2 + i, n)])
        return jnp.sum(c0[pl.ds(HALO + 1 + i, n)] * (t + 0.5 * z), axis=0)

    acc = lax.fori_loop(0, cz_len // 16, lambda i, acc: acc + terms(16 * i, 16), zero)
    part[gz] = acc
    parts = []
    for j in range(1, n_z):
        parts.append(copy(part.at[gz], part.at[gz], pt_send.at[j], pt_recv.at[j],
                          (gx, gy, lax.rem(gz + j, n_z))))

    vflat = vb.reshape(vb.shape[0] * nd, lanes)
    own = jnp.zeros((cz_len, lanes), F32)
    to_slot = lax.broadcasted_iota(jnp.int32, (cz_len, lanes), 1) // cy_len % n_y
    for a in range(n_y):
        row = vflat[pl.ds((HALO + 1) * nd + gx * n_y + a, cz_len, stride=nd), :]
        moved = pltpu.roll(row, lax.rem((a - gy) * cy_len + lanes, lanes), 1)
        own = jnp.where(to_slot == a, moved, own)
    field = own.T.reshape(x_row, n_y, cy_len, cz_len)
    for a in range(n_y):
        for i in range(x_row):
            adj_ref[a * x_row + i] = field[i, a]

    for c in parts:
        c.wait()
    total = part[0]
    for j in range(1, n_z):
        total = total + part[j]
    rows = jnp.zeros((cx_len, lanes), F32)
    for a in range(n_y):
        row = jnp.sum(jnp.where(sub == gx * n_y + a, total, 0.0), axis=0, keepdims=True)
        rows = jnp.where(row8 // x_row == a, jnp.broadcast_to(row, rows.shape), rows)
    rows = rows * (-1.0 / math.sqrt(n_total))
    width = cy_len // n_z
    for j in range(width):
        here = lane8 == row8 % x_row * y_all + gy * cy_len + gz * width + j
        grad_ref[:, j : j + 1] = jnp.sum(jnp.where(here, rows, 0.0), axis=1, keepdims=True)


def solution(mesh):
    n_x, n_y, n_z = mesh.shape["gx"], mesh.shape["gy"], mesh.shape["gz"]
    nd = n_x * n_y

    def per_device(source, state, log_coef, lateral, owners):
        cx, cy, cz = source.shape
        lanes = cx * cy
        Z0, Z1, Z2, H1 = cz + 2 * HALO, cz // 2 + HALO, cz // 4 + 2, HALO // 2
        V = lambda *shape: pltpu.VMEM(shape, F32)
        pln = lambda k: V(k, nd, lanes)
        D = lambda k: pltpu.SemaphoreType.DMA((k,))
        vm = pl.BlockSpec(memory_space=pltpu.VMEM)
        return pl.pallas_call(
            functools.partial(kernel, n_x, n_y, n_z, cx, cy, cz, cz * n_z),
            out_shape=(
                jax.ShapeDtypeStruct((cx, cy, cz), F32),
                jax.ShapeDtypeStruct((cx, cy // n_z), F32),
            ),
            in_specs=[vm] * 5,
            out_specs=(vm, vm),
            scratch_shapes=[
                V(nd, 2 * cz + 16 + 4 * SEND, lanes), V(nd, cz + 16, lanes),
                V(2 * SEND, lanes), V(2 * SEND, lanes), V(8, lanes), V(8, lanes),
                pln(Z0 + 2), pln(Z0), pln(Z0), pln(Z0), pln(Z0 + 1), pln(Z0), pln(Z0), pln(Z0),
                pln(Z0 + 2), pln(Z0 + 2),
                pln(Z1 + 2), pln(Z1), pln(Z1), pln(Z1), pln(Z1 + 1), pln(Z1), pln(Z1), pln(Z1),
                pln(Z1 + 2), pln(Z1 + 2),
                pln(Z2 + 2), pln(Z2 + 1), pln(Z2), pln(cz // 4), pln(cz // 4),
                V(3, cz // 4, nd, lanes),
                pln(cz + 2), V(n_z, 7, nd, lanes), V(n_z, 2, nd, lanes),
                V(2, H1, nd, lanes), V(2, H1, nd, lanes),
                V(3, 3, nd, lanes), V(3, 3, nd, lanes), V(n_z, nd, lanes),
                D(nd), D(nd), D(nd), D(nd), D(nd), D(nd), D(nd), D(nd),
                D(nd), D(nd), D(2), D(2),
                D(4), D(4), D(n_z + 2), D(n_z + 2), D(n_z), D(n_z),
            ],
            compiler_params=pltpu.CompilerParams(
                collective_id=0, has_side_effects=True, vmem_limit_bytes=56 * 1024 * 1024
            ),
            cost_estimate=pl.CostEstimate(
                flops=100_000_000, bytes_accessed=400_000, transcendentals=20_000
            ),
        )(source, state, log_coef, lateral, owners)

    placed = (
        P("gx", "gy", "gz"),
        P("gx", "gy", "gz"),
        P("gx", "gy", "gz"),
        P("gx", "gy"),
        P("gx", "gy", None),
    )
    return jax.shard_map(
        per_device,
        mesh=mesh,
        in_specs=placed,
        out_specs=(P("gx", "gy", "gz"), P("gx", ("gy", "gz"))),
        check_vma=False,
    )
```

```python
import functools
import math

import jax
import jax.numpy as jnp
from jax import lax
from jax.experimental import pallas as pl
from jax.experimental.pallas import tpu as pltpu
from jax.sharding import PartitionSpec as P

ANISO = 200.0
OMEGA = 0.8
HALO = 10
SEND = 16
MESH = pl.DeviceIdType.MESH
F32 = jnp.float32


def kernel(
    n_x, n_y, n_z, cx_len, cy_len, cz_len, n_total,
    source_ref, state_ref, logc_ref, lat_ref, owners_ref,
    adj_ref, grad_ref,
    ext, stage, gath,
    c0, x0, w0, y0, z0, d0, i0, b0, va, vb,
    c1, x1, w1, y1, z1, d1, i1, b1, ma, mb,
    c2, z2, d2, low, rlow, fac, spike, corr,
    s0, iface, sides, mid_lo, mid_hi, spk_lo, spk_hi, outs, fin, part,
    z_send, z_recv, main_send, main_recv, st_send, st_recv,
    low_send, low_recv, r_send, r_recv,
    mid_send, mid_recv, if_send, if_recv, fin_send, fin_recv, pt_send, pt_recv,
):
    nd = n_x * n_y
    lanes = cx_len * cy_len
    gx, gy, gz = lax.axis_index("gx"), lax.axis_index("gy"), lax.axis_index("gz")
    me = gx * n_y + gy
    up, down = lax.rem(gz + 1, n_z), lax.rem(gz + n_z - 1, n_z)
    parts_n = min(nd, 8)
    own_n = cz_len // parts_n
    mine = lax.rem(me, parts_n)
    group = me - mine
    Z0, Z1, Z2 = own_n + 2 * HALO, own_n // 2 + HALO, own_n // 4 + 2
    H1 = HALO // 2
    L1, L2, NL = own_n // 2, own_n // 4, cz_len // 4
    WIN = own_n + 2 * SEND

    def place(k, z):
        peer = lax.rem(me + k, nd)
        return (lax.div(peer, n_y), lax.rem(peer, n_y), z)

    def member(k):
        peer = group + lax.rem(mine + k, parts_n)
        return peer, (lax.div(peer, n_y), lax.rem(peer, n_y), gz)

    def along(step):
        t = lax.rem(gz * parts_n + mine + step + n_z * parts_n, n_z * parts_n)
        peer = group + lax.rem(t, parts_n)
        return (lax.div(peer, n_y), lax.rem(peer, n_y), lax.div(t, parts_n))

    barrier = pltpu.get_barrier_semaphore()
    greeted = [place(k, gz) for k in range(1, nd)]
    greeted += [(gx, gy, lax.rem(gz + j, n_z)) for j in range(1, n_z)]
    greeted += [along(1), along(-1)]
    for device in greeted:
        pl.semaphore_signal(barrier, inc=1, device_id=device, device_id_type=MESH)

    lane = lax.broadcasted_iota(jnp.int32, (nd, lanes), 1)
    sub = lax.broadcasted_iota(jnp.int32, (nd, lanes), 0)
    y_all = n_y * cy_len
    x_row = lanes // y_all
    xm, ys = lane // y_all, lane % y_all
    xs = sub * x_row + xm
    slot = ys // cy_len - sub % n_y
    lane8 = lax.broadcasted_iota(jnp.int32, (cx_len, lanes), 1)
    row8 = lax.broadcasted_iota(jnp.int32, (cx_len, lanes), 0)
    lat = jnp.zeros((cx_len, lanes), F32)
    for y in range(cy_len):
        lat = jnp.where(lane8 % cy_len == y, lat_ref[:, y : y + 1], lat)
    lane_x = lane8 // cy_len % n_y * x_row + lane8 // y_all
    lat = jnp.sum(jnp.where(lane_x == row8, lat, 0.0), axis=0, keepdims=True)

    def rows_of(ref):
        v = ref[...].reshape(n_y, x_row, cy_len, cz_len)
        v = jnp.stack([v[:, i] for i in range(x_row)])
        return v.reshape(lanes, cz_len).T

    coef = jnp.exp(rows_of(logc_ref) + lat)
    src = rows_of(source_ref)
    state = rows_of(state_ref)
    for i, v in enumerate((coef, src, state)):
        ext[i, SEND : SEND + cz_len, :] = v
        stage[0, i] = v[cz_len - SEND :]
        stage[1, i] = v[:SEND]
    line = owners_ref[0]
    flags = []
    for j in range(SEND):
        if 0 < j < n_z:
            same = jnp.broadcast_to(line[:, j : j + 1], (1, lanes)) == jnp.broadcast_to(
                line[:, j - 1 : j], (1, lanes)
            )
            flags.append(jnp.where(same, 1.0, 0.0))
        else:
            flags.append(jnp.zeros((1, lanes), F32))
    flags = jnp.concatenate(flags, axis=0)
    for j in range(0, cz_len + 2 * SEND, SEND):
        ext[3, j : j + SEND, :] = flags
    pl.semaphore_wait(barrier, len(greeted))

    def copy(src_at, dst_at, ssem, rsem, device):
        c = pltpu.make_async_remote_copy(
            src_ref=src_at, dst_ref=dst_at, send_sem=ssem, recv_sem=rsem,
            device_id=device, device_id_type=MESH,
        )
        c.start()
        return c

    ends = [
        copy(stage.at[0], ext.at[pl.ds(0, 3), pl.ds(0, SEND)], z_send.at[0], z_recv.at[0],
             (gx, gy, up)),
        copy(stage.at[1], ext.at[pl.ds(0, 3), pl.ds(SEND + cz_len, SEND)],
             z_send.at[1], z_recv.at[1], (gx, gy, down)),
    ]
    for c in ends:
        c.wait()

    def window(first, part):
        at = pl.multiple_of(part * own_n, 8)
        return ext.at[pl.ds(first, 2), pl.ds(at, WIN)]

    main, states = [], []
    for first, group_of, ssem, rsem in (
        (0, main, main_send, main_recv), (2, states, st_send, st_recv),
    ):
        for k in range(1, nd):
            part_of = lax.rem(lax.rem(me + k, nd), parts_n)
            group_of.append(copy(window(first, part_of), gath.at[me, pl.ds(first, 2)],
                                 ssem.at[k], rsem.at[k], place(k, gz)))
    gath[me] = ext[:, pl.ds(pl.multiple_of(mine * own_n, 8), WIN), :]

    def roll(v, shift, axis):
        return pltpu.roll(v, shift % v.shape[axis], axis)

    nx_all = n_x * cx_len

    def masks(s):
        ends_x = jnp.where(xs < s, 1.0, 0.0) + jnp.where(xs >= nx_all - s, 1.0, 0.0)
        ends_y = jnp.where(ys < s, 1.0, 0.0) + jnp.where(ys >= y_all - s, 1.0, 0.0)
        return dict(
            s=s, xhi=(xm >= x_row - s)[None], xlo=(xm < s)[None],
            xin=jnp.where(xs >= nx_all - s, 0.0, 0.5)[None],
            yin=jnp.where(ys >= y_all - s, 0.0, 0.5)[None],
            edge=(ends_x + ends_y)[None],
            xbit=(xs // s % 2 == 0)[None], ybit=(ys // s % 2 == 0)[None],
        )

    def pick(mask, a, b):
        return jnp.where(jnp.broadcast_to(mask, a.shape), a, b)

    def x_next(v, m, row=None):
        s = m["s"]
        if s >= x_row:
            return roll(v, -(s // x_row), 1)
        row = roll(v, -1, 1) if row is None else row
        return roll(pick(m["xlo"], row, v), -s * y_all, 2)

    def x_prev(v, m, row=None):
        s = m["s"]
        if s >= x_row:
            return roll(v, s // x_row, 1)
        row = roll(v, 1, 1) if row is None else row
        return roll(pick(m["xhi"], row, v), s * y_all, 2)

    def y_next(v, m):
        return roll(v, -m["s"], 2)

    def y_prev(v, m):
        return roll(v, m["s"], 2)

    def block_mean(pair, m):
        s = m["s"]
        v = pair + pick(m["ybit"], roll(pair, -s, 2), roll(pair, s, 2))
        if s >= x_row:
            near, far = roll(v, -(s // x_row), 1), roll(v, s // x_row, 1)
        else:
            near, far = roll(v, -s * y_all, 2), roll(v, s * y_all, 2)
        return 0.125 * (v + pick(m["xbit"], near, far))

    def to_plane(v):
        out = v
        for shift in range(1 - n_y, n_y):
            if shift:
                moved = roll(roll(v, -shift, 1), shift * cy_len, 2)
                out = pick((slot == shift)[None], moved, out)
        return out

    m0, m1, m2 = masks(1), masks(2), masks(4)
    first_dev = (gz == 0) & (mine == 0)
    last_dev = (gz == n_z - 1) & (mine == parts_n - 1)
    zero_plane = jnp.zeros((1, nd, lanes), F32)

    def chunks(start, stop, body, step=12):
        for k in range(start, stop, step):
            body(k, min(step, stop - k))

    def pads(ref):
        ref[0:1] = zero_plane
        ref[ref.shape[0] - 1 :] = zero_plane

    for ref in (va, vb, ma, mb):
        pads(ref)

    def level(c, length, halo, own, scale, m, xr, wr, yr, zr, dr, ir):
        half = 0.5 * scale * ANISO
        c[0:1], c[length + 1 :] = c[1:2], c[length : length + 1]
        lo, hi = halo, halo + own + 1
        c[lo : lo + 1] = jnp.where(first_dev, c[lo + 1 : lo + 2], c[lo : lo + 1])
        c[hi : hi + 1] = jnp.where(last_dev, c[hi - 1 : hi], c[hi : hi + 1])

        def body(k, n):
            here = c[pl.ds(k + 1, n)]
            wz = half * (c[pl.ds(k, n)] + here)
            zr[pl.ds(k, n)] = wz
            wx = (scale * m["xin"]) * (here + x_next(here, m))
            wy = (scale * m["yin"]) * (here + y_next(here, m))
            wp = x_prev(wx, m)
            diag = wx + wp + wy + y_prev(wy, m) + (scale * m["edge"]) * here
            diag = diag + wz + half * (c[pl.ds(k + 2, n)] + here)
            dr[pl.ds(k, n)] = diag
            if xr is not None:
                xr[pl.ds(k, n)] = wx
                wr[pl.ds(k, n)] = wp
                yr[pl.ds(k, n)] = wy
                ir[pl.ds(k, n)] = OMEGA / diag

        chunks(0, length, body)
        zr[0:1] = zero_plane
        zr[length : length + 1] = zero_plane
        lo, hi = halo, halo + own
        zr[lo : lo + 1] = jnp.where(first_dev, 0.0, zr[lo : lo + 1])
        zr[hi : hi + 1] = jnp.where(last_dev, 0.0, zr[hi : hi + 1])

    def pull(v, k, n, m, xr, wr, yr, zr):
        near, wz = v[pl.ds(k, n + 2)], zr[pl.ds(k, n + 1)]
        here = near[1 : n + 1]
        if m["s"] < x_row:
            rows = v.reshape(v.shape[0] * nd, lanes)
            later = rows[pl.ds((k + 1) * nd + 1, n * nd), :].reshape(n, nd, lanes)
            prior = rows[pl.ds((k + 1) * nd - 1, n * nd), :].reshape(n, nd, lanes)
        else:
            later = prior = None
        wy = yr[pl.ds(k, n)]
        total = wz[:n] * near[:n] + wz[1:] * near[2:]
        total = total + (wy * y_next(here, m) + y_prev(wy * here, m))
        total = total + xr[pl.ds(k, n)] * x_next(here, m, later)
        total = total + wr[pl.ds(k, n)] * x_prev(here, m, prior)
        return here, total

    def sweep(v, out, b, start, stop, m, xr, wr, yr, zr, ir):
        def body(k, n):
            here, total = pull(v, k, n, m, xr, wr, yr, zr)
            out[pl.ds(k + 1, n)] = (1.0 - OMEGA) * here + ir[pl.ds(k, n)] * (
                b[pl.ds(k, n)] + total)
        chunks(start, stop, body)

    fine = (m0, x0, w0, y0, z0)
    mid = (m1, x1, w1, y1, z1)

    for c in main:
        c.wait()
    flat = gath.reshape(nd * 4 * WIN, lanes)

    def planes(which, start, n):
        return to_plane(jnp.stack([
            flat[pl.ds(which * WIN + start + u, nd, stride=4 * WIN), :] for u in range(n)]))

    def spread(k, n):
        c0[pl.ds(1 + k, n)] = planes(0, SEND - HALO + k, n)
        b0[pl.ds(k, n)] = planes(1, SEND - HALO + k, n)

    chunks(0, Z0, spread)

    def pairs(ref, k, step):
        v = ref[pl.ds(k, 2 * step)].reshape(step, 2, nd, lanes)
        return v[:, 0] + v[:, 1]

    def coarsen1(K, n):
        c1[pl.ds(K + 1, n)] = block_mean(pairs(c0, 1 + 2 * K, n), m0)

    chunks(0, Z1, coarsen1)

    def coarsen2(K, n):
        c2[pl.ds(K + 1, n)] = block_mean(pairs(c1, 1 + H1 - 2 + 2 * K, n), m1)

    chunks(0, Z2, coarsen2)
    level(c0, Z0, HALO, own_n, 1.0, m0, x0, w0, y0, z0, d0, i0)
    level(c1, Z1, H1, L1, 0.25, m1, x1, w1, y1, z1, d1, i1)
    level(c2, Z2, 1, L2, 0.0625, m2, None, None, None, z2, d2, None)

    low[mine, 0] = d2[1 : 1 + L2]
    low[mine, 1] = z2[1 : 1 + L2]
    lows = []
    for k in range(1, parts_n):
        lows.append(copy(low.at[mine], low.at[mine], low_send.at[k], low_recv.at[k], member(k)[1]))

    def first0(k, n):
        va[pl.ds(k + 1, n)] = i0[pl.ds(k, n)] * b0[pl.ds(k, n)]

    chunks(0, Z0, first0)
    sweep(va, vb, b0, 1, Z0 - 1, *fine, i0)
    sweep(vb, va, b0, 2, Z0 - 2, *fine, i0)

    def residual(v, b, d, k, n, m, *weights):
        here, total = pull(v, k, 2 * n, m, *weights)
        r = b[pl.ds(k, 2 * n)] + total - d[pl.ds(k, 2 * n)] * here
        r = r.reshape(n, 2, nd, lanes)
        return block_mean(r[:, 0] + r[:, 1], m)

    def resid0(K, n):
        b1[pl.ds(K, n)] = residual(va, b0, d0, 2 * K, n, *fine)

    chunks(2, Z1 - 2, resid0, 8)

    def first1(k, n):
        ma[pl.ds(k + 1, n)] = i1[pl.ds(k, n)] * b1[pl.ds(k, n)]

    chunks(2, Z1 - 2, first1)
    sweep(ma, mb, b1, 3, Z1 - 3, *mid, i1)
    sweep(mb, ma, b1, 4, Z1 - 4, *mid, i1)

    mids = [
        copy(ma.at[pl.ds(1 + L1, H1)], mid_lo.at[0], mid_send.at[0], mid_recv.at[0], along(1)),
        copy(b1.at[pl.ds(L1, H1)], mid_lo.at[1], mid_send.at[1], mid_recv.at[1], along(1)),
        copy(ma.at[pl.ds(1 + H1, H1)], mid_hi.at[0], mid_send.at[2], mid_recv.at[2], along(-1)),
        copy(b1.at[pl.ds(H1, H1)], mid_hi.at[1], mid_send.at[3], mid_recv.at[3], along(-1)),
    ]

    rlow[mine] = residual(ma, b1, d1, H1, L2, *mid)
    rights = []
    for k in range(1, parts_n):
        rights.append(copy(rlow.at[mine], rlow.at[mine], r_send.at[k], r_recv.at[k], member(k)[1]))
    for c in lows:
        c.wait()

    def dk(k):
        return low[k // L2, 0, k % L2]

    def ek(k):
        return low[k // L2, 1, k % L2]

    inv = 1.0 / dk(0)
    fac[2, 0] = inv
    p_now = jnp.ones((nd, lanes), F32)
    forward_p = [p_now]
    for k in range(1, NL):
        e = ek(k)
        t = e * inv
        fac[1, k - 1] = t
        inv = 1.0 / (dk(k) - e * t)
        p_now = t * p_now
        fac[0, k], fac[2, k] = t, inv
        spike[1, k] = p_now
    spike[1, 0] = forward_p[0]
    p, q = p_now * inv, inv
    spike[1, NL - 1], spike[2, NL - 1] = p, q
    last_p, last_q = p, q
    for k in range(NL - 2, -1, -1):
        f = fac[1, k]
        p = spike[1, k] * fac[2, k] + f * p
        q = f * q
        spike[1, k], spike[2, k] = p, q
    for c in states:
        c.wait()
    cut_plane = planes(3, gz, 1)[0]
    for c in rights:
        c.wait()
    y = rlow[0, 0]
    spike[0, 0] = y
    for k in range(1, NL):
        y = rlow[k // L2, k % L2] + fac[0, k] * y
        spike[0, k] = y
    g = y * fac[2, NL - 1]
    spike[0, NL - 1] = g
    last_g = g
    for k in range(NL - 2, -1, -1):
        g = spike[0, k] * fac[2, k] + fac[1, k] * g
        spike[0, k] = g
    for i, (a, b) in enumerate(((g, last_g), (p, last_p), (q, last_q))):
        iface[gz, i], iface[gz, 3 + i] = a, b
    iface[gz, 6] = ek(0) * cut_plane
    ifs = []
    for j in range(1, n_z):
        ifs.append(copy(iface.at[gz], iface.at[gz], if_send.at[j], if_recv.at[j],
                        (gx, gy, lax.rem(gz + j, n_z))))
    ifs.append(copy(spike.at[:, pl.ds(NL - 3, 3)], spk_lo, if_send.at[n_z], if_recv.at[n_z],
                    (gx, gy, up)))
    ifs.append(copy(spike.at[:, pl.ds(0, 3)], spk_hi, if_send.at[n_z + 1], if_recv.at[n_z + 1],
                    (gx, gy, down)))

    s0[...] = planes(2, SEND - 1, own_n + 2)
    s0[0:1] = jnp.where(first_dev, 0.0, s0[0:1])
    s0[own_n + 1 :] = jnp.where(last_dev, 0.0, s0[own_n + 1 :])

    for c in mids + ifs:
        c.wait()

    zero = jnp.zeros((nd, lanes), F32)
    A, B = zero, zero
    kept = []
    for j in range(n_z):
        c = iface[j, 6]
        g, p, q = iface[j, 0], iface[j, 1], iface[j, 2]
        gl, plast, ql = iface[j, 3], iface[j, 4], iface[j, 5]
        inv = 1.0 / (1.0 - p * c * B)
        F = (g + p * c * A) * inv
        G = q * inv
        kept.append((c, A, B, F, G))
        nxt = iface[j + 1, 6] if j + 1 < n_z else zero
        tail = plast * c
        A, B = gl + tail * (A + B * F), (ql + tail * B * G) * nxt
    right = zero
    for j in reversed(range(n_z)):
        c, A, B, F, G = kept[j]
        head = F + G * right
        sides[j, 0] = c * (A + B * head)
        sides[j, 1] = right
        right = c * head

    L, R = sides[gz, 0], sides[gz, 1]

    def twice(v):
        return jnp.broadcast_to(v[:, None], (v.shape[0], 2, nd, lanes)).reshape(
            2 * v.shape[0], nd, lanes)

    corr[3 : 3 + NL] = spike[0] + spike[1] * L + spike[2] * R
    corr[0:3] = spk_lo[0] + spk_lo[1] * sides[down, 0] + spk_lo[2] * sides[down, 1]
    corr[3 + NL :] = spk_hi[0] + spk_hi[1] * sides[up, 0] + spk_hi[2] * sides[up, 1]
    near = twice(corr[pl.ds(mine * L2, L2 + 6)])
    ma[1 : 1 + H1] = mid_lo[0]
    ma[1 + H1 + L1 : 1 + 2 * H1 + L1] = mid_hi[0]
    ma[1 : 1 + Z1] = ma[1 : 1 + Z1] + near[6 - H1 : 6 - H1 + Z1]
    b1[0:H1] = mid_lo[1]
    b1[H1 + L1 :] = mid_hi[1]

    sweep(ma, mb, b1, 1, Z1 - 1, *mid, i1)
    sweep(mb, ma, b1, 2, Z1 - 2, *mid, i1)
    sweep(ma, mb, b1, 3, Z1 - 3, *mid, i1)

    def raise0(K, n):
        k = 1 + 2 * K
        va[pl.ds(k, 2 * n)] = va[pl.ds(k, 2 * n)] + twice(mb[pl.ds(K + 1, n)])

    chunks(3, Z1 - 3, raise0, 8)
    sweep(va, vb, b0, HALO - 3, HALO + own_n + 3, *fine, i0)
    sweep(vb, va, b0, HALO - 2, HALO + own_n + 2, *fine, i0)
    sweep(va, vb, b0, HALO - 1, HALO + own_n + 1, *fine, i0)

    lo, hi = HALO, HALO + own_n + 1
    vb[lo : lo + 1] = jnp.where(first_dev, -vb[lo + 1 : lo + 2], vb[lo : lo + 1])
    vb[hi : hi + 1] = jnp.where(last_dev, -vb[hi - 1 : hi], vb[hi : hi + 1])

    def terms(i, n):
        a, s = vb[pl.ds(HALO + 1 + i, n)], s0[pl.ds(1 + i, n)]
        tx = m0["xin"] * ((a - x_next(a, m0)) * (s - x_next(s, m0)))
        ty = m0["yin"] * ((a - y_next(a, m0)) * (s - y_next(s, m0)))
        t = tx + x_prev(tx, m0) + ty + y_prev(ty, m0) + m0["edge"] * (a * s)
        z = (a - vb[pl.ds(HALO + i, n)]) * (s - s0[pl.ds(i, n)])
        z = z + (a - vb[pl.ds(HALO + 2 + i, n)]) * (s - s0[pl.ds(2 + i, n)])
        return jnp.sum(c0[pl.ds(HALO + 1 + i, n)] * (t + 0.5 * z), axis=0)

    acc = terms(0, own_n)

    vb[HALO + 1 : HALO + 1 + own_n] = to_plane(vb[HALO + 1 : HALO + 1 + own_n])
    va[0] = to_plane(acc[None])[0]
    vflat = vb.reshape(vb.shape[0] * nd, lanes)
    for d in range(nd):
        outs[d, 0:own_n, :] = vflat[pl.ds((HALO + 1) * nd + d, own_n, stride=nd), :]
        outs[d, own_n:, :] = jnp.broadcast_to(va[0, d : d + 1, :], (8, lanes))
    fins = []
    for k in range(1, parts_n):
        peer, device = member(k)
        fins.append(copy(outs.at[peer], fin.at[mine], fin_send.at[k], fin_recv.at[k], device))
    fin[mine] = outs[me]
    for c in fins:
        c.wait()
    sums = fin[0, own_n:, :]
    for i in range(1, parts_n):
        sums = sums + fin[i, own_n:, :]
    part[gz] = sums
    parts = []
    for j in range(1, n_z):
        parts.append(copy(part.at[gz], part.at[gz], pt_send.at[j], pt_recv.at[j],
                          (gx, gy, lax.rem(gz + j, n_z))))
    field = fin[:, 0:own_n, :].reshape(cz_len, lanes).T.reshape(x_row, n_y, cy_len, cz_len)
    for a in range(n_y):
        for i in range(x_row):
            adj_ref[a * x_row + i] = field[i, a]

    for c in parts:
        c.wait()
    total = part[0]
    for j in range(1, n_z):
        total = total + part[j]
    rows = total[0:cx_len] * (-1.0 / math.sqrt(n_total))
    width = cy_len // n_z
    for j in range(width):
        here = lane8 == row8 % x_row * y_all + row8 // x_row * cy_len + gz * width + j
        grad_ref[:, j : j + 1] = jnp.sum(jnp.where(here, rows, 0.0), axis=1, keepdims=True)


def solution(mesh):
    n_x, n_y, n_z = mesh.shape["gx"], mesh.shape["gy"], mesh.shape["gz"]
    nd = n_x * n_y

    def per_device(source, state, log_coef, lateral, owners):
        cx, cy, cz = source.shape
        lanes = cx * cy
        parts_n = min(nd, 8)
        own = cz // parts_n
        Z0, Z1, Z2, H1 = own + 2 * HALO, own // 2 + HALO, own // 4 + 2, HALO // 2
        L2, NL = own // 4, cz // 4
        V = lambda *shape: pltpu.VMEM(shape, F32)
        pln = lambda k: V(k, nd, lanes)
        D = lambda k: pltpu.SemaphoreType.DMA((k,))
        vm = pl.BlockSpec(memory_space=pltpu.VMEM)
        return pl.pallas_call(
            functools.partial(kernel, n_x, n_y, n_z, cx, cy, cz, cz * n_z),
            out_shape=(
                jax.ShapeDtypeStruct((cx, cy, cz), F32),
                jax.ShapeDtypeStruct((cx, cy // n_z), F32),
            ),
            in_specs=[vm] * 5,
            out_specs=(vm, vm),
            scratch_shapes=[
                V(4, cz + 2 * SEND, lanes), V(2, 3, SEND, lanes),
                V(nd, 4, own + 2 * SEND, lanes),
                pln(Z0 + 2), pln(Z0), pln(Z0), pln(Z0), pln(Z0 + 1), pln(Z0), pln(Z0), pln(Z0),
                pln(Z0 + 2), pln(Z0 + 2),
                pln(Z1 + 2), pln(Z1), pln(Z1), pln(Z1), pln(Z1 + 1), pln(Z1), pln(Z1), pln(Z1),
                pln(Z1 + 2), pln(Z1 + 2),
                pln(Z2 + 2), pln(Z2 + 1), pln(Z2),
                V(parts_n, 2, L2, nd, lanes), V(parts_n, L2, nd, lanes),
                V(3, NL, nd, lanes), V(3, NL, nd, lanes), pln(NL + 6),
                pln(own + 2), V(n_z, 7, nd, lanes), V(n_z, 2, nd, lanes),
                V(2, H1, nd, lanes), V(2, H1, nd, lanes),
                V(3, 3, nd, lanes), V(3, 3, nd, lanes),
                V(nd, own + 8, lanes), V(parts_n, own + 8, lanes), V(n_z, 8, lanes),
                D(2), D(2), D(nd), D(nd), D(nd), D(nd),
                D(nd), D(nd), D(nd), D(nd),
                D(4), D(4), D(n_z + 2), D(n_z + 2), D(nd), D(nd), D(n_z), D(n_z),
            ],
            compiler_params=pltpu.CompilerParams(
                collective_id=0, has_side_effects=True, vmem_limit_bytes=56 * 1024 * 1024
            ),
            cost_estimate=pl.CostEstimate(
                flops=100_000_000, bytes_accessed=400_000, transcendentals=20_000
            ),
        )(source, state, log_coef, lateral, owners)

    placed = (
        P("gx", "gy", "gz"),
        P("gx", "gy", "gz"),
        P("gx", "gy", "gz"),
        P("gx", "gy"),
        P("gx", "gy", None),
    )
    return jax.shard_map(
        per_device,
        mesh=mesh,
        in_specs=placed,
        out_specs=(P("gx", "gy", "gz"), P("gx", ("gy", "gz"))),
        check_vma=False,
    )
```

```python
import functools
import math

import jax
import jax.numpy as jnp
from jax import lax
from jax.experimental import pallas as pl
from jax.experimental.pallas import tpu as pltpu
from jax.sharding import PartitionSpec as P

ANISO = 200.0
OMEGA = 0.8
HALO = 10
SEND = 16
MESH = pl.DeviceIdType.MESH
F32 = jnp.float32


def kernel(
    n_x, n_y, n_z, cx_len, cy_len, cz_len, n_total,
    source_ref, state_ref, logc_ref, lat_ref, owners_ref,
    adj_ref, grad_ref,
    ext, gath,
    c0, x0, w0, y0, z0, d0, i0, b0, va, vb,
    c1, x1, w1, y1, z1, d1, i1, b1, ma, mb,
    c2, z2, d2, low, rlow, fac, spike, corr,
    s0, iface, sides, mid_lo, mid_hi, spk_lo, spk_hi, outs, fin, part,
    z_send, z_recv, main_send, main_recv, st_send, st_recv,
    low_send, low_recv, r_send, r_recv,
    mid_send, mid_recv, if_send, if_recv, fin_send, fin_recv, pt_send, pt_recv,
):
    nd = n_x * n_y
    lanes = cx_len * cy_len
    gx, gy, gz = lax.axis_index("gx"), lax.axis_index("gy"), lax.axis_index("gz")
    me = gx * n_y + gy
    up, down = lax.rem(gz + 1, n_z), lax.rem(gz + n_z - 1, n_z)
    parts_n = min(nd, 8)
    own_n = cz_len // parts_n
    mine = lax.rem(me, parts_n)
    group = me - mine
    Z0, Z1, Z2 = own_n + 2 * HALO, own_n // 2 + HALO, own_n // 4 + 2
    H1 = HALO // 2
    L1, L2, NL = own_n // 2, own_n // 4, cz_len // 4
    WIN = own_n + 2 * SEND

    def place(k, z):
        peer = lax.rem(me + k, nd)
        return (lax.div(peer, n_y), lax.rem(peer, n_y), z)

    def member(k):
        peer = group + lax.rem(mine + k, parts_n)
        return peer, (lax.div(peer, n_y), lax.rem(peer, n_y), gz)

    def along(step):
        t = lax.rem(gz * parts_n + mine + step + n_z * parts_n, n_z * parts_n)
        peer = group + lax.rem(t, parts_n)
        return (lax.div(peer, n_y), lax.rem(peer, n_y), lax.div(t, parts_n))

    barrier = pltpu.get_barrier_semaphore()
    greeted = [place(k, gz) for k in range(1, nd)]
    greeted += [(gx, gy, lax.rem(gz + j, n_z)) for j in range(1, n_z)]
    greeted += [along(1), along(-1)]
    groups = nd // parts_n

    def greet(devices):
        for device in devices:
            pl.semaphore_signal(barrier, inc=1, device_id=device, device_id_type=MESH)

    greet(greeted)
    pl.when(mine == 0)(lambda: greet([place(k, down) for k in range(nd)]))
    pl.when(mine == parts_n - 1)(lambda: greet([place(k, up) for k in range(nd)]))

    lane = lax.broadcasted_iota(jnp.int32, (nd, lanes), 1)
    sub = lax.broadcasted_iota(jnp.int32, (nd, lanes), 0)
    y_all = n_y * cy_len
    x_row = lanes // y_all
    xm, ys = lane // y_all, lane % y_all
    xs = sub * x_row + xm
    slot = ys // cy_len - sub % n_y
    lane8 = lax.broadcasted_iota(jnp.int32, (cx_len, lanes), 1)
    row8 = lax.broadcasted_iota(jnp.int32, (cx_len, lanes), 0)
    lat = jnp.zeros((cx_len, lanes), F32)
    for y in range(cy_len):
        lat = jnp.where(lane8 % cy_len == y, lat_ref[:, y : y + 1], lat)
    lane_x = lane8 // cy_len % n_y * x_row + lane8 // y_all
    lat = jnp.sum(jnp.where(lane_x == row8, lat, 0.0), axis=0, keepdims=True)

    def rows_of(ref):
        v = ref[...].reshape(n_y, x_row, cy_len, cz_len)
        v = jnp.stack([v[:, i] for i in range(x_row)])
        return v.reshape(lanes, cz_len).T

    coef = jnp.exp(rows_of(logc_ref) + lat)
    src = rows_of(source_ref)
    for i, v in enumerate((coef, src)):
        ext[i, SEND : SEND + cz_len, :] = v
        ext[i, 0:SEND, :] = jnp.zeros((SEND, lanes), F32)
        ext[i, SEND + cz_len :, :] = jnp.zeros((SEND, lanes), F32)
    pl.semaphore_wait(barrier, len(greeted) + 2 * groups)

    def copy(src_at, dst_at, ssem, rsem, device):
        c = pltpu.make_async_remote_copy(
            src_ref=src_at, dst_ref=dst_at, send_sem=ssem, recv_sem=rsem,
            device_id=device, device_id_type=MESH,
        )
        c.start()
        return c

    def window(first, part):
        at = pl.multiple_of(part * own_n, 8)
        return ext.at[pl.ds(first, 2), pl.ds(at, WIN)]

    def deal(first, ssem, rsem):
        sent = []
        for k in range(1, nd):
            part_of = lax.rem(lax.rem(me + k, nd), parts_n)
            sent.append(copy(window(first, part_of), gath.at[me, pl.ds(first, 2), pl.ds(0, WIN)],
                             ssem.at[k], rsem.at[k], place(k, gz)))
        return sent

    def beyond(first, at):
        sent = []
        for i in range(groups):
            for end, row, z, to in (
                (0, cz_len, up, i * parts_n), (1, SEND, down, (i + 1) * parts_n - 1),
            ):
                sent.append(copy(
                    ext.at[pl.ds(first, 2), pl.ds(row, SEND)],
                    gath.at[me, pl.ds(first, 2), pl.ds(WIN + end * SEND, SEND)],
                    z_send.at[at + 2 * i + end], z_recv.at[at * nd // 2 // groups + me],
                    (to // n_y, to % n_y, z)))
        return sent

    def beyond_wait(first, at, sent):
        for c in sent:
            c.wait_send()

        def arrive(end):
            for d in range(nd):
                pltpu.make_async_remote_copy(
                    src_ref=ext.at[pl.ds(first, 2), pl.ds(0, SEND)],
                    dst_ref=gath.at[d, pl.ds(first, 2), pl.ds(WIN + end * SEND, SEND)],
                    send_sem=z_send.at[0], recv_sem=z_recv.at[at * nd // 2 // groups + d],
                    device_id=place(1, gz), device_id_type=MESH,
                ).wait_recv()

        pl.when(mine == 0)(lambda: arrive(0))
        pl.when(mine == parts_n - 1)(lambda: arrive(1))

    main = deal(0, main_send, main_recv)
    main_z = beyond(0, 0)
    ext[2, SEND : SEND + cz_len, :] = rows_of(state_ref)
    ext[2, 0:SEND, :] = jnp.zeros((SEND, lanes), F32)
    ext[2, SEND + cz_len :, :] = jnp.zeros((SEND, lanes), F32)
    line = owners_ref[0]
    flags = []
    for j in range(SEND):
        if 0 < j < n_z:
            same = jnp.broadcast_to(line[:, j : j + 1], (1, lanes)) == jnp.broadcast_to(
                line[:, j - 1 : j], (1, lanes)
            )
            flags.append(jnp.where(same, 1.0, 0.0))
        else:
            flags.append(jnp.zeros((1, lanes), F32))
    flags = jnp.concatenate(flags, axis=0)
    for j in range(0, cz_len + 2 * SEND, SEND):
        ext[3, j : j + SEND, :] = flags
    states = deal(2, st_send, st_recv)
    states_z = beyond(2, 2 * groups)
    gath[me, :, 0:WIN, :] = ext[:, pl.ds(pl.multiple_of(mine * own_n, 8), WIN), :]
    from_lo = (parts_n - 1 - mine) // (parts_n - 1) * WIN
    from_hi = mine // (parts_n - 1) * (2 * SEND)
    HIGH = WIN + 2 * SEND

    def roll(v, shift, axis):
        return pltpu.roll(v, shift % v.shape[axis], axis)

    nx_all = n_x * cx_len

    def masks(s):
        ends_x = jnp.where(xs < s, 1.0, 0.0) + jnp.where(xs >= nx_all - s, 1.0, 0.0)
        ends_y = jnp.where(ys < s, 1.0, 0.0) + jnp.where(ys >= y_all - s, 1.0, 0.0)
        return dict(
            s=s, xhi=(xm >= x_row - s)[None], xlo=(xm < s)[None],
            xin=jnp.where(xs >= nx_all - s, 0.0, 0.5)[None],
            yin=jnp.where(ys >= y_all - s, 0.0, 0.5)[None],
            edge=(ends_x + ends_y)[None],
            xbit=(xs // s % 2 == 0)[None], ybit=(ys // s % 2 == 0)[None],
        )

    def pick(mask, a, b):
        return jnp.where(jnp.broadcast_to(mask, a.shape), a, b)

    def x_next(v, m, row=None):
        s = m["s"]
        if s >= x_row:
            return roll(v, -(s // x_row), 1)
        row = roll(v, -1, 1) if row is None else row
        return roll(pick(m["xlo"], row, v), -s * y_all, 2)

    def x_prev(v, m, row=None):
        s = m["s"]
        if s >= x_row:
            return roll(v, s // x_row, 1)
        row = roll(v, 1, 1) if row is None else row
        return roll(pick(m["xhi"], row, v), s * y_all, 2)

    def y_next(v, m):
        return roll(v, -m["s"], 2)

    def y_prev(v, m):
        return roll(v, m["s"], 2)

    def block_mean(pair, m):
        s = m["s"]
        v = pair + pick(m["ybit"], roll(pair, -s, 2), roll(pair, s, 2))
        if s >= x_row:
            near, far = roll(v, -(s // x_row), 1), roll(v, s // x_row, 1)
        else:
            near, far = roll(v, -s * y_all, 2), roll(v, s * y_all, 2)
        return 0.125 * (v + pick(m["xbit"], near, far))

    def to_plane(v):
        out = v
        for shift in range(1 - n_y, n_y):
            if shift:
                moved = roll(roll(v, -shift, 1), shift * cy_len, 2)
                out = pick((slot == shift)[None], moved, out)
        return out

    m0, m1, m2 = masks(1), masks(2), masks(4)
    first_dev = (gz == 0) & (mine == 0)
    last_dev = (gz == n_z - 1) & (mine == parts_n - 1)
    zero_plane = jnp.zeros((1, nd, lanes), F32)

    def chunks(start, stop, body, step=12):
        for k in range(start, stop, step):
            body(k, min(step, stop - k))

    def pads(ref):
        ref[0:1] = zero_plane
        ref[ref.shape[0] - 1 :] = zero_plane

    for ref in (va, vb, ma, mb):
        pads(ref)

    def level(c, length, halo, own, scale, m, xr, wr, yr, zr, dr, ir):
        half = 0.5 * scale * ANISO
        c[0:1], c[length + 1 :] = c[1:2], c[length : length + 1]
        lo, hi = halo, halo + own + 1
        c[lo : lo + 1] = jnp.where(first_dev, c[lo + 1 : lo + 2], c[lo : lo + 1])
        c[hi : hi + 1] = jnp.where(last_dev, c[hi - 1 : hi], c[hi : hi + 1])

        def body(k, n):
            here = c[pl.ds(k + 1, n)]
            wz = half * (c[pl.ds(k, n)] + here)
            zr[pl.ds(k, n)] = wz
            wx = (scale * m["xin"]) * (here + x_next(here, m))
            wy = (scale * m["yin"]) * (here + y_next(here, m))
            wp = x_prev(wx, m)
            diag = wx + wp + wy + y_prev(wy, m) + (scale * m["edge"]) * here
            diag = diag + wz + half * (c[pl.ds(k + 2, n)] + here)
            dr[pl.ds(k, n)] = diag
            if xr is not None:
                xr[pl.ds(k, n)] = wx
                wr[pl.ds(k, n)] = wp
                yr[pl.ds(k, n)] = wy
                ir[pl.ds(k, n)] = OMEGA / diag

        chunks(0, length, body)
        zr[0:1] = zero_plane
        zr[length : length + 1] = zero_plane
        lo, hi = halo, halo + own
        zr[lo : lo + 1] = jnp.where(first_dev, 0.0, zr[lo : lo + 1])
        zr[hi : hi + 1] = jnp.where(last_dev, 0.0, zr[hi : hi + 1])

    def pull(v, k, n, m, xr, wr, yr, zr):
        near, wz = v[pl.ds(k, n + 2)], zr[pl.ds(k, n + 1)]
        here = near[1 : n + 1]
        if m["s"] < x_row:
            rows = v.reshape(v.shape[0] * nd, lanes)
            later = rows[pl.ds((k + 1) * nd + 1, n * nd), :].reshape(n, nd, lanes)
            prior = rows[pl.ds((k + 1) * nd - 1, n * nd), :].reshape(n, nd, lanes)
        else:
            later = prior = None
        wy = yr[pl.ds(k, n)]
        total = wz[:n] * near[:n] + wz[1:] * near[2:]
        total = total + (wy * y_next(here, m) + y_prev(wy * here, m))
        total = total + xr[pl.ds(k, n)] * x_next(here, m, later)
        total = total + wr[pl.ds(k, n)] * x_prev(here, m, prior)
        return here, total

    def sweep(v, out, b, start, stop, m, xr, wr, yr, zr, ir):
        def body(k, n):
            here, total = pull(v, k, n, m, xr, wr, yr, zr)
            out[pl.ds(k + 1, n)] = (1.0 - OMEGA) * here + ir[pl.ds(k, n)] * (
                b[pl.ds(k, n)] + total)
        chunks(start, stop, body)

    fine = (m0, x0, w0, y0, z0)
    mid = (m1, x1, w1, y1, z1)

    for c in main:
        c.wait()
    beyond_wait(0, 0, main_z)
    flat = gath.reshape(nd * 4 * HIGH, lanes)

    def planes(which, start, n):
        return to_plane(jnp.stack([
            flat[pl.ds(which * HIGH + start + u, nd, stride=4 * HIGH), :] for u in range(n)]))

    def spread(k, n):
        c0[pl.ds(1 + k, n)] = planes(0, SEND - HALO + k, n)
        b0[pl.ds(k, n)] = planes(1, SEND - HALO + k, n)

    chunks(HALO, HALO + own_n, spread)
    for which, ref, pad in ((0, c0, 1), (1, b0, 0)):
        ref[pad : pad + HALO] = planes(which, from_lo + SEND - HALO, HALO)
        hi = pad + HALO + own_n
        ref[hi : hi + HALO] = planes(which, from_hi + SEND + own_n, HALO)

    def pairs(ref, k, step):
        v = ref[pl.ds(k, 2 * step)].reshape(step, 2, nd, lanes)
        return v[:, 0] + v[:, 1]

    def coarsen1(K, n):
        c1[pl.ds(K + 1, n)] = block_mean(pairs(c0, 1 + 2 * K, n), m0)

    chunks(0, Z1, coarsen1)

    def coarsen2(K, n):
        c2[pl.ds(K + 1, n)] = block_mean(pairs(c1, 1 + H1 - 2 + 2 * K, n), m1)

    chunks(0, Z2, coarsen2)
    level(c0, Z0, HALO, own_n, 1.0, m0, x0, w0, y0, z0, d0, i0)
    level(c1, Z1, H1, L1, 0.25, m1, x1, w1, y1, z1, d1, i1)
    level(c2, Z2, 1, L2, 0.0625, m2, None, None, None, z2, d2, None)

    low[mine, 0] = d2[1 : 1 + L2]
    low[mine, 1] = z2[1 : 1 + L2]
    lows = []
    for k in range(1, parts_n):
        lows.append(copy(low.at[mine], low.at[mine], low_send.at[k], low_recv.at[k], member(k)[1]))

    def first0(k, n):
        va[pl.ds(k + 1, n)] = i0[pl.ds(k, n)] * b0[pl.ds(k, n)]

    chunks(0, Z0, first0)
    sweep(va, vb, b0, 1, Z0 - 1, *fine, i0)
    sweep(vb, va, b0, 2, Z0 - 2, *fine, i0)

    def residual(v, b, d, k, n, m, *weights):
        here, total = pull(v, k, 2 * n, m, *weights)
        r = b[pl.ds(k, 2 * n)] + total - d[pl.ds(k, 2 * n)] * here
        r = r.reshape(n, 2, nd, lanes)
        return block_mean(r[:, 0] + r[:, 1], m)

    def resid0(K, n):
        b1[pl.ds(K, n)] = residual(va, b0, d0, 2 * K, n, *fine)

    chunks(2, Z1 - 2, resid0, 8)

    def first1(k, n):
        ma[pl.ds(k + 1, n)] = i1[pl.ds(k, n)] * b1[pl.ds(k, n)]

    chunks(2, Z1 - 2, first1)
    sweep(ma, mb, b1, 3, Z1 - 3, *mid, i1)
    sweep(mb, ma, b1, 4, Z1 - 4, *mid, i1)

    mids = [
        copy(ma.at[pl.ds(1 + L1, H1)], mid_lo.at[0], mid_send.at[0], mid_recv.at[0], along(1)),
        copy(b1.at[pl.ds(L1, H1)], mid_lo.at[1], mid_send.at[1], mid_recv.at[1], along(1)),
        copy(ma.at[pl.ds(1 + H1, H1)], mid_hi.at[0], mid_send.at[2], mid_recv.at[2], along(-1)),
        copy(b1.at[pl.ds(H1, H1)], mid_hi.at[1], mid_send.at[3], mid_recv.at[3], along(-1)),
    ]

    rlow[mine] = residual(ma, b1, d1, H1, L2, *mid)
    rights = []
    for k in range(1, parts_n):
        rights.append(copy(rlow.at[mine], rlow.at[mine], r_send.at[k], r_recv.at[k], member(k)[1]))
    for c in lows:
        c.wait()

    def dk(k):
        return low[k // L2, 0, k % L2]

    def ek(k):
        return low[k // L2, 1, k % L2]

    inv = 1.0 / dk(0)
    fac[2, 0] = inv
    p_now = jnp.ones((nd, lanes), F32)
    forward_p = [p_now]
    for k in range(1, NL):
        e = ek(k)
        t = e * inv
        fac[1, k - 1] = t
        inv = 1.0 / (dk(k) - e * t)
        p_now = t * p_now
        fac[0, k], fac[2, k] = t, inv
        spike[1, k] = p_now
    spike[1, 0] = forward_p[0]
    p, q = p_now * inv, inv
    spike[1, NL - 1], spike[2, NL - 1] = p, q
    last_p, last_q = p, q
    for k in range(NL - 2, -1, -1):
        f = fac[1, k]
        p = spike[1, k] * fac[2, k] + f * p
        q = f * q
        spike[1, k], spike[2, k] = p, q
    for c in states:
        c.wait()
    beyond_wait(2, 2 * groups, states_z)
    cut_plane = planes(3, SEND + gz, 1)[0]
    for c in rights:
        c.wait()
    y = rlow[0, 0]
    spike[0, 0] = y
    for k in range(1, NL):
        y = rlow[k // L2, k % L2] + fac[0, k] * y
        spike[0, k] = y
    g = y * fac[2, NL - 1]
    spike[0, NL - 1] = g
    last_g = g
    for k in range(NL - 2, -1, -1):
        g = spike[0, k] * fac[2, k] + fac[1, k] * g
        spike[0, k] = g
    for i, (a, b) in enumerate(((g, last_g), (p, last_p), (q, last_q))):
        iface[gz, i], iface[gz, 3 + i] = a, b
    iface[gz, 6] = ek(0) * cut_plane
    ifs = []
    for j in range(1, n_z):
        ifs.append(copy(iface.at[gz], iface.at[gz], if_send.at[j], if_recv.at[j],
                        (gx, gy, lax.rem(gz + j, n_z))))
    ifs.append(copy(spike.at[:, pl.ds(NL - 3, 3)], spk_lo, if_send.at[n_z], if_recv.at[n_z],
                    (gx, gy, up)))
    ifs.append(copy(spike.at[:, pl.ds(0, 3)], spk_hi, if_send.at[n_z + 1], if_recv.at[n_z + 1],
                    (gx, gy, down)))

    s0[1 : own_n + 1] = planes(2, SEND, own_n)
    s0[0:1] = planes(2, from_lo + SEND - 1, 1)
    s0[own_n + 1 :] = planes(2, from_hi + SEND + own_n, 1)
    s0[0:1] = jnp.where(first_dev, 0.0, s0[0:1])
    s0[own_n + 1 :] = jnp.where(last_dev, 0.0, s0[own_n + 1 :])

    for c in mids + ifs:
        c.wait()

    zero = jnp.zeros((nd, lanes), F32)
    A, B = zero, zero
    kept = []
    for j in range(n_z):
        c = iface[j, 6]
        g, p, q = iface[j, 0], iface[j, 1], iface[j, 2]
        gl, plast, ql = iface[j, 3], iface[j, 4], iface[j, 5]
        inv = 1.0 / (1.0 - p * c * B)
        F = (g + p * c * A) * inv
        G = q * inv
        kept.append((c, A, B, F, G))
        nxt = iface[j + 1, 6] if j + 1 < n_z else zero
        tail = plast * c
        A, B = gl + tail * (A + B * F), (ql + tail * B * G) * nxt
    right = zero
    for j in reversed(range(n_z)):
        c, A, B, F, G = kept[j]
        head = F + G * right
        sides[j, 0] = c * (A + B * head)
        sides[j, 1] = right
        right = c * head

    L, R = sides[gz, 0], sides[gz, 1]

    def twice(v):
        return jnp.broadcast_to(v[:, None], (v.shape[0], 2, nd, lanes)).reshape(
            2 * v.shape[0], nd, lanes)

    corr[3 : 3 + NL] = spike[0] + spike[1] * L + spike[2] * R
    corr[0:3] = spk_lo[0] + spk_lo[1] * sides[down, 0] + spk_lo[2] * sides[down, 1]
    corr[3 + NL :] = spk_hi[0] + spk_hi[1] * sides[up, 0] + spk_hi[2] * sides[up, 1]
    near = twice(corr[pl.ds(mine * L2, L2 + 6)])
    ma[1 : 1 + H1] = mid_lo[0]
    ma[1 + H1 + L1 : 1 + 2 * H1 + L1] = mid_hi[0]
    ma[1 : 1 + Z1] = ma[1 : 1 + Z1] + near[6 - H1 : 6 - H1 + Z1]
    b1[0:H1] = mid_lo[1]
    b1[H1 + L1 :] = mid_hi[1]

    sweep(ma, mb, b1, 1, Z1 - 1, *mid, i1)
    sweep(mb, ma, b1, 2, Z1 - 2, *mid, i1)
    sweep(ma, mb, b1, 3, Z1 - 3, *mid, i1)

    def raise0(K, n):
        k = 1 + 2 * K
        va[pl.ds(k, 2 * n)] = va[pl.ds(k, 2 * n)] + twice(mb[pl.ds(K + 1, n)])

    chunks(3, Z1 - 3, raise0, 8)
    sweep(va, vb, b0, HALO - 3, HALO + own_n + 3, *fine, i0)
    sweep(vb, va, b0, HALO - 2, HALO + own_n + 2, *fine, i0)
    sweep(va, vb, b0, HALO - 1, HALO + own_n + 1, *fine, i0)

    lo, hi = HALO, HALO + own_n + 1
    vb[lo : lo + 1] = jnp.where(first_dev, -vb[lo + 1 : lo + 2], vb[lo : lo + 1])
    vb[hi : hi + 1] = jnp.where(last_dev, -vb[hi - 1 : hi], vb[hi : hi + 1])

    def terms(i, n):
        a, s = vb[pl.ds(HALO + 1 + i, n)], s0[pl.ds(1 + i, n)]
        tx = m0["xin"] * ((a - x_next(a, m0)) * (s - x_next(s, m0)))
        ty = m0["yin"] * ((a - y_next(a, m0)) * (s - y_next(s, m0)))
        t = tx + x_prev(tx, m0) + ty + y_prev(ty, m0) + m0["edge"] * (a * s)
        z = (a - vb[pl.ds(HALO + i, n)]) * (s - s0[pl.ds(i, n)])
        z = z + (a - vb[pl.ds(HALO + 2 + i, n)]) * (s - s0[pl.ds(2 + i, n)])
        return jnp.sum(c0[pl.ds(HALO + 1 + i, n)] * (t + 0.5 * z), axis=0)

    acc = terms(0, own_n)

    vb[HALO + 1 : HALO + 1 + own_n] = to_plane(vb[HALO + 1 : HALO + 1 + own_n])
    va[0] = to_plane(acc[None])[0]
    vflat = vb.reshape(vb.shape[0] * nd, lanes)
    for d in range(nd):
        outs[d, 0:own_n, :] = vflat[pl.ds((HALO + 1) * nd + d, own_n, stride=nd), :]
        outs[d, own_n:, :] = jnp.broadcast_to(va[0, d : d + 1, :], (8, lanes))
    fins = []
    for k in range(1, parts_n):
        peer, device = member(k)
        fins.append(copy(outs.at[peer], fin.at[mine], fin_send.at[k], fin_recv.at[k], device))
    fin[mine] = outs[me]
    for c in fins:
        c.wait()
    sums = fin[0, own_n:, :]
    for i in range(1, parts_n):
        sums = sums + fin[i, own_n:, :]
    part[gz] = sums
    parts = []
    for j in range(1, n_z):
        parts.append(copy(part.at[gz], part.at[gz], pt_send.at[j], pt_recv.at[j],
                          (gx, gy, lax.rem(gz + j, n_z))))
    field = fin[:, 0:own_n, :].reshape(cz_len, lanes).T.reshape(x_row, n_y, cy_len, cz_len)
    for a in range(n_y):
        for i in range(x_row):
            adj_ref[a * x_row + i] = field[i, a]

    for c in parts:
        c.wait()
    total = part[0]
    for j in range(1, n_z):
        total = total + part[j]
    rows = total[0:cx_len] * (-1.0 / math.sqrt(n_total))
    width = cy_len // n_z
    for j in range(width):
        here = lane8 == row8 % x_row * y_all + row8 // x_row * cy_len + gz * width + j
        grad_ref[:, j : j + 1] = jnp.sum(jnp.where(here, rows, 0.0), axis=1, keepdims=True)


def solution(mesh):
    n_x, n_y, n_z = mesh.shape["gx"], mesh.shape["gy"], mesh.shape["gz"]
    nd = n_x * n_y

    def per_device(source, state, log_coef, lateral, owners):
        cx, cy, cz = source.shape
        lanes = cx * cy
        parts_n = min(nd, 8)
        own = cz // parts_n
        Z0, Z1, Z2, H1 = own + 2 * HALO, own // 2 + HALO, own // 4 + 2, HALO // 2
        L2, NL = own // 4, cz // 4
        V = lambda *shape: pltpu.VMEM(shape, F32)
        pln = lambda k: V(k, nd, lanes)
        D = lambda k: pltpu.SemaphoreType.DMA((k,))
        vm = pl.BlockSpec(memory_space=pltpu.VMEM)
        return pl.pallas_call(
            functools.partial(kernel, n_x, n_y, n_z, cx, cy, cz, cz * n_z),
            out_shape=(
                jax.ShapeDtypeStruct((cx, cy, cz), F32),
                jax.ShapeDtypeStruct((cx, cy // n_z), F32),
            ),
            in_specs=[vm] * 5,
            out_specs=(vm, vm),
            scratch_shapes=[
                V(4, cz + 2 * SEND, lanes),
                V(nd, 4, own + 4 * SEND, lanes),
                pln(Z0 + 2), pln(Z0), pln(Z0), pln(Z0), pln(Z0 + 1), pln(Z0), pln(Z0), pln(Z0),
                pln(Z0 + 2), pln(Z0 + 2),
                pln(Z1 + 2), pln(Z1), pln(Z1), pln(Z1), pln(Z1 + 1), pln(Z1), pln(Z1), pln(Z1),
                pln(Z1 + 2), pln(Z1 + 2),
                pln(Z2 + 2), pln(Z2 + 1), pln(Z2),
                V(parts_n, 2, L2, nd, lanes), V(parts_n, L2, nd, lanes),
                V(3, NL, nd, lanes), V(3, NL, nd, lanes), pln(NL + 6),
                pln(own + 2), V(n_z, 7, nd, lanes), V(n_z, 2, nd, lanes),
                V(2, H1, nd, lanes), V(2, H1, nd, lanes),
                V(3, 3, nd, lanes), V(3, 3, nd, lanes),
                V(nd, own + 8, lanes), V(parts_n, own + 8, lanes), V(n_z, 8, lanes),
                D(4 * nd // parts_n), D(2 * nd), D(nd), D(nd), D(nd), D(nd),
                D(nd), D(nd), D(nd), D(nd),
                D(4), D(4), D(n_z + 2), D(n_z + 2), D(nd), D(nd), D(n_z), D(n_z),
            ],
            compiler_params=pltpu.CompilerParams(
                collective_id=0, has_side_effects=True, vmem_limit_bytes=56 * 1024 * 1024
            ),
            cost_estimate=pl.CostEstimate(
                flops=100_000_000, bytes_accessed=400_000, transcendentals=20_000
            ),
        )(source, state, log_coef, lateral, owners)

    placed = (
        P("gx", "gy", "gz"),
        P("gx", "gy", "gz"),
        P("gx", "gy", "gz"),
        P("gx", "gy"),
        P("gx", "gy", None),
    )
    return jax.shard_map(
        per_device,
        mesh=mesh,
        in_specs=placed,
        out_specs=(P("gx", "gy", "gz"), P("gx", ("gy", "gz"))),
        check_vma=False,
    )
```

```python
import functools
import math

import jax
import jax.numpy as jnp
from jax import lax
from jax.experimental import pallas as pl
from jax.experimental.pallas import tpu as pltpu
from jax.sharding import PartitionSpec as P

ANISO = 200.0
OMEGA = 0.8
HALO = 10
SEND = 16
MESH = pl.DeviceIdType.MESH
F32 = jnp.float32


def kernel(
    n_x, n_y, n_z, cx_len, cy_len, cz_len, n_total,
    source_in, state_in, logc_in, lat_ref, owners_ref,
    adj_ref, grad_ref,
    logc_ref, source_ref, state_ref, in_sem, ext, gath,
    c0, x0, w0, y0, z0, d0, i0, b0, va, vb,
    c1, x1, w1, y1, z1, d1, i1, b1, ma, mb,
    c2, z2, d2, low, rlow, fac, spike, corr,
    s0, iface, sides, mid_lo, mid_hi, spk_lo, spk_hi, outs, fin, part,
    z_send, z_recv, main_send, main_recv, src_send, src_recv, st_send, st_recv,
    low_send, low_recv, r_send, r_recv,
    mid_send, mid_recv, if_send, if_recv, fin_send, fin_recv, pt_send, pt_recv,
):
    nd = n_x * n_y
    lanes = cx_len * cy_len
    gx, gy, gz = lax.axis_index("gx"), lax.axis_index("gy"), lax.axis_index("gz")
    me = gx * n_y + gy
    up, down = lax.rem(gz + 1, n_z), lax.rem(gz + n_z - 1, n_z)
    parts_n = min(nd, 8)
    own_n = cz_len // parts_n
    mine = lax.rem(me, parts_n)
    group = me - mine
    Z0, Z1, Z2 = own_n + 2 * HALO, own_n // 2 + HALO, own_n // 4 + 2
    H1 = HALO // 2
    L1, L2, NL = own_n // 2, own_n // 4, cz_len // 4
    WIN = own_n + 2 * SEND

    def place(k, z):
        peer = lax.rem(me + k, nd)
        return (lax.div(peer, n_y), lax.rem(peer, n_y), z)

    def member(k):
        peer = group + lax.rem(mine + k, parts_n)
        return peer, (lax.div(peer, n_y), lax.rem(peer, n_y), gz)

    def along(step):
        t = lax.rem(gz * parts_n + mine + step + n_z * parts_n, n_z * parts_n)
        peer = group + lax.rem(t, parts_n)
        return (lax.div(peer, n_y), lax.rem(peer, n_y), lax.div(t, parts_n))

    fetches = []
    for i, (a, b) in enumerate(
        ((logc_in, logc_ref), (source_in, source_ref), (state_in, state_ref))
    ):
        fetches.append(pltpu.make_async_copy(a, b, in_sem.at[i]))
        fetches[i].start()
    barrier = pltpu.get_barrier_semaphore()
    greeted = [place(k, gz) for k in range(1, nd)]
    greeted += [(gx, gy, lax.rem(gz + j, n_z)) for j in range(1, n_z)]
    greeted += [along(1), along(-1)]
    groups = nd // parts_n

    def greet(devices):
        for device in devices:
            pl.semaphore_signal(barrier, inc=1, device_id=device, device_id_type=MESH)

    greet(greeted)
    pl.when(mine == 0)(lambda: greet([place(k, down) for k in range(nd)]))
    pl.when(mine == parts_n - 1)(lambda: greet([place(k, up) for k in range(nd)]))

    lane = lax.broadcasted_iota(jnp.int32, (nd, lanes), 1)
    sub = lax.broadcasted_iota(jnp.int32, (nd, lanes), 0)
    y_all = n_y * cy_len
    x_row = lanes // y_all
    xm, ys = lane // y_all, lane % y_all
    xs = sub * x_row + xm
    slot = ys // cy_len - sub % n_y
    lane8 = lax.broadcasted_iota(jnp.int32, (cx_len, lanes), 1)
    row8 = lax.broadcasted_iota(jnp.int32, (cx_len, lanes), 0)
    lat = jnp.zeros((cx_len, lanes), F32)
    for y in range(cy_len):
        lat = jnp.where(lane8 % cy_len == y, lat_ref[:, y : y + 1], lat)
    lane_x = lane8 // cy_len % n_y * x_row + lane8 // y_all
    lat = jnp.sum(jnp.where(lane_x == row8, lat, 0.0), axis=0, keepdims=True)

    def rows_of(ref):
        v = ref[...].reshape(n_y, x_row, cy_len, cz_len)
        v = jnp.stack([v[:, i] for i in range(x_row)])
        return v.reshape(lanes, cz_len).T

    fetches[0].wait()
    coef = jnp.exp(rows_of(logc_ref) + lat)
    fetches[1].wait()
    src = rows_of(source_ref)
    for i, v in enumerate((coef, src)):
        ext[i, SEND : SEND + cz_len, :] = v
        ext[i, 0:SEND, :] = jnp.zeros((SEND, lanes), F32)
        ext[i, SEND + cz_len :, :] = jnp.zeros((SEND, lanes), F32)
    pl.semaphore_wait(barrier, len(greeted) + 2 * groups)

    def copy(src_at, dst_at, ssem, rsem, device):
        c = pltpu.make_async_remote_copy(
            src_ref=src_at, dst_ref=dst_at, send_sem=ssem, recv_sem=rsem,
            device_id=device, device_id_type=MESH,
        )
        c.start()
        return c

    def window(first, count, part):
        at = pl.multiple_of(part * own_n, 8)
        return ext.at[pl.ds(first, count), pl.ds(at, WIN)]

    def deal(first, count, ssem, rsem):
        sent = []
        for k in range(1, nd):
            part_of = lax.rem(lax.rem(me + k, nd), parts_n)
            sent.append(copy(window(first, count, part_of),
                             gath.at[me, pl.ds(first, count), pl.ds(0, WIN)],
                             ssem.at[k], rsem.at[k], place(k, gz)))
        return sent

    def beyond(first, at):
        sent = []
        for i in range(groups):
            for end, row, z, to in (
                (0, cz_len, up, i * parts_n), (1, SEND, down, (i + 1) * parts_n - 1),
            ):
                sent.append(copy(
                    ext.at[pl.ds(first, 2), pl.ds(row, SEND)],
                    gath.at[me, pl.ds(first, 2), pl.ds(WIN + end * SEND, SEND)],
                    z_send.at[at + 2 * i + end], z_recv.at[at * nd // 2 // groups + me],
                    (to // n_y, to % n_y, z)))
        return sent

    def beyond_wait(first, at, sent):
        for c in sent:
            c.wait_send()

        def arrive(end):
            for d in range(nd):
                pltpu.make_async_remote_copy(
                    src_ref=ext.at[pl.ds(first, 2), pl.ds(0, SEND)],
                    dst_ref=gath.at[d, pl.ds(first, 2), pl.ds(WIN + end * SEND, SEND)],
                    send_sem=z_send.at[0], recv_sem=z_recv.at[at * nd // 2 // groups + d],
                    device_id=place(1, gz), device_id_type=MESH,
                ).wait_recv()

        pl.when(mine == 0)(lambda: arrive(0))
        pl.when(mine == parts_n - 1)(lambda: arrive(1))

    main = deal(0, 1, main_send, main_recv)
    main_z = beyond(0, 0)
    sources = deal(1, 1, src_send, src_recv)
    fetches[2].wait()
    ext[2, SEND : SEND + cz_len, :] = rows_of(state_ref)
    ext[2, 0:SEND, :] = jnp.zeros((SEND, lanes), F32)
    ext[2, SEND + cz_len :, :] = jnp.zeros((SEND, lanes), F32)
    line = owners_ref[0]
    flags = []
    for j in range(SEND):
        if 0 < j < n_z:
            same = jnp.broadcast_to(line[:, j : j + 1], (1, lanes)) == jnp.broadcast_to(
                line[:, j - 1 : j], (1, lanes)
            )
            flags.append(jnp.where(same, 1.0, 0.0))
        else:
            flags.append(jnp.zeros((1, lanes), F32))
    flags = jnp.concatenate(flags, axis=0)
    for j in range(0, cz_len + 2 * SEND, SEND):
        ext[3, j : j + SEND, :] = flags
    gath[me, :, 0:WIN, :] = ext[:, pl.ds(pl.multiple_of(mine * own_n, 8), WIN), :]
    from_lo = (parts_n - 1 - mine) // (parts_n - 1) * WIN
    from_hi = mine // (parts_n - 1) * (2 * SEND)
    HIGH = WIN + 2 * SEND

    def roll(v, shift, axis):
        return pltpu.roll(v, shift % v.shape[axis], axis)

    nx_all = n_x * cx_len

    def masks(s):
        ends_x = jnp.where(xs < s, 1.0, 0.0) + jnp.where(xs >= nx_all - s, 1.0, 0.0)
        ends_y = jnp.where(ys < s, 1.0, 0.0) + jnp.where(ys >= y_all - s, 1.0, 0.0)
        return dict(
            s=s, xhi=(xm >= x_row - s)[None], xlo=(xm < s)[None],
            xin=jnp.where(xs >= nx_all - s, 0.0, 0.5)[None],
            yin=jnp.where(ys >= y_all - s, 0.0, 0.5)[None],
            edge=(ends_x + ends_y)[None],
            xbit=(xs // s % 2 == 0)[None], ybit=(ys // s % 2 == 0)[None],
        )

    def pick(mask, a, b):
        return jnp.where(jnp.broadcast_to(mask, a.shape), a, b)

    def x_next(v, m, row=None):
        s = m["s"]
        if s >= x_row:
            return roll(v, -(s // x_row), 1)
        row = roll(v, -1, 1) if row is None else row
        return roll(pick(m["xlo"], row, v), -s * y_all, 2)

    def x_prev(v, m, row=None):
        s = m["s"]
        if s >= x_row:
            return roll(v, s // x_row, 1)
        row = roll(v, 1, 1) if row is None else row
        return roll(pick(m["xhi"], row, v), s * y_all, 2)

    def y_next(v, m):
        return roll(v, -m["s"], 2)

    def y_prev(v, m):
        return roll(v, m["s"], 2)

    def block_mean(pair, m):
        s = m["s"]
        v = pair + pick(m["ybit"], roll(pair, -s, 2), roll(pair, s, 2))
        if s >= x_row:
            near, far = roll(v, -(s // x_row), 1), roll(v, s // x_row, 1)
        else:
            near, far = roll(v, -s * y_all, 2), roll(v, s * y_all, 2)
        return 0.125 * (v + pick(m["xbit"], near, far))

    def to_plane(v):
        out = v
        for shift in range(1 - n_y, n_y):
            if shift:
                moved = roll(roll(v, -shift, 1), shift * cy_len, 2)
                out = pick((slot == shift)[None], moved, out)
        return out

    m0, m1, m2 = masks(1), masks(2), masks(4)
    first_dev = (gz == 0) & (mine == 0)
    last_dev = (gz == n_z - 1) & (mine == parts_n - 1)
    zero_plane = jnp.zeros((1, nd, lanes), F32)

    def chunks(start, stop, body, step=12):
        for k in range(start, stop, step):
            body(k, min(step, stop - k))

    def pads(ref):
        ref[0:1] = zero_plane
        ref[ref.shape[0] - 1 :] = zero_plane

    for ref in (va, vb, ma, mb):
        pads(ref)

    def level(c, length, halo, own, scale, m, xr, wr, yr, zr, dr, ir):
        half = 0.5 * scale * ANISO
        c[0:1], c[length + 1 :] = c[1:2], c[length : length + 1]
        lo, hi = halo, halo + own + 1
        c[lo : lo + 1] = jnp.where(first_dev, c[lo + 1 : lo + 2], c[lo : lo + 1])
        c[hi : hi + 1] = jnp.where(last_dev, c[hi - 1 : hi], c[hi : hi + 1])

        def body(k, n):
            here = c[pl.ds(k + 1, n)]
            wz = half * (c[pl.ds(k, n)] + here)
            zr[pl.ds(k, n)] = wz
            wx = (scale * m["xin"]) * (here + x_next(here, m))
            wy = (scale * m["yin"]) * (here + y_next(here, m))
            wp = x_prev(wx, m)
            diag = wx + wp + wy + y_prev(wy, m) + (scale * m["edge"]) * here
            diag = diag + wz + half * (c[pl.ds(k + 2, n)] + here)
            dr[pl.ds(k, n)] = diag
            if xr is not None:
                xr[pl.ds(k, n)] = wx
                wr[pl.ds(k, n)] = wp
                yr[pl.ds(k, n)] = wy
                ir[pl.ds(k, n)] = OMEGA / diag

        chunks(0, length, body)
        zr[0:1] = zero_plane
        zr[length : length + 1] = zero_plane
        lo, hi = halo, halo + own
        zr[lo : lo + 1] = jnp.where(first_dev, 0.0, zr[lo : lo + 1])
        zr[hi : hi + 1] = jnp.where(last_dev, 0.0, zr[hi : hi + 1])

    def pull(v, k, n, m, xr, wr, yr, zr):
        near, wz = v[pl.ds(k, n + 2)], zr[pl.ds(k, n + 1)]
        here = near[1 : n + 1]
        if m["s"] < x_row:
            rows = v.reshape(v.shape[0] * nd, lanes)
            later = rows[pl.ds((k + 1) * nd + 1, n * nd), :].reshape(n, nd, lanes)
            prior = rows[pl.ds((k + 1) * nd - 1, n * nd), :].reshape(n, nd, lanes)
        else:
            later = prior = None
        wy = yr[pl.ds(k, n)]
        total = wz[:n] * near[:n] + wz[1:] * near[2:]
        total = total + (wy * y_next(here, m) + y_prev(wy * here, m))
        total = total + xr[pl.ds(k, n)] * x_next(here, m, later)
        total = total + wr[pl.ds(k, n)] * x_prev(here, m, prior)
        return here, total

    def sweep(v, out, b, start, stop, m, xr, wr, yr, zr, ir):
        def body(k, n):
            here, total = pull(v, k, n, m, xr, wr, yr, zr)
            out[pl.ds(k + 1, n)] = (1.0 - OMEGA) * here + ir[pl.ds(k, n)] * (
                b[pl.ds(k, n)] + total)
        chunks(start, stop, body)

    fine = (m0, x0, w0, y0, z0)
    mid = (m1, x1, w1, y1, z1)

    for c in main:
        c.wait()
    beyond_wait(0, 0, main_z)
    flat = gath.reshape(nd * 4 * HIGH, lanes)

    def planes(which, start, n):
        return to_plane(jnp.stack([
            flat[pl.ds(which * HIGH + start + u, nd, stride=4 * HIGH), :] for u in range(n)]))

    def spread(which, ref, pad):
        def body(k, n):
            ref[pl.ds(pad + k, n)] = planes(which, SEND - HALO + k, n)

        chunks(HALO, HALO + own_n, body)
        ref[pad : pad + HALO] = planes(which, from_lo + SEND - HALO, HALO)
        hi = pad + HALO + own_n
        ref[hi : hi + HALO] = planes(which, from_hi + SEND + own_n, HALO)

    spread(0, c0, 1)

    def pairs(ref, k, step):
        v = ref[pl.ds(k, 2 * step)].reshape(step, 2, nd, lanes)
        return v[:, 0] + v[:, 1]

    def coarsen1(K, n):
        c1[pl.ds(K + 1, n)] = block_mean(pairs(c0, 1 + 2 * K, n), m0)

    chunks(0, Z1, coarsen1)

    def coarsen2(K, n):
        c2[pl.ds(K + 1, n)] = block_mean(pairs(c1, 1 + H1 - 2 + 2 * K, n), m1)

    chunks(0, Z2, coarsen2)
    level(c0, Z0, HALO, own_n, 1.0, m0, x0, w0, y0, z0, d0, i0)
    level(c1, Z1, H1, L1, 0.25, m1, x1, w1, y1, z1, d1, i1)
    level(c2, Z2, 1, L2, 0.0625, m2, None, None, None, z2, d2, None)

    for c in sources:
        c.wait()
    states = deal(2, 2, st_send, st_recv)
    states_z = beyond(2, 2 * groups)
    spread(1, b0, 0)

    low[mine, 0] = d2[1 : 1 + L2]
    low[mine, 1] = z2[1 : 1 + L2]
    lows = []
    for k in range(1, parts_n):
        lows.append(copy(low.at[mine], low.at[mine], low_send.at[k], low_recv.at[k], member(k)[1]))

    def first0(k, n):
        va[pl.ds(k + 1, n)] = i0[pl.ds(k, n)] * b0[pl.ds(k, n)]

    chunks(0, Z0, first0)
    sweep(va, vb, b0, 1, Z0 - 1, *fine, i0)
    sweep(vb, va, b0, 2, Z0 - 2, *fine, i0)

    def residual(v, b, d, k, n, m, *weights):
        here, total = pull(v, k, 2 * n, m, *weights)
        r = b[pl.ds(k, 2 * n)] + total - d[pl.ds(k, 2 * n)] * here
        r = r.reshape(n, 2, nd, lanes)
        return block_mean(r[:, 0] + r[:, 1], m)

    def resid0(K, n):
        b1[pl.ds(K, n)] = residual(va, b0, d0, 2 * K, n, *fine)

    chunks(2, Z1 - 2, resid0, 8)

    def first1(k, n):
        ma[pl.ds(k + 1, n)] = i1[pl.ds(k, n)] * b1[pl.ds(k, n)]

    chunks(2, Z1 - 2, first1)
    sweep(ma, mb, b1, 3, Z1 - 3, *mid, i1)
    sweep(mb, ma, b1, 4, Z1 - 4, *mid, i1)

    mids = [
        copy(ma.at[pl.ds(1 + L1, H1)], mid_lo.at[0], mid_send.at[0], mid_recv.at[0], along(1)),
        copy(b1.at[pl.ds(L1, H1)], mid_lo.at[1], mid_send.at[1], mid_recv.at[1], along(1)),
        copy(ma.at[pl.ds(1 + H1, H1)], mid_hi.at[0], mid_send.at[2], mid_recv.at[2], along(-1)),
        copy(b1.at[pl.ds(H1, H1)], mid_hi.at[1], mid_send.at[3], mid_recv.at[3], along(-1)),
    ]

    rlow[mine] = residual(ma, b1, d1, H1, L2, *mid)
    rights = []
    for k in range(1, parts_n):
        rights.append(copy(rlow.at[mine], rlow.at[mine], r_send.at[k], r_recv.at[k], member(k)[1]))
    for c in lows:
        c.wait()

    def dk(k):
        return low[k // L2, 0, k % L2]

    def ek(k):
        return low[k // L2, 1, k % L2]

    inv = 1.0 / dk(0)
    fac[2, 0] = inv
    p_now = jnp.ones((nd, lanes), F32)
    forward_p = [p_now]
    for k in range(1, NL):
        e = ek(k)
        t = e * inv
        fac[1, k - 1] = t
        inv = 1.0 / (dk(k) - e * t)
        p_now = t * p_now
        fac[0, k], fac[2, k] = t, inv
        spike[1, k] = p_now
    spike[1, 0] = forward_p[0]
    p, q = p_now * inv, inv
    spike[1, NL - 1], spike[2, NL - 1] = p, q
    last_p, last_q = p, q
    for k in range(NL - 2, -1, -1):
        f = fac[1, k]
        p = spike[1, k] * fac[2, k] + f * p
        q = f * q
        spike[1, k], spike[2, k] = p, q
    for c in states:
        c.wait()
    beyond_wait(2, 2 * groups, states_z)
    cut_plane = planes(3, SEND + gz, 1)[0]
    for c in rights:
        c.wait()
    y = rlow[0, 0]
    spike[0, 0] = y
    for k in range(1, NL):
        y = rlow[k // L2, k % L2] + fac[0, k] * y
        spike[0, k] = y
    g = y * fac[2, NL - 1]
    spike[0, NL - 1] = g
    last_g = g
    for k in range(NL - 2, -1, -1):
        g = spike[0, k] * fac[2, k] + fac[1, k] * g
        spike[0, k] = g
    for i, (a, b) in enumerate(((g, last_g), (p, last_p), (q, last_q))):
        iface[gz, i], iface[gz, 3 + i] = a, b
    iface[gz, 6] = ek(0) * cut_plane
    ifs = []
    for j in range(1, n_z):
        ifs.append(copy(iface.at[gz], iface.at[gz], if_send.at[j], if_recv.at[j],
                        (gx, gy, lax.rem(gz + j, n_z))))
    ifs.append(copy(spike.at[:, pl.ds(NL - 3, 3)], spk_lo, if_send.at[n_z], if_recv.at[n_z],
                    (gx, gy, up)))
    ifs.append(copy(spike.at[:, pl.ds(0, 3)], spk_hi, if_send.at[n_z + 1], if_recv.at[n_z + 1],
                    (gx, gy, down)))

    s0[1 : own_n + 1] = planes(2, SEND, own_n)
    s0[0:1] = planes(2, from_lo + SEND - 1, 1)
    s0[own_n + 1 :] = planes(2, from_hi + SEND + own_n, 1)
    s0[0:1] = jnp.where(first_dev, 0.0, s0[0:1])
    s0[own_n + 1 :] = jnp.where(last_dev, 0.0, s0[own_n + 1 :])

    for c in mids + ifs:
        c.wait()

    zero = jnp.zeros((nd, lanes), F32)
    A, B = zero, zero
    kept = []
    for j in range(n_z):
        c = iface[j, 6]
        g, p, q = iface[j, 0], iface[j, 1], iface[j, 2]
        gl, plast, ql = iface[j, 3], iface[j, 4], iface[j, 5]
        inv = 1.0 / (1.0 - p * c * B)
        F = (g + p * c * A) * inv
        G = q * inv
        kept.append((c, A, B, F, G))
        nxt = iface[j + 1, 6] if j + 1 < n_z else zero
        tail = plast * c
        A, B = gl + tail * (A + B * F), (ql + tail * B * G) * nxt
    right = zero
    for j in reversed(range(n_z)):
        c, A, B, F, G = kept[j]
        head = F + G * right
        sides[j, 0] = c * (A + B * head)
        sides[j, 1] = right
        right = c * head

    L, R = sides[gz, 0], sides[gz, 1]

    def twice(v):
        return jnp.broadcast_to(v[:, None], (v.shape[0], 2, nd, lanes)).reshape(
            2 * v.shape[0], nd, lanes)

    corr[3 : 3 + NL] = spike[0] + spike[1] * L + spike[2] * R
    corr[0:3] = spk_lo[0] + spk_lo[1] * sides[down, 0] + spk_lo[2] * sides[down, 1]
    corr[3 + NL :] = spk_hi[0] + spk_hi[1] * sides[up, 0] + spk_hi[2] * sides[up, 1]
    near = twice(corr[pl.ds(mine * L2, L2 + 6)])
    ma[1 : 1 + H1] = mid_lo[0]
    ma[1 + H1 + L1 : 1 + 2 * H1 + L1] = mid_hi[0]
    ma[1 : 1 + Z1] = ma[1 : 1 + Z1] + near[6 - H1 : 6 - H1 + Z1]
    b1[0:H1] = mid_lo[1]
    b1[H1 + L1 :] = mid_hi[1]

    sweep(ma, mb, b1, 1, Z1 - 1, *mid, i1)
    sweep(mb, ma, b1, 2, Z1 - 2, *mid, i1)
    sweep(ma, mb, b1, 3, Z1 - 3, *mid, i1)

    def raise0(K, n):
        k = 1 + 2 * K
        va[pl.ds(k, 2 * n)] = va[pl.ds(k, 2 * n)] + twice(mb[pl.ds(K + 1, n)])

    chunks(3, Z1 - 3, raise0, 8)
    sweep(va, vb, b0, HALO - 3, HALO + own_n + 3, *fine, i0)
    sweep(vb, va, b0, HALO - 2, HALO + own_n + 2, *fine, i0)
    sweep(va, vb, b0, HALO - 1, HALO + own_n + 1, *fine, i0)

    lo, hi = HALO, HALO + own_n + 1
    vb[lo : lo + 1] = jnp.where(first_dev, -vb[lo + 1 : lo + 2], vb[lo : lo + 1])
    vb[hi : hi + 1] = jnp.where(last_dev, -vb[hi - 1 : hi], vb[hi : hi + 1])

    def terms(i, n):
        a, s = vb[pl.ds(HALO + 1 + i, n)], s0[pl.ds(1 + i, n)]
        tx = m0["xin"] * ((a - x_next(a, m0)) * (s - x_next(s, m0)))
        ty = m0["yin"] * ((a - y_next(a, m0)) * (s - y_next(s, m0)))
        t = tx + x_prev(tx, m0) + ty + y_prev(ty, m0) + m0["edge"] * (a * s)
        z = (a - vb[pl.ds(HALO + i, n)]) * (s - s0[pl.ds(i, n)])
        z = z + (a - vb[pl.ds(HALO + 2 + i, n)]) * (s - s0[pl.ds(2 + i, n)])
        return jnp.sum(c0[pl.ds(HALO + 1 + i, n)] * (t + 0.5 * z), axis=0)

    acc = terms(0, own_n)

    vb[HALO + 1 : HALO + 1 + own_n] = to_plane(vb[HALO + 1 : HALO + 1 + own_n])
    va[0] = to_plane(acc[None])[0]
    vflat = vb.reshape(vb.shape[0] * nd, lanes)
    for d in range(nd):
        outs[d, 0:own_n, :] = vflat[pl.ds((HALO + 1) * nd + d, own_n, stride=nd), :]
        outs[d, own_n:, :] = jnp.broadcast_to(va[0, d : d + 1, :], (8, lanes))
    fins = []
    for k in range(1, parts_n):
        peer, device = member(k)
        fins.append(copy(outs.at[peer], fin.at[mine], fin_send.at[k], fin_recv.at[k], device))
    fin[mine] = outs[me]
    for c in fins:
        c.wait()
    sums = fin[0, own_n:, :]
    for i in range(1, parts_n):
        sums = sums + fin[i, own_n:, :]
    part[gz] = sums
    parts = []
    for j in range(1, n_z):
        parts.append(copy(part.at[gz], part.at[gz], pt_send.at[j], pt_recv.at[j],
                          (gx, gy, lax.rem(gz + j, n_z))))
    field = fin[:, 0:own_n, :].reshape(cz_len, lanes).T.reshape(x_row, n_y, cy_len, cz_len)
    for a in range(n_y):
        for i in range(x_row):
            adj_ref[a * x_row + i] = field[i, a]

    for c in parts:
        c.wait()
    total = part[0]
    for j in range(1, n_z):
        total = total + part[j]
    rows = total[0:cx_len] * (-1.0 / math.sqrt(n_total))
    width = cy_len // n_z
    for j in range(width):
        here = lane8 == row8 % x_row * y_all + row8 // x_row * cy_len + gz * width + j
        grad_ref[:, j : j + 1] = jnp.sum(jnp.where(here, rows, 0.0), axis=1, keepdims=True)


def solution(mesh):
    n_x, n_y, n_z = mesh.shape["gx"], mesh.shape["gy"], mesh.shape["gz"]
    nd = n_x * n_y

    def per_device(source, state, log_coef, lateral, owners):
        cx, cy, cz = source.shape
        lanes = cx * cy
        parts_n = min(nd, 8)
        own = cz // parts_n
        Z0, Z1, Z2, H1 = own + 2 * HALO, own // 2 + HALO, own // 4 + 2, HALO // 2
        L2, NL = own // 4, cz // 4
        V = lambda *shape: pltpu.VMEM(shape, F32)
        pln = lambda k: V(k, nd, lanes)
        D = lambda k: pltpu.SemaphoreType.DMA((k,))
        vm = pl.BlockSpec(memory_space=pltpu.VMEM)
        return pl.pallas_call(
            functools.partial(kernel, n_x, n_y, n_z, cx, cy, cz, cz * n_z),
            out_shape=(
                jax.ShapeDtypeStruct((cx, cy, cz), F32),
                jax.ShapeDtypeStruct((cx, cy // n_z), F32),
            ),
            in_specs=[pl.BlockSpec(memory_space=pl.ANY)] * 3 + [vm] * 2,
            out_specs=(vm, vm),
            scratch_shapes=[
                V(cx, cy, cz), V(cx, cy, cz), V(cx, cy, cz), D(3),
                V(4, cz + 2 * SEND, lanes),
                V(nd, 4, own + 4 * SEND, lanes),
                pln(Z0 + 2), pln(Z0), pln(Z0), pln(Z0), pln(Z0 + 1), pln(Z0), pln(Z0), pln(Z0),
                pln(Z0 + 2), pln(Z0 + 2),
                pln(Z1 + 2), pln(Z1), pln(Z1), pln(Z1), pln(Z1 + 1), pln(Z1), pln(Z1), pln(Z1),
                pln(Z1 + 2), pln(Z1 + 2),
                pln(Z2 + 2), pln(Z2 + 1), pln(Z2),
                V(parts_n, 2, L2, nd, lanes), V(parts_n, L2, nd, lanes),
                V(3, NL, nd, lanes), V(3, NL, nd, lanes), pln(NL + 6),
                pln(own + 2), V(n_z, 7, nd, lanes), V(n_z, 2, nd, lanes),
                V(2, H1, nd, lanes), V(2, H1, nd, lanes),
                V(3, 3, nd, lanes), V(3, 3, nd, lanes),
                V(nd, own + 8, lanes), V(parts_n, own + 8, lanes), V(n_z, 8, lanes),
                D(4 * nd // parts_n), D(2 * nd), D(nd), D(nd), D(nd), D(nd), D(nd), D(nd),
                D(nd), D(nd), D(nd), D(nd),
                D(4), D(4), D(n_z + 2), D(n_z + 2), D(nd), D(nd), D(n_z), D(n_z),
            ],
            compiler_params=pltpu.CompilerParams(
                collective_id=0, has_side_effects=True, vmem_limit_bytes=56 * 1024 * 1024
            ),
            cost_estimate=pl.CostEstimate(
                flops=100_000_000, bytes_accessed=400_000, transcendentals=20_000
            ),
        )(source, state, log_coef, lateral, owners)

    placed = (
        P("gx", "gy", "gz"),
        P("gx", "gy", "gz"),
        P("gx", "gy", "gz"),
        P("gx", "gy"),
        P("gx", "gy", None),
    )
    return jax.shard_map(
        per_device,
        mesh=mesh,
        in_specs=placed,
        out_specs=(P("gx", "gy", "gz"), P("gx", ("gy", "gz"))),
        check_vma=False,
    )
```

```python
import functools
import math

import jax
import jax.numpy as jnp
from jax import lax
from jax.experimental import pallas as pl
from jax.experimental.pallas import tpu as pltpu
from jax.sharding import PartitionSpec as P

ANISO = 200.0
OMEGA = 0.8
HALO = 10
SEND = 16
MESH = pl.DeviceIdType.MESH
F32 = jnp.float32


def kernel(
    n_x, n_y, n_z, cx_len, cy_len, cz_len, n_total,
    source_ref, state_ref, logc_ref, lat_ref, owners_ref,
    adj_ref, grad_ref,
    ext, gath,
    c0, x0, w0, y0, z0, d0, i0, b0, va, vb,
    c1, x1, w1, y1, z1, d1, i1, b1, ma, mb,
    c2, z2, d2, low, rlow, fac, spike, corr,
    s0, iface, sides, mstage, mid_lo, mid_hi, spk_lo, spk_hi, outs, fin, part,
    z_send, z_recv, main_send, main_recv,
    low_send, low_recv, r_send, r_recv,
    mid_send, mid_recv, if_send, if_recv, fin_send, fin_recv, pt_send, pt_recv,
):
    nd = n_x * n_y
    lanes = cx_len * cy_len
    gx, gy, gz = lax.axis_index("gx"), lax.axis_index("gy"), lax.axis_index("gz")
    me = gx * n_y + gy
    up, down = lax.rem(gz + 1, n_z), lax.rem(gz + n_z - 1, n_z)
    parts_n = min(nd, 8)
    own_n = cz_len // parts_n
    mine = lax.rem(me, parts_n)
    group = me - mine
    Z0, Z1, Z2 = own_n + 2 * HALO, own_n // 2 + HALO, own_n // 4 + 2
    H1 = HALO // 2
    L1, L2, NL = own_n // 2, own_n // 4, cz_len // 4
    WIN = own_n + 2 * SEND

    def place(k, z):
        peer = lax.rem(me + k, nd)
        return (lax.div(peer, n_y), lax.rem(peer, n_y), z)

    def member(k):
        peer = group + lax.rem(mine + k, parts_n)
        return peer, (lax.div(peer, n_y), lax.rem(peer, n_y), gz)

    def along(step):
        t = lax.rem(gz * parts_n + mine + step + n_z * parts_n, n_z * parts_n)
        peer = group + lax.rem(t, parts_n)
        return (lax.div(peer, n_y), lax.rem(peer, n_y), lax.div(t, parts_n))

    barrier = pltpu.get_barrier_semaphore()
    greeted = [place(k, gz) for k in range(1, nd)]
    greeted += [(gx, gy, lax.rem(gz + j, n_z)) for j in range(1, n_z)]
    greeted += [along(1), along(-1)]
    groups = nd // parts_n

    def greet(devices):
        for device in devices:
            pl.semaphore_signal(barrier, inc=1, device_id=device, device_id_type=MESH)

    greet(greeted)
    pl.when(mine == 0)(lambda: greet([place(k, down) for k in range(nd)]))
    pl.when(mine == parts_n - 1)(lambda: greet([place(k, up) for k in range(nd)]))

    lane = lax.broadcasted_iota(jnp.int32, (nd, lanes), 1)
    sub = lax.broadcasted_iota(jnp.int32, (nd, lanes), 0)
    y_all = n_y * cy_len
    x_row = lanes // y_all
    xm, ys = lane // y_all, lane % y_all
    xs = sub * x_row + xm
    slot = ys // cy_len - sub % n_y
    lane8 = lax.broadcasted_iota(jnp.int32, (cx_len, lanes), 1)
    row8 = lax.broadcasted_iota(jnp.int32, (cx_len, lanes), 0)
    lat = jnp.zeros((cx_len, lanes), F32)
    for y in range(cy_len):
        lat = jnp.where(lane8 % cy_len == y, lat_ref[:, y : y + 1], lat)
    lane_x = lane8 // cy_len % n_y * x_row + lane8 // y_all
    lat = jnp.sum(jnp.where(lane_x == row8, lat, 0.0), axis=0, keepdims=True)

    def rows_of(ref):
        v = ref[...].reshape(n_y, x_row, cy_len, cz_len)
        v = jnp.stack([v[:, i] for i in range(x_row)])
        return v.reshape(lanes, cz_len).T

    coef = jnp.exp(rows_of(logc_ref) + lat)
    src = rows_of(source_ref)
    for i, v in enumerate((coef, src)):
        ext[i, SEND : SEND + cz_len, :] = v
        ext[i, 0:SEND, :] = jnp.zeros((SEND, lanes), F32)
        ext[i, SEND + cz_len :, :] = jnp.zeros((SEND, lanes), F32)
    pl.semaphore_wait(barrier, len(greeted) + 2 * groups)

    def copy(src_at, dst_at, ssem, rsem, device):
        c = pltpu.make_async_remote_copy(
            src_ref=src_at, dst_ref=dst_at, send_sem=ssem, recv_sem=rsem,
            device_id=device, device_id_type=MESH,
        )
        c.start()
        return c

    def window(part):
        at = pl.multiple_of(part * own_n, 8)
        return ext.at[:, pl.ds(at, WIN)]

    def deal(ssem, rsem):
        sent = []
        for k in range(1, nd):
            part_of = lax.rem(lax.rem(me + k, nd), parts_n)
            sent.append(copy(window(part_of), gath.at[me, :, pl.ds(0, WIN)],
                             ssem.at[k], rsem.at[k], place(k, gz)))
        return sent

    def beyond():
        sent = []
        for i in range(groups):
            for end, row, z, to in (
                (0, cz_len, up, i * parts_n), (1, SEND, down, (i + 1) * parts_n - 1),
            ):
                sent.append(copy(
                    ext.at[:, pl.ds(row, SEND)],
                    gath.at[me, :, pl.ds(WIN + end * SEND, SEND)],
                    z_send.at[2 * i + end], z_recv.at[me],
                    (to // n_y, to % n_y, z)))
        return sent

    def beyond_wait(sent):
        for c in sent:
            c.wait_send()

        def arrive(end):
            for d in range(nd):
                pltpu.make_async_remote_copy(
                    src_ref=ext.at[:, pl.ds(0, SEND)],
                    dst_ref=gath.at[d, :, pl.ds(WIN + end * SEND, SEND)],
                    send_sem=z_send.at[0], recv_sem=z_recv.at[d],
                    device_id=place(1, gz), device_id_type=MESH,
                ).wait_recv()

        pl.when(mine == 0)(lambda: arrive(0))
        pl.when(mine == parts_n - 1)(lambda: arrive(1))

    ext[2, SEND : SEND + cz_len, :] = rows_of(state_ref)
    ext[2, 0:SEND, :] = jnp.zeros((SEND, lanes), F32)
    ext[2, SEND + cz_len :, :] = jnp.zeros((SEND, lanes), F32)
    line = owners_ref[0]
    flags = []
    for j in range(SEND):
        if 0 < j < n_z:
            same = jnp.broadcast_to(line[:, j : j + 1], (1, lanes)) == jnp.broadcast_to(
                line[:, j - 1 : j], (1, lanes)
            )
            flags.append(jnp.where(same, 1.0, 0.0))
        else:
            flags.append(jnp.zeros((1, lanes), F32))
    flags = jnp.concatenate(flags, axis=0)
    for j in range(0, cz_len + 2 * SEND, SEND):
        ext[3, j : j + SEND, :] = flags
    main = deal(main_send, main_recv)
    main_z = beyond()
    gath[me, :, 0:WIN, :] = ext[:, pl.ds(pl.multiple_of(mine * own_n, 8), WIN), :]
    from_lo = (parts_n - 1 - mine) // (parts_n - 1) * WIN
    from_hi = mine // (parts_n - 1) * (2 * SEND)
    HIGH = WIN + 2 * SEND

    def roll(v, shift, axis):
        return pltpu.roll(v, shift % v.shape[axis], axis)

    nx_all = n_x * cx_len

    def masks(s):
        ends_x = jnp.where(xs < s, 1.0, 0.0) + jnp.where(xs >= nx_all - s, 1.0, 0.0)
        ends_y = jnp.where(ys < s, 1.0, 0.0) + jnp.where(ys >= y_all - s, 1.0, 0.0)
        return dict(
            s=s, xhi=(xm >= x_row - s)[None], xlo=(xm < s)[None],
            xin=jnp.where(xs >= nx_all - s, 0.0, 0.5)[None],
            yin=jnp.where(ys >= y_all - s, 0.0, 0.5)[None],
            edge=(ends_x + ends_y)[None],
            xbit=(xs // s % 2 == 0)[None], ybit=(ys // s % 2 == 0)[None],
        )

    def pick(mask, a, b):
        return jnp.where(jnp.broadcast_to(mask, a.shape), a, b)

    def x_next(v, m, row=None):
        s = m["s"]
        if s >= x_row:
            return roll(v, -(s // x_row), 1)
        row = roll(v, -1, 1) if row is None else row
        return roll(pick(m["xlo"], row, v), -s * y_all, 2)

    def x_prev(v, m, row=None):
        s = m["s"]
        if s >= x_row:
            return roll(v, s // x_row, 1)
        row = roll(v, 1, 1) if row is None else row
        return roll(pick(m["xhi"], row, v), s * y_all, 2)

    def y_next(v, m):
        return roll(v, -m["s"], 2)

    def y_prev(v, m):
        return roll(v, m["s"], 2)

    def block_mean(pair, m):
        s = m["s"]
        v = pair + pick(m["ybit"], roll(pair, -s, 2), roll(pair, s, 2))
        if s >= x_row:
            near, far = roll(v, -(s // x_row), 1), roll(v, s // x_row, 1)
        else:
            near, far = roll(v, -s * y_all, 2), roll(v, s * y_all, 2)
        return 0.125 * (v + pick(m["xbit"], near, far))

    def to_plane(v):
        out = v
        for shift in range(1 - n_y, n_y):
            if shift:
                moved = roll(roll(v, -shift, 1), shift * cy_len, 2)
                out = pick((slot == shift)[None], moved, out)
        return out

    m0, m1, m2 = masks(1), masks(2), masks(4)
    first_dev = (gz == 0) & (mine == 0)
    last_dev = (gz == n_z - 1) & (mine == parts_n - 1)
    zero_plane = jnp.zeros((1, nd, lanes), F32)

    def chunks(start, stop, body, step=12):
        for k in range(start, stop, step):
            body(k, min(step, stop - k))

    def pads(ref):
        ref[0:1] = zero_plane
        ref[ref.shape[0] - 1 :] = zero_plane

    for ref in (va, vb, ma, mb):
        pads(ref)

    def level(c, length, halo, own, scale, m, xr, wr, yr, zr, dr, ir):
        half = 0.5 * scale * ANISO
        c[0:1], c[length + 1 :] = c[1:2], c[length : length + 1]
        lo, hi = halo, halo + own + 1
        c[lo : lo + 1] = jnp.where(first_dev, c[lo + 1 : lo + 2], c[lo : lo + 1])
        c[hi : hi + 1] = jnp.where(last_dev, c[hi - 1 : hi], c[hi : hi + 1])

        def body(k, n):
            here = c[pl.ds(k + 1, n)]
            wz = half * (c[pl.ds(k, n)] + here)
            zr[pl.ds(k, n)] = wz
            wx = (scale * m["xin"]) * (here + x_next(here, m))
            wy = (scale * m["yin"]) * (here + y_next(here, m))
            wp = x_prev(wx, m)
            diag = wx + wp + wy + y_prev(wy, m) + (scale * m["edge"]) * here
            diag = diag + wz + half * (c[pl.ds(k + 2, n)] + here)
            dr[pl.ds(k, n)] = diag
            if xr is not None:
                xr[pl.ds(k, n)] = wx
                wr[pl.ds(k, n)] = wp
                yr[pl.ds(k, n)] = wy
                ir[pl.ds(k, n)] = OMEGA / diag

        chunks(0, length, body)
        zr[0:1] = zero_plane
        zr[length : length + 1] = zero_plane
        lo, hi = halo, halo + own
        zr[lo : lo + 1] = jnp.where(first_dev, 0.0, zr[lo : lo + 1])
        zr[hi : hi + 1] = jnp.where(last_dev, 0.0, zr[hi : hi + 1])

    def pull(v, k, n, m, xr, wr, yr, zr):
        near, wz = v[pl.ds(k, n + 2)], zr[pl.ds(k, n + 1)]
        here = near[1 : n + 1]
        if m["s"] < x_row:
            rows = v.reshape(v.shape[0] * nd, lanes)
            later = rows[pl.ds((k + 1) * nd + 1, n * nd), :].reshape(n, nd, lanes)
            prior = rows[pl.ds((k + 1) * nd - 1, n * nd), :].reshape(n, nd, lanes)
        else:
            later = prior = None
        wy = yr[pl.ds(k, n)]
        total = wz[:n] * near[:n] + wz[1:] * near[2:]
        total = total + (wy * y_next(here, m) + y_prev(wy * here, m))
        total = total + xr[pl.ds(k, n)] * x_next(here, m, later)
        total = total + wr[pl.ds(k, n)] * x_prev(here, m, prior)
        return here, total

    def sweep(v, out, b, start, stop, m, xr, wr, yr, zr, ir):
        def body(k, n):
            here, total = pull(v, k, n, m, xr, wr, yr, zr)
            out[pl.ds(k + 1, n)] = (1.0 - OMEGA) * here + ir[pl.ds(k, n)] * (
                b[pl.ds(k, n)] + total)
        chunks(start, stop, body)

    fine = (m0, x0, w0, y0, z0)
    mid = (m1, x1, w1, y1, z1)

    for c in main:
        c.wait()
    beyond_wait(main_z)
    flat = gath.reshape(nd * 4 * HIGH, lanes)

    def planes(which, start, n):
        return to_plane(jnp.stack([
            flat[pl.ds(which * HIGH + start + u, nd, stride=4 * HIGH), :] for u in range(n)]))

    def spread(k, n):
        c0[pl.ds(1 + k, n)] = planes(0, SEND - HALO + k, n)
        b0[pl.ds(k, n)] = planes(1, SEND - HALO + k, n)

    chunks(HALO, HALO + own_n, spread)
    for which, ref, pad in ((0, c0, 1), (1, b0, 0)):
        ref[pad : pad + HALO] = planes(which, from_lo + SEND - HALO, HALO)
        hi = pad + HALO + own_n
        ref[hi : hi + HALO] = planes(which, from_hi + SEND + own_n, HALO)

    def pairs(ref, k, step):
        v = ref[pl.ds(k, 2 * step)].reshape(step, 2, nd, lanes)
        return v[:, 0] + v[:, 1]

    def coarsen1(K, n):
        c1[pl.ds(K + 1, n)] = block_mean(pairs(c0, 1 + 2 * K, n), m0)

    chunks(0, Z1, coarsen1)

    def coarsen2(K, n):
        c2[pl.ds(K + 1, n)] = block_mean(pairs(c1, 1 + H1 - 2 + 2 * K, n), m1)

    chunks(0, Z2, coarsen2)
    level(c0, Z0, HALO, own_n, 1.0, m0, x0, w0, y0, z0, d0, i0)
    level(c1, Z1, H1, L1, 0.25, m1, x1, w1, y1, z1, d1, i1)
    level(c2, Z2, 1, L2, 0.0625, m2, None, None, None, z2, d2, None)

    low[mine, 0] = d2[1 : 1 + L2]
    low[mine, 1] = z2[1 : 1 + L2]
    lows = []
    for k in range(1, parts_n):
        lows.append(copy(low.at[mine], low.at[mine], low_send.at[k], low_recv.at[k], member(k)[1]))

    def first0(k, n):
        va[pl.ds(k + 1, n)] = i0[pl.ds(k, n)] * b0[pl.ds(k, n)]

    chunks(0, Z0, first0)
    sweep(va, vb, b0, 1, Z0 - 1, *fine, i0)
    sweep(vb, va, b0, 2, Z0 - 2, *fine, i0)

    def residual(v, b, d, k, n, m, *weights):
        here, total = pull(v, k, 2 * n, m, *weights)
        r = b[pl.ds(k, 2 * n)] + total - d[pl.ds(k, 2 * n)] * here
        r = r.reshape(n, 2, nd, lanes)
        return block_mean(r[:, 0] + r[:, 1], m)

    def resid0(K, n):
        b1[pl.ds(K, n)] = residual(va, b0, d0, 2 * K, n, *fine)

    chunks(2, Z1 - 2, resid0, 8)

    def first1(k, n):
        ma[pl.ds(k + 1, n)] = i1[pl.ds(k, n)] * b1[pl.ds(k, n)]

    chunks(2, Z1 - 2, first1)
    sweep(ma, mb, b1, 3, Z1 - 3, *mid, i1)
    sweep(mb, ma, b1, 4, Z1 - 4, *mid, i1)

    for end, row in ((0, L1), (1, H1)):
        mstage[end, 0] = ma[1 + row : 1 + row + H1]
        mstage[end, 1] = b1[row : row + H1]
    mids = [
        copy(mstage.at[0], mid_lo, mid_send.at[0], mid_recv.at[0], along(1)),
        copy(mstage.at[1], mid_hi, mid_send.at[1], mid_recv.at[1], along(-1)),
    ]

    rlow[mine] = residual(ma, b1, d1, H1, L2, *mid)
    rights = []
    for k in range(1, parts_n):
        rights.append(copy(rlow.at[mine], rlow.at[mine], r_send.at[k], r_recv.at[k], member(k)[1]))
    for c in lows:
        c.wait()

    def dk(k):
        return low[k // L2, 0, k % L2]

    def ek(k):
        return low[k // L2, 1, k % L2]

    inv = 1.0 / dk(0)
    fac[2, 0] = inv
    p_now = jnp.ones((nd, lanes), F32)
    forward_p = [p_now]
    for k in range(1, NL):
        e = ek(k)
        t = e * inv
        fac[1, k - 1] = t
        inv = 1.0 / (dk(k) - e * t)
        p_now = t * p_now
        fac[0, k], fac[2, k] = t, inv
        spike[1, k] = p_now
    spike[1, 0] = forward_p[0]
    p, q = p_now * inv, inv
    spike[1, NL - 1], spike[2, NL - 1] = p, q
    last_p, last_q = p, q
    for k in range(NL - 2, -1, -1):
        f = fac[1, k]
        p = spike[1, k] * fac[2, k] + f * p
        q = f * q
        spike[1, k], spike[2, k] = p, q
    cut_plane = planes(3, SEND + gz, 1)[0]
    for c in rights:
        c.wait()
    y = rlow[0, 0]
    spike[0, 0] = y
    for k in range(1, NL):
        y = rlow[k // L2, k % L2] + fac[0, k] * y
        spike[0, k] = y
    g = y * fac[2, NL - 1]
    spike[0, NL - 1] = g
    last_g = g
    for k in range(NL - 2, -1, -1):
        g = spike[0, k] * fac[2, k] + fac[1, k] * g
        spike[0, k] = g
    for i, (a, b) in enumerate(((g, last_g), (p, last_p), (q, last_q))):
        iface[gz, i], iface[gz, 3 + i] = a, b
    iface[gz, 6] = ek(0) * cut_plane
    ifs = []
    for j in range(1, n_z):
        ifs.append(copy(iface.at[gz], iface.at[gz], if_send.at[j], if_recv.at[j],
                        (gx, gy, lax.rem(gz + j, n_z))))
    ifs.append(copy(spike.at[:, pl.ds(NL - 3, 3)], spk_lo, if_send.at[n_z], if_recv.at[n_z],
                    (gx, gy, up)))
    ifs.append(copy(spike.at[:, pl.ds(0, 3)], spk_hi, if_send.at[n_z + 1], if_recv.at[n_z + 1],
                    (gx, gy, down)))

    s0[1 : own_n + 1] = planes(2, SEND, own_n)
    s0[0:1] = planes(2, from_lo + SEND - 1, 1)
    s0[own_n + 1 :] = planes(2, from_hi + SEND + own_n, 1)
    s0[0:1] = jnp.where(first_dev, 0.0, s0[0:1])
    s0[own_n + 1 :] = jnp.where(last_dev, 0.0, s0[own_n + 1 :])

    for c in mids + ifs:
        c.wait()

    zero = jnp.zeros((nd, lanes), F32)
    A, B = zero, zero
    kept = []
    for j in range(n_z):
        c = iface[j, 6]
        g, p, q = iface[j, 0], iface[j, 1], iface[j, 2]
        gl, plast, ql = iface[j, 3], iface[j, 4], iface[j, 5]
        inv = 1.0 / (1.0 - p * c * B)
        F = (g + p * c * A) * inv
        G = q * inv
        kept.append((c, A, B, F, G))
        nxt = iface[j + 1, 6] if j + 1 < n_z else zero
        tail = plast * c
        A, B = gl + tail * (A + B * F), (ql + tail * B * G) * nxt
    right = zero
    for j in reversed(range(n_z)):
        c, A, B, F, G = kept[j]
        head = F + G * right
        sides[j, 0] = c * (A + B * head)
        sides[j, 1] = right
        right = c * head

    L, R = sides[gz, 0], sides[gz, 1]

    def twice(v):
        return jnp.broadcast_to(v[:, None], (v.shape[0], 2, nd, lanes)).reshape(
            2 * v.shape[0], nd, lanes)

    corr[3 : 3 + NL] = spike[0] + spike[1] * L + spike[2] * R
    corr[0:3] = spk_lo[0] + spk_lo[1] * sides[down, 0] + spk_lo[2] * sides[down, 1]
    corr[3 + NL :] = spk_hi[0] + spk_hi[1] * sides[up, 0] + spk_hi[2] * sides[up, 1]
    near = twice(corr[pl.ds(mine * L2, L2 + 6)])
    ma[1 : 1 + H1] = mid_lo[0]
    ma[1 + H1 + L1 : 1 + 2 * H1 + L1] = mid_hi[0]
    ma[1 : 1 + Z1] = ma[1 : 1 + Z1] + near[6 - H1 : 6 - H1 + Z1]
    b1[0:H1] = mid_lo[1]
    b1[H1 + L1 :] = mid_hi[1]

    sweep(ma, mb, b1, 1, Z1 - 1, *mid, i1)
    sweep(mb, ma, b1, 2, Z1 - 2, *mid, i1)
    sweep(ma, mb, b1, 3, Z1 - 3, *mid, i1)

    def raise0(K, n):
        k = 1 + 2 * K
        va[pl.ds(k, 2 * n)] = va[pl.ds(k, 2 * n)] + twice(mb[pl.ds(K + 1, n)])

    chunks(3, Z1 - 3, raise0, 8)
    sweep(va, vb, b0, HALO - 3, HALO + own_n + 3, *fine, i0)
    sweep(vb, va, b0, HALO - 2, HALO + own_n + 2, *fine, i0)
    sweep(va, vb, b0, HALO - 1, HALO + own_n + 1, *fine, i0)

    lo, hi = HALO, HALO + own_n + 1
    vb[lo : lo + 1] = jnp.where(first_dev, -vb[lo + 1 : lo + 2], vb[lo : lo + 1])
    vb[hi : hi + 1] = jnp.where(last_dev, -vb[hi - 1 : hi], vb[hi : hi + 1])

    def terms(i, n):
        a, s = vb[pl.ds(HALO + 1 + i, n)], s0[pl.ds(1 + i, n)]
        tx = m0["xin"] * ((a - x_next(a, m0)) * (s - x_next(s, m0)))
        ty = m0["yin"] * ((a - y_next(a, m0)) * (s - y_next(s, m0)))
        t = tx + x_prev(tx, m0) + ty + y_prev(ty, m0) + m0["edge"] * (a * s)
        z = (a - vb[pl.ds(HALO + i, n)]) * (s - s0[pl.ds(i, n)])
        z = z + (a - vb[pl.ds(HALO + 2 + i, n)]) * (s - s0[pl.ds(2 + i, n)])
        return jnp.sum(c0[pl.ds(HALO + 1 + i, n)] * (t + 0.5 * z), axis=0)

    acc = terms(0, own_n)

    vb[HALO + 1 : HALO + 1 + own_n] = to_plane(vb[HALO + 1 : HALO + 1 + own_n])
    va[0] = to_plane(acc[None])[0]
    vflat = vb.reshape(vb.shape[0] * nd, lanes)
    for d in range(nd):
        outs[d, 0:own_n, :] = vflat[pl.ds((HALO + 1) * nd + d, own_n, stride=nd), :]
        outs[d, own_n:, :] = jnp.broadcast_to(va[0, d : d + 1, :], (8, lanes))
    fins = []
    for k in range(1, parts_n):
        peer, device = member(k)
        fins.append(copy(outs.at[peer], fin.at[mine], fin_send.at[k], fin_recv.at[k], device))
    fin[mine] = outs[me]
    for c in fins:
        c.wait()
    sums = fin[0, own_n:, :]
    for i in range(1, parts_n):
        sums = sums + fin[i, own_n:, :]
    part[gz] = sums
    parts = []
    for j in range(1, n_z):
        parts.append(copy(part.at[gz], part.at[gz], pt_send.at[j], pt_recv.at[j],
                          (gx, gy, lax.rem(gz + j, n_z))))
    field = fin[:, 0:own_n, :].reshape(cz_len, lanes).T.reshape(x_row, n_y, cy_len, cz_len)
    for a in range(n_y):
        for i in range(x_row):
            adj_ref[a * x_row + i] = field[i, a]

    for c in parts:
        c.wait()
    total = part[0]
    for j in range(1, n_z):
        total = total + part[j]
    rows = total[0:cx_len] * (-1.0 / math.sqrt(n_total))
    width = cy_len // n_z
    for j in range(width):
        here = lane8 == row8 % x_row * y_all + row8 // x_row * cy_len + gz * width + j
        grad_ref[:, j : j + 1] = jnp.sum(jnp.where(here, rows, 0.0), axis=1, keepdims=True)


def solution(mesh):
    n_x, n_y, n_z = mesh.shape["gx"], mesh.shape["gy"], mesh.shape["gz"]
    nd = n_x * n_y

    def per_device(source, state, log_coef, lateral, owners):
        cx, cy, cz = source.shape
        lanes = cx * cy
        parts_n = min(nd, 8)
        own = cz // parts_n
        Z0, Z1, Z2, H1 = own + 2 * HALO, own // 2 + HALO, own // 4 + 2, HALO // 2
        L2, NL = own // 4, cz // 4
        V = lambda *shape: pltpu.VMEM(shape, F32)
        pln = lambda k: V(k, nd, lanes)
        D = lambda k: pltpu.SemaphoreType.DMA((k,))
        vm = pl.BlockSpec(memory_space=pltpu.VMEM)
        return pl.pallas_call(
            functools.partial(kernel, n_x, n_y, n_z, cx, cy, cz, cz * n_z),
            out_shape=(
                jax.ShapeDtypeStruct((cx, cy, cz), F32),
                jax.ShapeDtypeStruct((cx, cy // n_z), F32),
            ),
            in_specs=[vm] * 5,
            out_specs=(vm, vm),
            scratch_shapes=[
                V(4, cz + 2 * SEND, lanes),
                V(nd, 4, own + 4 * SEND, lanes),
                pln(Z0 + 2), pln(Z0), pln(Z0), pln(Z0), pln(Z0 + 1), pln(Z0), pln(Z0), pln(Z0),
                pln(Z0 + 2), pln(Z0 + 2),
                pln(Z1 + 2), pln(Z1), pln(Z1), pln(Z1), pln(Z1 + 1), pln(Z1), pln(Z1), pln(Z1),
                pln(Z1 + 2), pln(Z1 + 2),
                pln(Z2 + 2), pln(Z2 + 1), pln(Z2),
                V(parts_n, 2, L2, nd, lanes), V(parts_n, L2, nd, lanes),
                V(3, NL, nd, lanes), V(3, NL, nd, lanes), pln(NL + 6),
                pln(own + 2), V(n_z, 7, nd, lanes), V(n_z, 2, nd, lanes),
                V(2, 2, H1, nd, lanes), V(2, H1, nd, lanes), V(2, H1, nd, lanes),
                V(3, 3, nd, lanes), V(3, 3, nd, lanes),
                V(nd, own + 8, lanes), V(parts_n, own + 8, lanes), V(n_z, 8, lanes),
                D(2 * nd // parts_n), D(nd), D(nd), D(nd),
                D(nd), D(nd), D(nd), D(nd),
                D(2), D(2), D(n_z + 2), D(n_z + 2), D(nd), D(nd), D(n_z), D(n_z),
            ],
            compiler_params=pltpu.CompilerParams(
                collective_id=0, has_side_effects=True, vmem_limit_bytes=56 * 1024 * 1024
            ),
            cost_estimate=pl.CostEstimate(
                flops=100_000_000, bytes_accessed=400_000, transcendentals=20_000
            ),
        )(source, state, log_coef, lateral, owners)

    placed = (
        P("gx", "gy", "gz"),
        P("gx", "gy", "gz"),
        P("gx", "gy", "gz"),
        P("gx", "gy"),
        P("gx", "gy", None),
    )
    return jax.shard_map(
        per_device,
        mesh=mesh,
        in_specs=placed,
        out_specs=(P("gx", "gy", "gz"), P("gx", ("gy", "gz"))),
        check_vma=False,
    )
```
